32 devices in a mesh: segment: 4 (over y, core), ctx: 8 (over z, x).
Axes of the slice: x: 2, y: 2, z: 4, core: 2. Of those that a mesh axis runs over, the one named last changes fastest.
Arguments:
- queries: bfloat16 [128, 8192], P(('segment', 'ctx')), may hold values from -9 to 9
- cache: bfloat16 [65536, 2048], P(('segment', 'ctx')), may hold values from -9 to 9
- out_weight: bfloat16 [32768, 8192], P('segment', 'ctx'), may hold values from -2 to 2
- offsets: int32 [4], P('segment'), may hold values from 5461 to 16352, as said below
- starts: int32 [4], P('segment'), may hold values from 0 to 7261, as said below
Outputs:
- advanced: bfloat16 [128, 8192], P('segment', 'ctx')
The draws below stay inside these ranges and needn't reach their ends.
Inputs may be any that keep to these rules, and one draw needn't show every extreme that they name: `offsets`: each section's slice ends inside its cache; some section's slice ends at its last cache position. A section's document starts no later than its first query; some section's document starts at 0.
All inputs are finite; a program needn't handle non-finite values.
Results may differ from the reference program's by a relative error of at most 0.0054.
Values may be sent and summed in bfloat16 or wider, within the bound.
No kernel may reach another device: no remote copies, remote signals or barrier semaphores. Data moves between devices by JAX's collectives and lax.ppermute only.
A program may use at most 192 MiB of HBM per device.

```python
import jax
import jax.numpy as jnp
from jax import lax

D = 8192
H = 64
KVH = 8
HD = 128
QS = 32
CD = 2048
SECTIONS = 4
LMAX = 16384
N_CTX = 8


def section_plan(key):
    order = jax.random.permutation(jax.random.fold_in(key, 101), SECTIONS).astype(jnp.int32)
    lowest = LMAX // 3
    highest = LMAX - QS
    span = lowest + (highest - lowest) * order // max(SECTIONS - 1, 1)
    drawn = jax.random.randint(jax.random.fold_in(key, 102), (SECTIONS,), 0, highest - span + 1)
    doc_start = jnp.where(order == 0, 0, jnp.where(order == 1, highest - span, drawn))
    return ((doc_start + span).astype(jnp.int32), doc_start.astype(jnp.int32))


def draw_offsets(key, part):
    return section_plan(key)[0]


def draw_starts(key, part):
    return section_plan(key)[1]


def draw_queries(key, part):
    values = jax.random.normal(jax.random.fold_in(key, 1), (SECTIONS * QS, H * HD), jnp.float32)
    values = values * 1.5
    return jnp.clip(values, -9.0, 9.0).astype(jnp.bfloat16)


def draw_cache(key, part):
    values = jnp.clip(jax.random.normal(jax.random.fold_in(key, 5), (SECTIONS * LMAX, 2 * KVH * HD), jnp.float32), -5.0, 5.0)
    return jnp.clip(values, -9.0, 9.0).astype(jnp.bfloat16)


def steps_of(own_key, dims, shards, low, high):
    def one(position, parts):
        draws = jax.random.uniform(jax.random.fold_in(jax.random.fold_in(own_key, 6), position), (parts,), jnp.float32, low / len(shards), high / len(shards))
        return jnp.repeat(jnp.exp(draws), dims[position] // parts).reshape((-1,) + (1,) * (len(dims) - position - 1))

    gain = one(*shards[0])
    for cut in shards[1:]:
        gain = gain * one(*cut)
    return gain


def centred(key, shape, spread, bound, cuts=(), held_as=jnp.bfloat16):
    entries = jax.random.normal(key, shape, jnp.float32) * spread
    if len(cuts) > 0:
        entries = steps_of(key, shape, cuts, -0.22, 0.18) * entries
    return jnp.clip(entries, min=-bound, max=bound).astype(held_as)


def setup_inputs(seed: int = 0) -> dict:
    key_list = jax.random.split(jax.random.key(seed), 6)
    return {
        "queries": draw_queries(jax.random.fold_in(key_list[5], 71), 0),
        "cache": draw_cache(jax.random.fold_in(key_list[5], 71), 0),
        "out_weight": centred(key_list[2], (SECTIONS * H * HD, D), (max(H * HD // 1024, 1)) ** -0.5, 2.0, ((0, 4), (1, 8))),
        "offsets": draw_offsets(jax.random.fold_in(key_list[5], 71), 0),
        "starts": draw_starts(jax.random.fold_in(key_list[5], 71), 0),
    }


def block_state(query_block, cache_block, offset, doc_start, first_position):
    rows = query_block.shape[0]
    span = cache_block.shape[0]
    positions = first_position + jnp.arange(span, dtype=jnp.int32)
    query_pos = offset + jnp.arange(rows, dtype=jnp.int32)
    visible = (positions[None, :] >= doc_start) & (positions[None, :] <= query_pos[:, None])
    visible = visible[:, None, None, :]
    keys = cache_block[:, :KVH * HD].reshape(span, KVH, HD).astype(jnp.float32)
    values = cache_block[:, KVH * HD:].reshape(span, KVH, HD).astype(jnp.float32)
    scores = jnp.einsum('qgjd,pgd->qgjp', query_block, keys) * (HD ** -0.5)
    masked = jnp.where(visible, scores, -1e30)
    row_max = jnp.max(masked, axis=-1)
    weights = jnp.where(visible, jnp.exp(masked - row_max[..., None]), 0.0)
    weight_sum = jnp.sum(weights, axis=-1)
    rounded = lax.optimization_barrier(weights.astype(jnp.bfloat16)).astype(jnp.float32)
    numerator = jnp.einsum('qgjp,pgd->qgjd', rounded, values)
    outputs = numerator / jnp.maximum(weight_sum, 1.0)[..., None]
    return row_max, weight_sum, outputs


def reference(queries, cache, out_weight, offsets, starts):
    results = []
    tile = CD // 2
    for section in range(SECTIONS):
        query_block = queries[section * QS:(section + 1) * QS].reshape(QS, KVH, H // KVH, HD).astype(jnp.float32)
        section_cache = cache[section * LMAX:(section + 1) * LMAX]
        offset = offsets[section]
        doc_start = starts[section]

        def one_tile(index):
            block = lax.dynamic_slice_in_dim(section_cache, index * tile, tile, 0)
            return block_state(query_block, block, offset, doc_start, index * tile)

        maxima, sums, outputs = lax.map(one_tile, jnp.arange(2 * N_CTX, dtype=jnp.int32))
        overall = jnp.max(maxima, axis=0)
        factors = sums * jnp.exp(maxima - overall[None])
        attention = jnp.sum(factors[..., None] * outputs, axis=0) / jnp.sum(factors, axis=0)[..., None]
        attention = attention.reshape(QS, H * HD).astype(jnp.bfloat16)
        weight_rows = out_weight[section * H * HD:(section + 1) * H * HD]
        projected = jnp.dot(attention, weight_rows, preferred_element_type=jnp.float32).astype(jnp.bfloat16)
        results.append(projected)
    return jnp.concatenate([results[-1]] + results[:-1], axis=0)
```

```python
import functools
import math

import jax
import jax.numpy as jnp
from jax import lax
from jax.experimental import pallas as pl
from jax.experimental.pallas import tpu as pltpu
from jax.sharding import PartitionSpec as P

H = 64
KVH = 8
HD = 128
GROUP = H // KVH
LOG2_SCALE = HD ** (-0.5) * math.log2(math.e)
STEP = 8.0
FLOOR = -4096.0
HIDDEN = -1e30
STATS = 16
VMEM_LIMIT = 24 * 1024 * 1024


def swap(value, axis, bits):
    devices = lax.axis_size(axis)
    return lax.ppermute(value, axis, [(i, i ^ bits) for i in range(devices)])


def from_behind(value, axis, by):
    devices = lax.axis_size(axis)
    return lax.ppermute(value, axis, [(i, (i + by) % devices) for i in range(devices)])


class Plan:
    def __init__(self, ctx, rows_here):
        self.ctx = ctx
        self.half = ctx // 2
        self.rows_here = rows_here
        self.rows = ctx * rows_here
        self.heads = H // self.half
        self.unit_heads = min(self.heads, GROUP)
        self.units = self.heads // self.unit_heads
        self.unit_rows = self.unit_heads * self.rows
        self.stat_blocks = self.unit_rows // 128
        self.num_rows = self.units * self.unit_rows
        self.payload_rows = self.num_rows + self.units * self.stat_blocks * STATS

    def stats_at(self, unit):
        return self.num_rows + unit * self.stat_blocks * STATS


def pack_stats(plan, out_ref, unit, peak, total):
    lane = lax.broadcasted_iota(jnp.int32, (plan.unit_rows, 128), 1)
    high = total.astype(jnp.bfloat16).astype(jnp.float32)
    table = jnp.where(lane == 0, peak, jnp.where(lane == 1, high, total - high))
    turned = jnp.transpose(table)[:STATS].astype(jnp.bfloat16)
    for block in range(plan.stat_blocks):
        at = plan.stats_at(unit) + block * STATS
        out_ref[at : at + STATS, :] = turned[:, block * 128 : (block + 1) * 128]


def unpack_stats(plan, ref, unit):
    at = plan.stats_at(unit)
    rows = jnp.concatenate(
        [ref[at + b * STATS : at + (b + 1) * STATS, :] for b in range(plan.stat_blocks)], axis=1
    ).astype(jnp.float32)
    padded = jnp.concatenate([rows, jnp.zeros((128 - STATS, plan.unit_rows), jnp.float32)], axis=0)
    table = jnp.transpose(padded)
    return table[:, 0:1], table[:, 1:2] + table[:, 2:3]


def attend_kernel(plan, part, offset_ref, start_ref, *refs):
    *query_refs, cache_ref, out_ref, score_ref, bias_ref = refs
    span = cache_ref.shape[0]
    chunk = min(span, 512)
    me = lax.axis_index("ctx")
    low, high = me % plan.half, me // plan.half
    offset, start = offset_ref[0], start_ref[0]
    first = me * span
    none = (first + span - 1 < start) | (first > offset + plan.rows - 1)
    every = (first >= start) & (first + span - 1 <= offset)
    mine = low ^ part

    @pl.when(none)
    def _():
        out_ref[...] = jnp.zeros_like(out_ref)
        for unit in range(plan.units):
            pack_stats(
                plan,
                out_ref,
                unit,
                jnp.full((plan.unit_rows, 128), FLOOR / STEP, jnp.float32),
                jnp.zeros((plan.unit_rows, 128), jnp.float32),
            )

    @pl.when(every)
    def _():
        bias_ref[...] = jnp.zeros_like(bias_ref)

    @pl.when(jnp.logical_not(every | none))
    def _():
        position = first + lax.broadcasted_iota(jnp.int32, (span, 128), 0)
        last = offset + lax.broadcasted_iota(jnp.int32, (span, 128), 1)
        shown = (position >= start) & (position <= last)
        bias_ref[...] = jnp.where(shown, 0.0, HIDDEN).astype(jnp.bfloat16)

    @pl.when(jnp.logical_not(none))
    def _():
        source_rows = GROUP * plan.rows
        row = lax.broadcasted_iota(jnp.int32, (plan.unit_rows, source_rows), 0)
        column = lax.broadcasted_iota(jnp.int32, (plan.unit_rows, source_rows), 1)
        query = lax.rem(row, plan.rows)
        device = lax.div(query, plan.rows_here)
        block = 2 * (lax.rem(device, plan.half) ^ low) + (lax.div(device, plan.half) ^ high)
        first_head = (mine * plan.heads) % GROUP
        head = first_head + lax.div(row, plan.rows)
        origin = (block * GROUP + head) * plan.rows_here + lax.rem(query, plan.rows_here)
        order = jnp.where(column == origin, 1.0, 0.0).astype(jnp.bfloat16)
        one_hot = jnp.where(
            lax.rem(lax.broadcasted_iota(jnp.int32, (plan.unit_rows, 128), 0), plan.rows)
            == lax.broadcasted_iota(jnp.int32, (plan.unit_rows, 128), 1),
            1.0,
            0.0,
        ).astype(jnp.bfloat16)
        ones = jnp.ones((chunk, 128), jnp.bfloat16)
        for unit in range(plan.units):
            group = (mine * plan.heads + unit * plan.unit_heads) // GROUP
            stacked = jnp.concatenate([ref[group] for ref in query_refs], axis=0)
            queries = jnp.dot(order, stacked, preferred_element_type=jnp.float32)
            queries = jnp.concatenate([queries.astype(jnp.bfloat16), one_hot], axis=1)
            key_at = pl.multiple_of(group * HD, HD)
            value_at = pl.multiple_of((KVH + group) * HD, HD)
            peak = None
            for at in range(0, span, chunk):
                keys = jnp.concatenate(
                    [cache_ref[at : at + chunk, pl.ds(key_at, HD)], bias_ref[at : at + chunk, :]], axis=1
                )
                scores = lax.dot_general(
                    queries, keys, (((1,), (1,)), ((), ())), preferred_element_type=jnp.float32
                )
                score_ref[unit, :, at : at + chunk] = scores
                for lane in range(0, chunk, 128):
                    piece = scores[:, lane : lane + 128]
                    peak = piece if peak is None else jnp.maximum(peak, piece)
            peak = jnp.max(peak, axis=1, keepdims=True) * LOG2_SCALE
            peak = jnp.maximum(jnp.ceil(peak * (1.0 / STEP)), FLOOR / STEP)
            shift = peak * STEP
            both = jnp.zeros((plan.unit_rows, 2 * HD), jnp.float32)
            for at in range(0, span, chunk):
                weights = jnp.exp2(score_ref[unit, :, at : at + chunk] * LOG2_SCALE - shift)
                values = jnp.concatenate([cache_ref[at : at + chunk, pl.ds(value_at, HD)], ones], axis=1)
                both += jnp.dot(weights.astype(jnp.bfloat16), values, preferred_element_type=jnp.float32)
            at = unit * plan.unit_rows
            out_ref[at : at + plan.unit_rows, :] = both[:, :HD].astype(jnp.bfloat16)
            pack_stats(plan, out_ref, unit, peak, both[:, HD:])


def attend(plan, part, offsets, starts, queries, cache):
    span = cache.shape[0]
    smem = pl.BlockSpec(memory_space=pltpu.SMEM)
    vmem = pl.BlockSpec(memory_space=pltpu.VMEM)
    return pl.pallas_call(
        functools.partial(attend_kernel, plan, part),
        out_shape=jax.ShapeDtypeStruct((plan.payload_rows, HD), jnp.bfloat16),
        in_specs=[smem, smem] + [vmem] * (len(queries) + 1),
        out_specs=vmem,
        scratch_shapes=[
            pltpu.VMEM((plan.units, plan.unit_rows, span), jnp.float32),
            pltpu.VMEM((span, 128), jnp.bfloat16),
        ],
        compiler_params=pltpu.CompilerParams(vmem_limit_bytes=VMEM_LIMIT),
        cost_estimate=pl.CostEstimate(
            flops=4 * plan.num_rows * span * HD,
            bytes_accessed=2 * plan.units * span * HD * 2,
            transcendentals=plan.num_rows * span,
        ),
        name="attend",
    )(offsets, starts, *queries, cache)


def merged(plan, refs, unit):
    stats = [unpack_stats(plan, ref, unit) for ref in refs]
    joint = functools.reduce(jnp.maximum, [peak for peak, _ in stats])
    at = unit * plan.unit_rows
    mixed, total = None, None
    for ref, (peak, weight) in zip(refs, stats):
        factor = jnp.exp2((peak - joint) * STEP)
        term = factor * ref[at : at + plan.unit_rows, :].astype(jnp.float32)
        mixed = term if mixed is None else mixed + term
        total = factor * weight if total is None else total + factor * weight
    return joint, total, mixed


def merge_kernel(plan, *refs):
    *parts, out_ref = refs
    for unit in range(plan.units):
        joint, total, mixed = merged(plan, parts, unit)
        at = unit * plan.unit_rows
        out_ref[at : at + plan.unit_rows, :] = mixed.astype(jnp.bfloat16)
        pack_stats(plan, out_ref, unit, joint, total)


def settle_kernel(plan, *refs):
    *parts, out_ref = refs
    for unit in range(plan.units):
        _, total, mixed = merged(plan, parts, unit)
        done = (mixed / total).astype(jnp.bfloat16)
        for head in range(plan.unit_heads):
            at = (unit * plan.unit_heads + head) * HD
            out_ref[:, at : at + HD] = done[head * plan.rows : (head + 1) * plan.rows, :]


def merge(plan, parts):
    vmem = pl.BlockSpec(memory_space=pltpu.VMEM)
    return pl.pallas_call(
        functools.partial(merge_kernel, plan),
        out_shape=jax.ShapeDtypeStruct((plan.payload_rows, HD), jnp.bfloat16),
        in_specs=[vmem] * len(parts),
        out_specs=vmem,
        compiler_params=pltpu.CompilerParams(vmem_limit_bytes=VMEM_LIMIT),
        name="merge",
    )(*parts)


def settle(plan, parts):
    vmem = pl.BlockSpec(memory_space=pltpu.VMEM)
    return pl.pallas_call(
        functools.partial(settle_kernel, plan),
        out_shape=jax.ShapeDtypeStruct((plan.rows, plan.heads * HD), jnp.bfloat16),
        in_specs=[vmem] * len(parts),
        out_specs=vmem,
        compiler_params=pltpu.CompilerParams(vmem_limit_bytes=VMEM_LIMIT),
        name="settle",
    )(*parts)


def project_kernel(plan, first, last, *refs):
    *refs, weight_ref, out_ref = refs
    depth = plan.heads * HD
    low = lax.axis_index("ctx") % plan.half
    total = None
    for k, ref in zip(range(first, last), refs):
        at = pl.multiple_of((low ^ k) * depth, depth)
        term = jnp.dot(ref[...], weight_ref[pl.ds(at, depth), :], preferred_element_type=jnp.float32)
        total = term if total is None else total + term
    if len(refs) > last - first:
        total = total + refs[-1][...]
    out_ref[...] = total.astype(out_ref.dtype)


def project(plan, first, blocks, weight, before, dtype):
    vmem = pl.BlockSpec(memory_space=pltpu.VMEM)
    extra = [] if before is None else [before]
    return pl.pallas_call(
        functools.partial(project_kernel, plan, first, first + len(blocks)),
        out_shape=jax.ShapeDtypeStruct((plan.rows, weight.shape[1]), dtype),
        in_specs=[vmem] * (len(blocks) + len(extra) + 1),
        out_specs=vmem,
        compiler_params=pltpu.CompilerParams(vmem_limit_bytes=VMEM_LIMIT),
        name="project",
    )(*blocks, *extra, weight)


def per_device(queries, cache, out_weight, offsets, starts):
    plan = Plan(lax.axis_size("ctx"), queries.shape[0])
    half = plan.half
    cache = pltpu.with_memory_space_constraint(cache, pltpu.VMEM)
    out_weight = pltpu.with_memory_space_constraint(out_weight, pltpu.VMEM)

    own = queries.reshape(plan.rows_here, KVH, GROUP, HD)
    own = own.transpose(1, 2, 0, 3).reshape(KVH, GROUP * plan.rows_here, HD)
    pair = jnp.concatenate([own, swap(own, "ctx", half)], axis=1)
    gathered = [pair] + [swap(pair, "ctx", k) for k in range(1, half)]

    received = []
    for part in range(1, half):
        piece = attend(plan, part, offsets, starts, gathered, cache)
        received.append(swap(piece, "ctx", part))
    kept = attend(plan, 0, offsets, starts, gathered, cache)
    near = merge(plan, [kept] + received)
    block = settle(plan, [near, swap(near, "ctx", half)])

    blocks = [block] + [swap(block, "ctx", k) for k in range(1, half)]
    begun = project(plan, 0, blocks[:1], out_weight, None, jnp.float32)
    projected = project(plan, 1, blocks[1:], out_weight, begun, jnp.bfloat16)
    return from_behind(projected, "segment", 1)


def solution(mesh):
    in_specs = (
        P(("segment", "ctx"), None),
        P(("segment", "ctx"), None),
        P("segment", "ctx"),
        P("segment"),
        P("segment"),
    )
    out_specs = P("segment", "ctx")
    return jax.shard_map(
        per_device, mesh=mesh, in_specs=in_specs, out_specs=out_specs, check_vma=False
    )
```

```python
import functools
import math

import jax
import jax.numpy as jnp
from jax import lax
from jax.experimental import pallas as pl
from jax.experimental.pallas import tpu as pltpu
from jax.sharding import PartitionSpec as P

H = 64
KVH = 8
HD = 128
GROUP = H // KVH
LOG2_SCALE = HD ** (-0.5) * math.log2(math.e)
STEP = 8.0
FLOOR = -4096.0
HIDDEN = -1e30
STATS = 16
VMEM_LIMIT = 12 * 1024 * 1024


def swap(value, axis, bits):
    devices = lax.axis_size(axis)
    return lax.ppermute(value, axis, [(i, i ^ bits) for i in range(devices)])


def from_behind(value, axis, by):
    devices = lax.axis_size(axis)
    return lax.ppermute(value, axis, [(i, (i + by) % devices) for i in range(devices)])


class Plan:
    def __init__(self, ctx, rows_here):
        self.ctx = ctx
        self.half = ctx // 2
        self.rows_here = rows_here
        self.rows = ctx * rows_here
        self.heads = H // self.half
        self.unit_heads = min(self.heads, GROUP)
        self.units = self.heads // self.unit_heads
        self.unit_rows = self.unit_heads * self.rows
        self.stat_blocks = self.unit_rows // 128
        self.num_rows = self.units * self.unit_rows
        self.payload_rows = self.num_rows + self.units * self.stat_blocks * STATS

    def stats_at(self, unit):
        return self.num_rows + unit * self.stat_blocks * STATS


def stage_kernel(rows, offset_ref, start_ref, cache_ref, staged_ref, bias_ref, sem):
    copy = pltpu.make_async_copy(cache_ref, staged_ref, sem)
    copy.start()
    span = cache_ref.shape[0]
    offset, start = offset_ref[0], start_ref[0]
    first = lax.axis_index("ctx") * span
    every = (first >= start) & (first + span - 1 <= offset)

    @pl.when(every)
    def _():
        bias_ref[...] = jnp.zeros_like(bias_ref)

    @pl.when(jnp.logical_not(every))
    def _():
        position = first + lax.broadcasted_iota(jnp.int32, (span, 128), 0)
        last = offset + lax.broadcasted_iota(jnp.int32, (span, 128), 1)
        shown = (position >= start) & (position <= last)
        bias_ref[...] = jnp.where(shown, 0.0, HIDDEN).astype(jnp.bfloat16)

    copy.wait()


def stage(plan, offsets, starts, cache):
    smem = pl.BlockSpec(memory_space=pltpu.SMEM)
    vmem = pl.BlockSpec(memory_space=pltpu.VMEM)
    return pl.pallas_call(
        functools.partial(stage_kernel, plan.rows),
        out_shape=[
            pltpu.VMEM(cache.shape, cache.dtype),
            pltpu.VMEM((cache.shape[0], 128), jnp.bfloat16),
        ],
        in_specs=[smem, smem, pl.BlockSpec(memory_space=pltpu.HBM)],
        out_specs=[vmem, vmem],
        scratch_shapes=[pltpu.SemaphoreType.DMA],
        compiler_params=pltpu.CompilerParams(vmem_limit_bytes=VMEM_LIMIT),
        cost_estimate=pl.CostEstimate(
            flops=0, bytes_accessed=2 * cache.shape[0] * cache.shape[1] * 2, transcendentals=0
        ),
        name="stage",
    )(offsets, starts, cache)


def pack_stats(plan, out_ref, unit, peak, total):
    lane = lax.broadcasted_iota(jnp.int32, (plan.unit_rows, 128), 1)
    high = total.astype(jnp.bfloat16).astype(jnp.float32)
    table = jnp.where(lane == 0, peak, jnp.where(lane == 1, high, total - high))
    turned = jnp.transpose(table)[:STATS].astype(jnp.bfloat16)
    for block in range(plan.stat_blocks):
        at = plan.stats_at(unit) + block * STATS
        out_ref[at : at + STATS, :] = turned[:, block * 128 : (block + 1) * 128]


def attend_kernel(plan, part, offset_ref, start_ref, *refs):
    *query_refs, cache_ref, bias_ref, out_ref = refs[: -1 - (part == 0)]
    score_ref = refs[-1]
    wide_ref = refs[-2] if part == 0 else None
    span = cache_ref.shape[0]
    me = lax.axis_index("ctx")
    low, high = me % plan.half, me // plan.half
    offset, start = offset_ref[0], start_ref[0]
    first = me * span
    none = (first + span - 1 < start) | (first > offset + plan.rows - 1)
    mine = low ^ part

    @pl.when(none)
    def _():
        out_ref[...] = jnp.zeros_like(out_ref)
        if wide_ref is not None:
            wide_ref[...] = jnp.zeros_like(wide_ref)
        for unit in range(plan.units):
            pack_stats(
                plan,
                out_ref,
                unit,
                jnp.full((plan.unit_rows, 128), FLOOR / STEP, jnp.float32),
                jnp.zeros((plan.unit_rows, 128), jnp.float32),
            )

    @pl.when(jnp.logical_not(none))
    def _():
        row = lax.broadcasted_iota(jnp.int32, (plan.unit_rows, 128), 0)
        lane = lax.broadcasted_iota(jnp.int32, (plan.unit_rows, 128), 1)
        query = lax.rem(row, plan.rows)
        device = lax.div(query, plan.rows_here)
        block = 2 * (lax.rem(device, plan.half) ^ low) + (lax.div(device, plan.half) ^ high)
        head = (mine * plan.heads) % GROUP + lax.div(row, plan.rows)
        origin = (block * GROUP + head) * plan.rows_here + lax.rem(query, plan.rows_here)
        order = jnp.concatenate(
            [
                jnp.where(lane + at == origin, 1.0, 0.0).astype(jnp.bfloat16)
                for at in range(0, GROUP * plan.rows, 128)
            ],
            axis=1,
        )
        one_hot = jnp.where(query == lane, 1.0, 0.0).astype(jnp.bfloat16)
        ones = jnp.ones((span, HD), jnp.bfloat16)
        groups = [(mine * plan.heads + unit * plan.unit_heads) // GROUP for unit in range(plan.units)]
        peaks = []
        for unit, group in enumerate(groups):
            stacked = jnp.concatenate([ref[group] for ref in query_refs], axis=0)
            queries = jnp.dot(order, stacked, preferred_element_type=jnp.float32)
            queries = jnp.concatenate([queries.astype(jnp.bfloat16), one_hot], axis=1)
            key_at = pl.multiple_of(group * HD, HD)
            keys = jnp.concatenate([cache_ref[:, pl.ds(key_at, HD)], bias_ref[...]], axis=1)
            scores = lax.dot_general(
                queries, keys, (((1,), (1,)), ((), ())), preferred_element_type=jnp.float32
            )
            score_ref[unit] = scores
            peak = [scores[:, at : at + 128] for at in range(0, span, 128)]
            while len(peak) > 1:
                peak = [jnp.maximum(*peak[i : i + 2]) for i in range(0, len(peak) - 1, 2)] + (
                    peak[-1:] if len(peak) % 2 else []
                )
            peak = jnp.max(peak[0], axis=1, keepdims=True) * LOG2_SCALE
            peaks.append(jnp.maximum(jnp.ceil(peak * (1.0 / STEP)), FLOOR / STEP))
        for unit, group in enumerate(groups):
            weights = jnp.exp2(score_ref[unit] * LOG2_SCALE - peaks[unit] * STEP)
            value_at = pl.multiple_of((KVH + group) * HD, HD)
            values = jnp.concatenate([cache_ref[:, pl.ds(value_at, HD)], ones], axis=1)
            both = jnp.dot(weights.astype(jnp.bfloat16), values, preferred_element_type=jnp.float32)
            at = unit * plan.unit_rows
            if wide_ref is not None:
                wide_ref[at : at + plan.unit_rows, :] = both[:, :HD]
            else:
                out_ref[at : at + plan.unit_rows, :] = both[:, :HD].astype(jnp.bfloat16)
            pack_stats(plan, out_ref, unit, peaks[unit], both[:, HD:])


def attend(plan, part, offsets, starts, queries, cache, bias):
    span = cache.shape[0]
    smem = pl.BlockSpec(memory_space=pltpu.SMEM)
    vmem = pl.BlockSpec(memory_space=pltpu.VMEM)
    out_shape = [jax.ShapeDtypeStruct((plan.payload_rows, HD), jnp.bfloat16)]
    if part == 0:
        out_shape.append(jax.ShapeDtypeStruct((plan.num_rows, HD), jnp.float32))
    return pl.pallas_call(
        functools.partial(attend_kernel, plan, part),
        out_shape=out_shape,
        in_specs=[smem, smem] + [vmem] * (len(queries) + 2),
        out_specs=[vmem] * len(out_shape),
        scratch_shapes=[pltpu.VMEM((plan.units, plan.unit_rows, span), jnp.float32)],
        compiler_params=pltpu.CompilerParams(vmem_limit_bytes=VMEM_LIMIT),
        cost_estimate=pl.CostEstimate(
            flops=4 * plan.num_rows * span * HD,
            bytes_accessed=2 * plan.units * span * HD * 2,
            transcendentals=plan.num_rows * span,
        ),
        name="attend",
    )(offsets, starts, *queries, cache, bias)


def columns(rows):
    index = lax.broadcasted_iota(jnp.int32, (128, 128), 0)
    table = jnp.zeros((128, 128), jnp.float32)
    for i, row in enumerate(rows):
        table = jnp.where(index == i, row, table)
    turned = jnp.transpose(table)
    return [turned[:, i : i + 1] for i in range(len(rows))]


def factors(plan, refs, unit, block):
    at = plan.stats_at(unit) + block * STATS
    stats = [ref[at : at + STATS, :].astype(jnp.float32) for ref in refs]
    joint = functools.reduce(jnp.maximum, [stat[0:1] for stat in stats])
    scale = [jnp.exp2((stat[0:1] - joint) * STEP) for stat in stats]
    total = functools.reduce(
        jnp.add, [factor * (stat[1:2] + stat[2:3]) for factor, stat in zip(scale, stats)]
    )
    return joint, scale, total


def mix(wide_ref, refs, at, scale):
    mixed = scale[0] * wide_ref[at : at + 128, :]
    for ref, factor in zip(refs[1:], scale[1:]):
        mixed = mixed + factor * ref[at : at + 128, :].astype(jnp.float32)
    return mixed


def merge_kernel(plan, wide_ref, *refs):
    *parts, out_ref, wide_out_ref = refs
    index = lax.broadcasted_iota(jnp.int32, (STATS, 128), 0)
    for unit in range(plan.units):
        for block in range(plan.stat_blocks):
            joint, scale, total = factors(plan, parts, unit, block)
            high = total.astype(jnp.bfloat16).astype(jnp.float32)
            at = plan.stats_at(unit) + block * STATS
            table = jnp.where(index == 0, joint, jnp.where(index == 1, high, total - high))
            out_ref[at : at + STATS, :] = table.astype(jnp.bfloat16)
            at = unit * plan.unit_rows + block * 128
            mixed = mix(wide_ref, parts, at, columns(scale))
            wide_out_ref[at : at + 128, :] = mixed
            out_ref[at : at + 128, :] = mixed.astype(jnp.bfloat16)


def settle_kernel(plan, wide_ref, *refs):
    *parts, out_ref = refs
    for unit in range(plan.units):
        for block in range(plan.stat_blocks):
            _, scale, total = factors(plan, parts, unit, block)
            at = unit * plan.unit_rows + block * 128
            done = mix(wide_ref, parts, at, columns([factor / total for factor in scale]))
            done = done.astype(jnp.bfloat16)
            for row in range(0, 128, plan.rows):
                to = (at + row) // plan.rows * HD
                out_ref[:, to : to + HD] = done[row : row + plan.rows, :]


def merge(plan, wide, parts):
    vmem = pl.BlockSpec(memory_space=pltpu.VMEM)
    return pl.pallas_call(
        functools.partial(merge_kernel, plan),
        out_shape=[
            jax.ShapeDtypeStruct((plan.payload_rows, HD), jnp.bfloat16),
            jax.ShapeDtypeStruct((plan.num_rows, HD), jnp.float32),
        ],
        in_specs=[vmem] * (len(parts) + 1),
        out_specs=[vmem, vmem],
        compiler_params=pltpu.CompilerParams(vmem_limit_bytes=VMEM_LIMIT),
        name="merge",
    )(wide, *parts)


def settle(plan, wide, parts):
    vmem = pl.BlockSpec(memory_space=pltpu.VMEM)
    return pl.pallas_call(
        functools.partial(settle_kernel, plan),
        out_shape=jax.ShapeDtypeStruct((plan.rows, plan.heads * HD), jnp.bfloat16),
        in_specs=[vmem] * (len(parts) + 1),
        out_specs=vmem,
        compiler_params=pltpu.CompilerParams(vmem_limit_bytes=VMEM_LIMIT),
        name="settle",
    )(wide, *parts)


def project_kernel(plan, first, last, *refs):
    *refs, weight_ref, out_ref = refs
    depth = plan.heads * HD
    low = lax.axis_index("ctx") % plan.half
    total = None
    for k, ref in zip(range(first, last), refs):
        at = pl.multiple_of((low ^ k) * depth, depth)
        term = jnp.dot(ref[...], weight_ref[pl.ds(at, depth), :], preferred_element_type=jnp.float32)
        total = term if total is None else total + term
    if len(refs) > last - first:
        total = total + refs[-1][...]
    out_ref[...] = total.astype(out_ref.dtype)


def project(plan, first, blocks, weight, before, dtype):
    vmem = pl.BlockSpec(memory_space=pltpu.VMEM)
    extra = [] if before is None else [before]
    return pl.pallas_call(
        functools.partial(project_kernel, plan, first, first + len(blocks)),
        out_shape=jax.ShapeDtypeStruct((plan.rows, weight.shape[1]), dtype),
        in_specs=[vmem] * (len(blocks) + len(extra) + 1),
        out_specs=vmem,
        compiler_params=pltpu.CompilerParams(vmem_limit_bytes=VMEM_LIMIT),
        name="project",
    )(*blocks, *extra, weight)


def per_device(queries, cache, out_weight, offsets, starts):
    plan = Plan(lax.axis_size("ctx"), queries.shape[0])
    half = plan.half
    cache = pltpu.with_memory_space_constraint(cache, pltpu.HBM)
    out_weight = pltpu.with_memory_space_constraint(out_weight, pltpu.VMEM)

    own = queries.reshape(plan.rows_here, KVH, GROUP, HD)
    own = own.transpose(1, 2, 0, 3).reshape(KVH, GROUP * plan.rows_here, HD)
    staged, bias = stage(plan, offsets, starts, cache)
    staged = pltpu.with_memory_space_constraint(staged, pltpu.VMEM)
    pair = jnp.concatenate([own, swap(own, "ctx", half)], axis=1)
    gathered = [pair] + [swap(pair, "ctx", k) for k in range(1, half)]

    received = []
    for part in reversed(range(1, half)):
        (piece,) = attend(plan, part, offsets, starts, gathered, staged, bias)
        received.append(swap(piece, "ctx", part))
    kept, wide = attend(plan, 0, offsets, starts, gathered, staged, bias)
    near, wide = merge(plan, wide, [kept] + received)
    block = settle(plan, wide, [near, swap(near, "ctx", half)])

    blocks = [block] + [swap(block, "ctx", k) for k in range(1, half)]
    total = project(plan, 0, blocks[:1], out_weight, None, jnp.float32)
    for k in range(1, half):
        last = k == half - 1
        total = project(plan, k, blocks[k : k + 1], out_weight, total, jnp.bfloat16 if last else jnp.float32)
    return from_behind(total, "segment", 1)


def solution(mesh):
    in_specs = (
        P(("segment", "ctx"), None),
        P(("segment", "ctx"), None),
        P("segment", "ctx"),
        P("segment"),
        P("segment"),
    )
    out_specs = P("segment", "ctx")
    return jax.shard_map(
        per_device, mesh=mesh, in_specs=in_specs, out_specs=out_specs, check_vma=False
    )
```

```python
import functools
import math

import jax
import jax.numpy as jnp
from jax import lax
from jax.experimental import pallas as pl
from jax.experimental.pallas import tpu as pltpu
from jax.sharding import PartitionSpec as P

H = 64
KVH = 8
HD = 128
GROUP = H // KVH
LOG2_SCALE = HD ** (-0.5) * math.log2(math.e)
STEP = 8.0
FLOOR = -4096.0
HIDDEN = -1e30
STATS = 16
VMEM_LIMIT = 12 * 1024 * 1024


def swap(value, axis, bits):
    devices = lax.axis_size(axis)
    return lax.ppermute(value, axis, [(i, i ^ bits) for i in range(devices)])


def from_behind(value, axis, by):
    devices = lax.axis_size(axis)
    return lax.ppermute(value, axis, [(i, (i + by) % devices) for i in range(devices)])


class Plan:
    def __init__(self, ctx, rows_here):
        self.ctx = ctx
        self.half = ctx // 2
        self.rows_here = rows_here
        self.rows = ctx * rows_here
        self.group_rows = GROUP * self.rows
        self.heads = H // self.half
        self.unit_heads = min(self.heads, GROUP)
        self.units = self.heads // self.unit_heads
        self.unit_rows = self.unit_heads * self.rows
        self.blocks = self.unit_rows // 128
        self.share_rows = self.units * self.unit_rows


def stat_rows(blocks):
    return -(-3 * blocks // 16) * 16


def local(kernel, out_shape, spaces, name, scratch=(), cost=None):
    return pl.pallas_call(
        kernel,
        out_shape=out_shape,
        in_specs=[pl.BlockSpec(memory_space=space) for space in spaces],
        out_specs=jax.tree.map(lambda _: pl.BlockSpec(memory_space=pltpu.VMEM), out_shape),
        scratch_shapes=list(scratch),
        compiler_params=pltpu.CompilerParams(vmem_limit_bytes=VMEM_LIMIT),
        cost_estimate=cost,
        name=name,
    )


def ready_kernel(plan, own_ref, held_ref, order_ref, one_hot_ref, sem):
    copy = pltpu.make_async_copy(own_ref, held_ref, sem)
    copy.start()
    me = lax.axis_index("ctx")
    low, high = me % plan.half, me // plan.half
    row = lax.broadcasted_iota(jnp.int32, (plan.group_rows, 128), 0)
    lane = lax.broadcasted_iota(jnp.int32, (plan.group_rows, 128), 1)
    query = lax.rem(row, plan.rows)
    device = lax.div(query, plan.rows_here)
    block = 2 * (lax.rem(device, plan.half) ^ low) + (lax.div(device, plan.half) ^ high)
    origin = (block * GROUP + lax.div(row, plan.rows)) * plan.rows_here + lax.rem(query, plan.rows_here)
    for at in range(0, plan.group_rows, 128):
        order_ref[:, at : at + 128] = jnp.where(lane + at == origin, 1.0, 0.0).astype(jnp.bfloat16)
    one_hot_ref[...] = jnp.where(query == lane, 1.0, 0.0).astype(jnp.bfloat16)
    copy.wait()


def ready(plan, own):
    return local(
        functools.partial(ready_kernel, plan),
        [
            pltpu.VMEM(own.shape, own.dtype),
            jax.ShapeDtypeStruct((plan.group_rows, plan.group_rows), jnp.bfloat16),
            jax.ShapeDtypeStruct((plan.group_rows, 128), jnp.bfloat16),
        ],
        [pltpu.HBM],
        "ready",
        [pltpu.SemaphoreType.DMA],
    )(pltpu.with_memory_space_constraint(own, pltpu.HBM))


def stage_kernel(plan, offset_ref, start_ref, cache_ref, staged_ref, bias_ref, sem):
    copy = pltpu.make_async_copy(cache_ref, staged_ref, sem)
    copy.start()
    span = cache_ref.shape[0]
    offset, start = offset_ref[0], start_ref[0]
    first = lax.axis_index("ctx") * span
    every = (first >= start) & (first + span - 1 <= offset)

    @pl.when(every)
    def _():
        bias_ref[...] = jnp.zeros_like(bias_ref)

    @pl.when(jnp.logical_not(every))
    def _():
        position = first + lax.broadcasted_iota(jnp.int32, (span, 128), 0)
        last = offset + lax.broadcasted_iota(jnp.int32, (span, 128), 1)
        shown = (position >= start) & (position <= last)
        bias_ref[...] = jnp.where(shown, 0.0, HIDDEN).astype(jnp.bfloat16)

    copy.wait()


def stage(plan, offsets, starts, cache):
    return local(
        functools.partial(stage_kernel, plan),
        [
            pltpu.VMEM(cache.shape, cache.dtype),
            jax.ShapeDtypeStruct((cache.shape[0], 128), jnp.bfloat16),
        ],
        [pltpu.SMEM, pltpu.SMEM, pltpu.HBM],
        "stage",
        [pltpu.SemaphoreType.DMA],
        pl.CostEstimate(flops=0, bytes_accessed=2 * cache.size * 2, transcendentals=0),
    )(offsets, starts, pltpu.with_memory_space_constraint(cache, pltpu.HBM))


def join_kernel(first_ref, second_ref, out_ref):
    rows = first_ref.shape[1]
    out_ref[:, :rows, :] = first_ref[...]
    out_ref[:, rows:, :] = second_ref[...]


def join(first, second):
    groups, rows, width = first.shape
    return local(
        join_kernel,
        jax.ShapeDtypeStruct((groups, 2 * rows, width), first.dtype),
        [pltpu.VMEM] * 2,
        "join",
    )(first, second)


def write_stats(ref, at, rows):
    values = []
    for peak, total in zip(rows[::2], rows[1::2]):
        high = total.astype(jnp.bfloat16).astype(jnp.float32)
        values += [peak, high, total - high]
    size = stat_rows(len(rows) // 2)
    index = lax.broadcasted_iota(jnp.int32, (size, 128), 0)
    table = jnp.zeros((size, 128), jnp.float32)
    for i, value in enumerate(values):
        table = jnp.where(index == i, value, table)
    ref[at : at + size, :] = table.astype(jnp.bfloat16)


def attend_kernel(plan, part, offset_ref, start_ref, *refs):
    *query_refs, cache_ref, bias_ref, order_ref, one_hot_ref, out_ref = refs[: -1 - (part == 0)]
    score_ref = refs[-1]
    value_ref, stat_ref, stat_at = (out_ref, refs[-2], 0) if part == 0 else (out_ref, out_ref, plan.share_rows)
    span = cache_ref.shape[0]
    me = lax.axis_index("ctx")
    first = me * span
    none = (first + span - 1 < start_ref[0]) | (first > offset_ref[0] + plan.rows - 1)
    mine = (me % plan.half) ^ part

    @pl.when(none)
    def _():
        value_ref[: plan.share_rows, :] = jnp.zeros((plan.share_rows, HD), value_ref.dtype)
        empty = [jnp.full((1, 128), FLOOR / STEP, jnp.float32), jnp.zeros((1, 128), jnp.float32)]
        write_stats(stat_ref, stat_at, empty * (plan.units * plan.blocks))

    @pl.when(jnp.logical_not(none))
    def _():
        row_at = pl.multiple_of((mine * plan.heads) % GROUP * plan.rows, plan.unit_rows)
        order = order_ref[pl.ds(row_at, plan.unit_rows), :]
        one_hot = one_hot_ref[pl.ds(row_at, plan.unit_rows), :]
        ones = jnp.ones((span, HD), jnp.bfloat16)
        groups = [(mine * plan.heads + unit * plan.unit_heads) // GROUP for unit in range(plan.units)]
        peaks = []
        for unit, group in enumerate(groups):
            stacked = jnp.concatenate([ref[group] for ref in query_refs], axis=0)
            queries = jnp.dot(order, stacked, preferred_element_type=jnp.float32)
            queries = jnp.concatenate([queries.astype(jnp.bfloat16), one_hot], axis=1)
            key_at = pl.multiple_of(group * HD, HD)
            keys = jnp.concatenate([cache_ref[:, pl.ds(key_at, HD)], bias_ref[...]], axis=1)
            scores = lax.dot_general(
                queries, keys, (((1,), (1,)), ((), ())), preferred_element_type=jnp.float32
            )
            score_ref[unit] = scores
            peak = [scores[:, at : at + 128] for at in range(0, span, 128)]
            while len(peak) > 1:
                peak = [jnp.maximum(*peak[i : i + 2]) for i in range(0, len(peak) - 1, 2)] + (
                    peak[-1:] if len(peak) % 2 else []
                )
            peak = jnp.max(peak[0], axis=1, keepdims=True) * LOG2_SCALE
            peak = jnp.maximum(jnp.ceil(peak * (1.0 / STEP)), FLOOR / STEP)
            peaks.append(jnp.broadcast_to(peak, (plan.unit_rows, 128)))
        same = lax.broadcasted_iota(jnp.int32, (128, 128), 0) == lax.broadcasted_iota(
            jnp.int32, (128, 128), 1
        )
        stats = []
        for unit, group in enumerate(groups):
            shift = jnp.concatenate([peaks[unit] * STEP] * (span // 128), axis=1)
            weights = jnp.exp2(score_ref[unit] * LOG2_SCALE - shift)
            value_at = pl.multiple_of((KVH + group) * HD, HD)
            values = jnp.concatenate([cache_ref[:, pl.ds(value_at, HD)], ones], axis=1)
            both = jnp.dot(weights.astype(jnp.bfloat16), values, preferred_element_type=jnp.float32)
            at = unit * plan.unit_rows
            value_ref[at : at + plan.unit_rows, :] = both[:, :HD].astype(value_ref.dtype)
            for block in range(0, plan.unit_rows, 128):
                for wide in (peaks[unit], both[:, HD:]):
                    chosen = jnp.where(same, wide[block : block + 128, :], 0.0)
                    stats.append(jnp.sum(chosen, axis=0, keepdims=True))
        write_stats(stat_ref, stat_at, stats)


def attend(plan, part, offsets, starts, queries, cache, *tables):
    span = cache.shape[0]
    size = stat_rows(plan.units * plan.blocks)
    if part == 0:
        out_shape = [
            jax.ShapeDtypeStruct((plan.share_rows, HD), jnp.float32),
            jax.ShapeDtypeStruct((size, HD), jnp.bfloat16),
        ]
    else:
        out_shape = [jax.ShapeDtypeStruct((plan.share_rows + size, HD), jnp.bfloat16)]
    return local(
        functools.partial(attend_kernel, plan, part),
        out_shape,
        [pltpu.SMEM] * 2 + [pltpu.VMEM] * (len(queries) + 1 + len(tables)),
        "attend",
        [pltpu.VMEM((plan.units, plan.unit_rows, span), jnp.float32)],
        pl.CostEstimate(
            flops=4 * plan.share_rows * span * HD,
            bytes_accessed=2 * plan.units * span * HD * 2,
            transcendentals=plan.share_rows * span,
        ),
    )(offsets, starts, *queries, cache, *tables)


def columns(rows):
    index = lax.broadcasted_iota(jnp.int32, (128, 128), 0)
    table = jnp.zeros((128, 128), jnp.float32)
    for i, row in enumerate(rows):
        table = jnp.where(index == i, row, table)
    turned = jnp.transpose(table)
    return [turned[:, i : i + 1] for i in range(len(rows))]


def factors(stats, block):
    parts = []
    for ref, at in stats:
        base = 3 * block // 16 * 16
        tile = ref[at + base : at + min(base + 32, stat_rows(block + 1)), :].astype(jnp.float32)
        begin = 3 * block - base
        parts.append([tile[begin + i : begin + i + 1] for i in range(3)])
    joint = functools.reduce(jnp.maximum, [peak for peak, _, _ in parts])
    scale = [jnp.exp2((peak - joint) * STEP) for peak, _, _ in parts]
    total = functools.reduce(jnp.add, [f * (high + low) for f, (_, high, low) in zip(scale, parts)])
    return joint, scale, total


def mix(refs, at, scale):
    terms = [f * ref[at : at + 128, :].astype(jnp.float32) for ref, f in zip(refs, scale)]
    return functools.reduce(jnp.add, terms)


def merge_kernel(plan, unit, wide_ref, stat_ref, *refs):
    *parts, out_ref, wide_out_ref = refs
    stats = [(stat_ref, 0)] + [(ref, plan.share_rows) for ref in parts]
    rows = []
    for block in range(plan.blocks):
        joint, scale, total = factors(stats, unit * plan.blocks + block)
        rows += [joint, total]
        to = block * 128
        mixed = mix([wide_ref] + parts, unit * plan.unit_rows + to, columns(scale))
        wide_out_ref[to : to + 128, :] = mixed
        out_ref[to : to + 128, :] = mixed.astype(jnp.bfloat16)
    write_stats(out_ref, plan.unit_rows, rows)


def merge(plan, unit, wide, stats, parts):
    rows = plan.unit_rows + stat_rows(plan.blocks)
    return local(
        functools.partial(merge_kernel, plan, unit),
        [
            jax.ShapeDtypeStruct((rows, HD), jnp.bfloat16),
            jax.ShapeDtypeStruct((plan.unit_rows, HD), jnp.float32),
        ],
        [pltpu.VMEM] * (len(parts) + 2),
        "merge",
    )(wide, stats, *parts)


def settle_kernel(plan, wide_ref, own_ref, other_ref, out_ref):
    stats = [(own_ref, plan.unit_rows), (other_ref, plan.unit_rows)]
    for block in range(plan.blocks):
        _, scale, total = factors(stats, block)
        done = mix([wide_ref, other_ref], block * 128, columns([f / total for f in scale]))
        done = done.astype(jnp.bfloat16)
        for row in range(0, 128, plan.rows):
            to = (block * 128 + row) // plan.rows * HD
            out_ref[:, to : to + HD] = done[row : row + plan.rows, :]


def settle(plan, wide, own, other):
    return local(
        functools.partial(settle_kernel, plan),
        jax.ShapeDtypeStruct((plan.rows, plan.unit_heads * HD), jnp.bfloat16),
        [pltpu.VMEM] * 3,
        "settle",
    )(wide, own, other)


def project_kernel(plan, part, unit, *refs):
    block_ref, weight_ref, *before, out_ref = refs
    depth = plan.unit_heads * HD
    share = (lax.axis_index("ctx") % plan.half) ^ part
    at = pl.multiple_of((share * plan.units + unit) * depth, depth)
    total = jnp.dot(block_ref[...], weight_ref[pl.ds(at, depth), :], preferred_element_type=jnp.float32)
    for ref in before:
        total = total + ref[...]
    out_ref[...] = total.astype(out_ref.dtype)


def project(plan, part, unit, block, weight, before, dtype):
    operands = [block, weight] + ([] if before is None else [before])
    return local(
        functools.partial(project_kernel, plan, part, unit),
        jax.ShapeDtypeStruct((plan.rows, weight.shape[1]), dtype),
        [pltpu.VMEM] * len(operands),
        "project",
    )(*operands)


def per_device(queries, cache, out_weight, offsets, starts):
    plan = Plan(lax.axis_size("ctx"), queries.shape[0])
    half = plan.half
    out_weight = pltpu.with_memory_space_constraint(out_weight, pltpu.VMEM)

    own = queries.reshape(plan.rows_here, KVH, GROUP, HD)
    own = own.transpose(1, 2, 0, 3).reshape(KVH, GROUP * plan.rows_here, HD)
    held, *order = ready(plan, own)
    staged, bias = stage(plan, offsets, starts, cache)
    staged = pltpu.with_memory_space_constraint(staged, pltpu.VMEM)
    pair = join(held, swap(own, "ctx", half))
    gathered = [pair] + [swap(pair, "ctx", k) for k in range(1, half)]

    received = []
    for part in reversed(range(1, half)):
        (piece,) = attend(plan, part, offsets, starts, gathered, staged, bias, *order)
        received.append(swap(piece, "ctx", part))
    wide, stats = attend(plan, 0, offsets, starts, gathered, staged, bias, *order)

    blocks = []
    for unit in range(plan.units):
        near, near_wide = merge(plan, unit, wide, stats, received)
        block = settle(plan, near_wide, near, swap(near, "ctx", half))
        blocks.append([block] + [swap(block, "ctx", k) for k in range(1, half)])

    steps = [(part, unit) for unit in range(plan.units) for part in range(half)]
    total = None
    for part, unit in steps:
        dtype = jnp.bfloat16 if (part, unit) == steps[-1] else jnp.float32
        total = project(plan, part, unit, blocks[unit][part], out_weight, total, dtype)
    return from_behind(total, "segment", 1)


def solution(mesh):
    in_specs = (
        P(("segment", "ctx"), None),
        P(("segment", "ctx"), None),
        P("segment", "ctx"),
        P("segment"),
        P("segment"),
    )
    out_specs = P("segment", "ctx")
    return jax.shard_map(
        per_device, mesh=mesh, in_specs=in_specs, out_specs=out_specs, check_vma=False
    )
```

```python
import functools
import math

import jax
import jax.numpy as jnp
from jax import lax
from jax.experimental import pallas as pl
from jax.experimental.pallas import tpu as pltpu
from jax.sharding import PartitionSpec as P

H = 64
KVH = 8
HD = 128
GROUP = H // KVH
LOG2_SCALE = HD ** (-0.5) * math.log2(math.e)
STEP = 8.0
FLOOR = -4096.0
HIDDEN = -1e30
STATS = 16
VMEM_LIMIT = 12 * 1024 * 1024


def swap(value, axis, bits):
    devices = lax.axis_size(axis)
    return lax.ppermute(value, axis, [(i, i ^ bits) for i in range(devices)])


def from_behind(value, axis, by):
    devices = lax.axis_size(axis)
    return lax.ppermute(value, axis, [(i, (i + by) % devices) for i in range(devices)])


class Plan:
    def __init__(self, ctx, rows_here):
        self.ctx = ctx
        self.half = ctx // 2
        self.fold = self.half // 2
        self.across = self.half | self.fold
        self.rows_here = rows_here
        self.rows = ctx * rows_here
        self.group_rows = GROUP * self.rows
        self.heads = H // self.half
        self.unit_heads = min(self.heads, GROUP)
        self.units = self.heads // self.unit_heads
        self.unit_rows = self.unit_heads * self.rows
        self.blocks = self.unit_rows // 128
        self.share_rows = self.units * self.unit_rows

    def share(self, part):
        me = lax.axis_index("ctx")
        return (me % self.half) ^ (me // self.half * self.fold) ^ part


def stat_rows(blocks):
    return -(-3 * blocks // 16) * 16


def local(kernel, out_shape, spaces, name, scratch=(), cost=None):
    return pl.pallas_call(
        kernel,
        out_shape=out_shape,
        in_specs=[pl.BlockSpec(memory_space=space) for space in spaces],
        out_specs=jax.tree.map(lambda _: pl.BlockSpec(memory_space=pltpu.VMEM), out_shape),
        scratch_shapes=list(scratch),
        compiler_params=pltpu.CompilerParams(vmem_limit_bytes=VMEM_LIMIT),
        cost_estimate=cost,
        name=name,
    )


def ready_kernel(plan, offset_ref, start_ref, own_ref, held_ref, order_ref, one_hot_ref, bias_ref, sem):
    copy = pltpu.make_async_copy(own_ref, held_ref, sem)
    copy.start()
    me = lax.axis_index("ctx")
    low, high = me % plan.half, me // plan.half
    row = lax.broadcasted_iota(jnp.int32, (plan.group_rows, 128), 0)
    lane = lax.broadcasted_iota(jnp.int32, (plan.group_rows, 128), 1)
    query = lax.rem(row, plan.rows)
    device = lax.div(query, plan.rows_here)
    block = 2 * (lax.rem(device, plan.half) ^ low) + (lax.div(device, plan.half) ^ high)
    origin = (block * GROUP + lax.div(row, plan.rows)) * plan.rows_here + lax.rem(query, plan.rows_here)
    for at in range(0, plan.group_rows, 128):
        order_ref[:, at : at + 128] = jnp.where(lane + at == origin, 1.0, 0.0).astype(jnp.bfloat16)
    one_hot_ref[...] = jnp.where(query == lane, 1.0, 0.0).astype(jnp.bfloat16)
    span = bias_ref.shape[0]
    offset, start = offset_ref[0], start_ref[0]
    first = me * span
    every = (first >= start) & (first + span - 1 <= offset)

    @pl.when(every)
    def _():
        bias_ref[...] = jnp.zeros_like(bias_ref)

    @pl.when(jnp.logical_not(every))
    def _():
        position = first + lax.broadcasted_iota(jnp.int32, (span, 128), 0)
        last = offset + lax.broadcasted_iota(jnp.int32, (span, 128), 1)
        shown = (position >= start) & (position <= last)
        bias_ref[...] = jnp.where(shown, 0.0, HIDDEN).astype(jnp.bfloat16)

    copy.wait()


def ready(plan, span, offsets, starts, own):
    return local(
        functools.partial(ready_kernel, plan),
        [
            pltpu.VMEM(own.shape, own.dtype),
            jax.ShapeDtypeStruct((plan.group_rows, plan.group_rows), jnp.bfloat16),
            jax.ShapeDtypeStruct((plan.group_rows, 128), jnp.bfloat16),
            jax.ShapeDtypeStruct((span, 128), jnp.bfloat16),
        ],
        [pltpu.SMEM, pltpu.SMEM, pltpu.HBM],
        "ready",
        [pltpu.SemaphoreType.DMA],
        pl.CostEstimate(flops=8_000_000_000, bytes_accessed=4 * span * HD, transcendentals=0),
    )(offsets, starts, pltpu.with_memory_space_constraint(own, pltpu.HBM))


def write_stats(ref, at, rows):
    values = []
    for peak, total in zip(rows[::2], rows[1::2]):
        high = total.astype(jnp.bfloat16).astype(jnp.float32)
        values += [peak, high, total - high]
    size = stat_rows(len(rows) // 2)
    index = lax.broadcasted_iota(jnp.int32, (size, 128), 0)
    table = jnp.zeros((size, 128), jnp.float32)
    for i, value in enumerate(values):
        table = jnp.where(index == i, value, table)
    ref[at : at + size, :] = table.astype(jnp.bfloat16)


def attend_kernel(plan, part, *refs):
    *query_refs, cache_ref, bias_ref, order_ref, one_hot_ref, out_ref = refs[: -1 - (part == 0)]
    score_ref = refs[-1]
    value_ref, stat_ref, stat_at = (out_ref, refs[-2], 0) if part == 0 else (out_ref, out_ref, plan.share_rows)
    span = cache_ref.shape[0]
    mine = plan.share(part)
    row_at = pl.multiple_of((mine * plan.heads) % GROUP * plan.rows, plan.unit_rows)
    order = order_ref[pl.ds(row_at, plan.unit_rows), :]
    one_hot = one_hot_ref[pl.ds(row_at, plan.unit_rows), :]
    ones = jnp.ones((span, HD), jnp.bfloat16)
    groups = [(mine * plan.heads + unit * plan.unit_heads) // GROUP for unit in range(plan.units)]
    peaks = []
    for unit, group in enumerate(groups):
        stacked = jnp.concatenate([ref[group] for ref in query_refs], axis=0)
        queries = jnp.dot(order, stacked, preferred_element_type=jnp.float32)
        queries = jnp.concatenate([queries.astype(jnp.bfloat16), one_hot], axis=1)
        key_at = pl.multiple_of(group * HD, HD)
        keys = jnp.concatenate([cache_ref[:, pl.ds(key_at, HD)], bias_ref[...]], axis=1)
        scores = lax.dot_general(queries, keys, (((1,), (1,)), ((), ())), preferred_element_type=jnp.float32)
        score_ref[unit] = scores
        peak = [scores[:, at : at + 128] for at in range(0, span, 128)]
        while len(peak) > 1:
            peak = [jnp.maximum(*peak[i : i + 2]) for i in range(0, len(peak) - 1, 2)] + (
                peak[-1:] if len(peak) % 2 else []
            )
        peak = jnp.max(peak[0], axis=1, keepdims=True) * LOG2_SCALE
        peak = jnp.maximum(jnp.ceil(peak * (1.0 / STEP)), FLOOR / STEP)
        peaks.append(jnp.broadcast_to(peak, (plan.unit_rows, 128)))
    same = lax.broadcasted_iota(jnp.int32, (128, 128), 0) == lax.broadcasted_iota(jnp.int32, (128, 128), 1)
    stats = []
    for unit, group in enumerate(groups):
        shift = jnp.concatenate([peaks[unit] * STEP] * (span // 128), axis=1)
        weights = jnp.exp2(score_ref[unit] * LOG2_SCALE - shift)
        value_at = pl.multiple_of((KVH + group) * HD, HD)
        values = jnp.concatenate([cache_ref[:, pl.ds(value_at, HD)], ones], axis=1)
        both = jnp.dot(weights.astype(jnp.bfloat16), values, preferred_element_type=jnp.float32)
        at = unit * plan.unit_rows
        value_ref[at : at + plan.unit_rows, :] = both[:, :HD].astype(value_ref.dtype)
        for block in range(0, plan.unit_rows, 128):
            for wide in (peaks[unit], both[:, HD:]):
                chosen = jnp.where(same, wide[block : block + 128, :], 0.0)
                stats.append(jnp.sum(chosen, axis=0, keepdims=True))
    write_stats(stat_ref, stat_at, stats)


def attend(plan, part, queries, cache, *tables):
    span = cache.shape[0]
    size = stat_rows(plan.units * plan.blocks)
    if part == 0:
        out_shape = [
            jax.ShapeDtypeStruct((plan.share_rows, HD), jnp.float32),
            jax.ShapeDtypeStruct((size, HD), jnp.bfloat16),
        ]
    else:
        out_shape = [jax.ShapeDtypeStruct((plan.share_rows + size, HD), jnp.bfloat16)]
    return local(
        functools.partial(attend_kernel, plan, part),
        out_shape,
        [pltpu.VMEM] * (len(queries) + 1 + len(tables)),
        "attend",
        [pltpu.VMEM((plan.units, plan.unit_rows, span), jnp.float32)],
        pl.CostEstimate(
            flops=4 * plan.share_rows * span * HD,
            bytes_accessed=2 * plan.units * span * HD * 2,
            transcendentals=plan.share_rows * span,
        ),
    )(*queries, cache, *tables)


def columns(rows):
    index = lax.broadcasted_iota(jnp.int32, (128, 128), 0)
    table = jnp.zeros((128, 128), jnp.float32)
    for i, row in enumerate(rows):
        table = jnp.where(index == i, row, table)
    turned = jnp.transpose(table)
    return [turned[:, i : i + 1] for i in range(len(rows))]


def factors(stats, block):
    parts = []
    for ref, at in stats:
        base = 3 * block // 16 * 16
        tile = ref[at + base : at + min(base + 32, stat_rows(block + 1)), :].astype(jnp.float32)
        begin = 3 * block - base
        parts.append([tile[begin + i : begin + i + 1] for i in range(3)])
    joint = functools.reduce(jnp.maximum, [peak for peak, _, _ in parts])
    scale = [jnp.exp2((peak - joint) * STEP) for peak, _, _ in parts]
    total = functools.reduce(jnp.add, [f * (high + low) for f, (_, high, low) in zip(scale, parts)])
    return joint, scale, total


def mix(refs, at, scale):
    terms = [f * ref[at : at + 128, :].astype(jnp.float32) for ref, f in zip(refs, scale)]
    return functools.reduce(jnp.add, terms)


def merge_kernel(plan, wide_ref, stat_ref, *refs):
    *parts, out_ref, wide_out_ref = refs
    stats = [(stat_ref, 0)] + [(ref, plan.share_rows) for ref in parts]
    rows = []
    for block in range(plan.units * plan.blocks):
        joint, scale, total = factors(stats, block)
        rows += [joint, total]
        at = block * 128
        mixed = mix([wide_ref] + parts, at, columns(scale))
        wide_out_ref[at : at + 128, :] = mixed
        out_ref[at : at + 128, :] = mixed.astype(jnp.bfloat16)
    write_stats(out_ref, plan.share_rows, rows)


def merge(plan, wide, stats, parts):
    rows = plan.share_rows + stat_rows(plan.units * plan.blocks)
    return local(
        functools.partial(merge_kernel, plan),
        [
            jax.ShapeDtypeStruct((rows, HD), jnp.bfloat16),
            jax.ShapeDtypeStruct((plan.share_rows, HD), jnp.float32),
        ],
        [pltpu.VMEM] * (len(parts) + 2),
        "merge",
    )(wide, stats, *parts)


def settle_kernel(plan, wide_ref, own_ref, other_ref, out_ref):
    stats = [(own_ref, plan.share_rows), (other_ref, plan.share_rows)]
    for block in range(plan.units * plan.blocks):
        _, scale, total = factors(stats, block)
        done = mix([wide_ref, other_ref], block * 128, columns([f / total for f in scale]))
        done = done.astype(jnp.bfloat16)
        for row in range(0, 128, plan.rows):
            to = (block * 128 + row) // plan.rows * HD
            out_ref[:, to : to + HD] = done[row : row + plan.rows, :]


def settle(plan, wide, own, other):
    return local(
        functools.partial(settle_kernel, plan),
        jax.ShapeDtypeStruct((plan.rows, plan.heads * HD), jnp.bfloat16),
        [pltpu.VMEM] * 3,
        "settle",
    )(wide, own, other)


def project_kernel(plan, part, *refs):
    block_ref, weight_ref, *before, out_ref = refs
    depth = plan.heads * HD
    at = pl.multiple_of(plan.share(part) * depth, depth)
    total = jnp.dot(block_ref[...], weight_ref[pl.ds(at, depth), :], preferred_element_type=jnp.float32)
    for ref in before:
        total = total + ref[...]
    out_ref[...] = total.astype(out_ref.dtype)


def project(plan, part, block, weight, before, dtype):
    operands = [block, weight] + ([] if before is None else [before])
    return local(
        functools.partial(project_kernel, plan, part),
        jax.ShapeDtypeStruct((plan.rows, weight.shape[1]), dtype),
        [pltpu.VMEM] * len(operands),
        "project",
    )(*operands)


def per_device(queries, cache, out_weight, offsets, starts):
    plan = Plan(lax.axis_size("ctx"), queries.shape[0])
    half = plan.half
    cache = pltpu.with_memory_space_constraint(cache, pltpu.VMEM)
    out_weight = pltpu.with_memory_space_constraint(out_weight, pltpu.VMEM)

    own = queries.reshape(plan.rows_here, KVH, GROUP, HD)
    own = own.transpose(1, 2, 0, 3).reshape(KVH, GROUP * plan.rows_here, HD)
    held, order, one_hot, bias = ready(plan, cache.shape[0], offsets, starts, own)
    far = swap(own, "ctx", half)
    if own.shape[1] % 16 == 0:
        gathered = [held, far]
        near = [swap(own, "ctx", k) for k in range(1, half)]
        for k in range(1, half):
            gathered += [near[k - 1], swap(far, "ctx", k)]
    else:
        pair = jnp.concatenate([own, far], axis=1)
        gathered = [pair] + [swap(pair, "ctx", k) for k in range(1, half)]

    received = []
    for part in reversed(range(1, half)):
        (piece,) = attend(plan, part, gathered, cache, bias, order, one_hot)
        received.append(swap(piece, "ctx", part))
    wide, stats = attend(plan, 0, gathered, cache, bias, order, one_hot)

    near, near_wide = merge(plan, wide, stats, received)
    block = settle(plan, near_wide, near, swap(near, "ctx", plan.across))

    total = project(plan, 0, block, out_weight, None, jnp.float32)
    blocks = [swap(block, "ctx", k) for k in range(1, half)]
    for k in range(1, half):
        dtype = jnp.float32 if k < half - 1 else jnp.bfloat16
        total = project(plan, k, blocks[k - 1], out_weight, total, dtype)
    return from_behind(total, "segment", 1)


def solution(mesh):
    in_specs = (
        P(("segment", "ctx"), None),
        P(("segment", "ctx"), None),
        P("segment", "ctx"),
        P("segment"),
        P("segment"),
    )
    out_specs = P("segment", "ctx")
    return jax.shard_map(
        per_device, mesh=mesh, in_specs=in_specs, out_specs=out_specs, check_vma=False
    )
```

```python
import functools
import math

import jax
import jax.numpy as jnp
from jax import lax
from jax.experimental import pallas as pl
from jax.experimental.pallas import tpu as pltpu
from jax.sharding import PartitionSpec as P

H = 64
KVH = 8
HD = 128
GROUP = H // KVH
LOG2_SCALE = HD ** (-0.5) * math.log2(math.e)
STEP = 8.0
FLOOR = -4096.0
HIDDEN = -1e30
STATS = 16
VMEM_LIMIT = 12 * 1024 * 1024


def swap(value, axis, bits):
    devices = lax.axis_size(axis)
    return lax.ppermute(value, axis, [(i, i ^ bits) for i in range(devices)])


def from_behind(value, axis, by):
    devices = lax.axis_size(axis)
    return lax.ppermute(value, axis, [(i, (i + by) % devices) for i in range(devices)])


class Plan:
    def __init__(self, ctx, rows_here):
        self.ctx = ctx
        self.half = ctx // 2
        self.fold = self.half // 2
        self.across = self.half | self.fold
        self.rows_here = rows_here
        self.rows = ctx * rows_here
        self.side_rows = self.rows // 2
        self.group_rows = GROUP * self.side_rows
        self.heads = H // self.half
        self.unit_heads = min(self.heads, GROUP)
        self.units = self.heads // self.unit_heads
        self.piece = self.unit_heads * self.side_rows
        self.side = self.units * self.piece
        self.share_rows = 2 * self.side
        self.stats = stat_rows(2 * self.units)

    def share(self, part):
        me = lax.axis_index("ctx")
        return (me % self.half) ^ (me // self.half * self.fold) ^ part


def stat_rows(pieces):
    return -(-3 * pieces // 16) * 16


def local(kernel, out_shape, spaces, name, scratch=(), cost=None):
    return pl.pallas_call(
        kernel,
        out_shape=out_shape,
        in_specs=[pl.BlockSpec(memory_space=space) for space in spaces],
        out_specs=jax.tree.map(lambda _: pl.BlockSpec(memory_space=pltpu.VMEM), out_shape),
        scratch_shapes=list(scratch),
        compiler_params=pltpu.CompilerParams(vmem_limit_bytes=VMEM_LIMIT),
        cost_estimate=cost,
        name=name,
    )


def ready_kernel(plan, offset_ref, start_ref, after_ref, order_ref, one_hot_ref, bias_ref):
    del after_ref
    me = lax.axis_index("ctx")
    low, high = me % plan.half, me // plan.half
    row = lax.broadcasted_iota(jnp.int32, (plan.group_rows, 128), 0)
    lane = lax.broadcasted_iota(jnp.int32, (plan.group_rows, 128), 1)
    query = lax.rem(row, plan.side_rows)
    block = lax.div(query, plan.rows_here) ^ low
    origin = (block * GROUP + lax.div(row, plan.side_rows)) * plan.rows_here + lax.rem(query, plan.rows_here)
    for at in range(0, plan.group_rows, 128):
        order_ref[:, at : at + 128] = jnp.where(lane + at == origin, 1.0, 0.0).astype(jnp.bfloat16)
    for side in range(2):
        here = jnp.where(query + side * plan.side_rows == lane, 1.0, 0.0)
        one_hot_ref[side] = here.astype(jnp.bfloat16)
    span = bias_ref.shape[1]
    first = me * span
    position = first + lax.broadcasted_iota(jnp.int32, (plan.rows, span), 1)
    index = lax.broadcasted_iota(jnp.int32, (plan.rows, span), 0)
    asked = jnp.where(index < plan.side_rows, index + high * plan.side_rows, index - high * plan.side_rows)
    shown = (position >= start_ref[...]) & (position <= offset_ref[...] + asked)
    bias_ref[: plan.rows, :] = jnp.where(shown, 0.0, HIDDEN).astype(jnp.bfloat16)
    bias_ref[plan.rows :, :] = jnp.zeros((128 - plan.rows, span), jnp.bfloat16)


def ready(plan, span, offsets, starts, after):
    return local(
        functools.partial(ready_kernel, plan),
        [
            jax.ShapeDtypeStruct((plan.group_rows, plan.group_rows), jnp.bfloat16),
            jax.ShapeDtypeStruct((2, plan.group_rows, 128), jnp.bfloat16),
            jax.ShapeDtypeStruct((128, span), jnp.bfloat16),
        ],
        [pltpu.VMEM, pltpu.VMEM, pl.ANY],
        "ready",
    )(offsets.reshape(1, 1), starts.reshape(1, 1), after)


def turn_kernel(cache_ref, after_ref, out_ref, held_ref, sems):
    del after_ref
    copies = [
        pltpu.make_async_copy(cache_ref.at[:, pl.ds(group * HD, HD)], held_ref.at[group], sems.at[group])
        for group in range(KVH)
    ]
    for copy in copies:
        copy.start()
    for group, copy in enumerate(copies):
        copy.wait()
        out_ref[group] = jnp.transpose(held_ref[group])


def turn(cache, after):
    span = cache.shape[0]
    return local(
        turn_kernel,
        pltpu.VMEM((KVH, HD, span), cache.dtype),
        [pltpu.HBM, pl.ANY],
        "turn",
        [pltpu.VMEM((KVH, span, HD), cache.dtype), pltpu.SemaphoreType.DMA((KVH,))],
        pl.CostEstimate(flops=8_000_000_000, bytes_accessed=4 * KVH * HD * span, transcendentals=0),
    )(pltpu.with_memory_space_constraint(cache, pltpu.HBM), after)


def write_stats(ref, at, rows, begin, kept=None):
    values = []
    for peak, total in zip(rows[::2], rows[1::2]):
        high = total.astype(jnp.bfloat16).astype(jnp.float32)
        values += [peak, high, total - high]
    size = stat_rows(begin + len(rows) // 2) if kept is None else kept.shape[0]
    index = lax.broadcasted_iota(jnp.int32, (size, 128), 0)
    table = jnp.zeros((size, 128), jnp.float32) if kept is None else kept.astype(jnp.float32)
    for i, value in enumerate(values):
        table = jnp.where(index == 3 * begin + i, value, table)
    ref[at : at + size, :] = table.astype(jnp.bfloat16)


def attend_kernel(plan, part, side, *refs):
    refs, score_ref = refs[:-1], refs[-1]
    outs = 2 if part == 0 else 1
    refs, outs = refs[:-outs], refs[-outs:]
    earlier = ()
    if side == 1:
        refs, earlier = refs[:-1], refs[-1:]
    *query_refs, keys_ref, cache_ref, bias_ref, order_ref, one_hot_ref = refs
    span = cache_ref.shape[0]
    mine = plan.share(part)
    row_at = pl.multiple_of((mine * plan.heads) % GROUP * plan.side_rows, plan.piece)
    order = order_ref[pl.ds(row_at, plan.piece), :]
    one_hot = one_hot_ref[side, pl.ds(row_at, plan.piece), :]
    ones = jnp.ones((span, HD), jnp.bfloat16)
    groups = [(mine * plan.heads + unit * plan.unit_heads) // GROUP for unit in range(plan.units)]
    peaks = []
    for unit, group in enumerate(groups):
        stacked = jnp.concatenate([ref[group] for ref in query_refs], axis=0)
        queries = jnp.dot(order, stacked, preferred_element_type=jnp.float32)
        queries = jnp.concatenate([queries.astype(jnp.bfloat16), one_hot], axis=1)
        keys = jnp.concatenate([keys_ref[group], bias_ref[...]], axis=0)
        scores = jnp.dot(queries, keys, preferred_element_type=jnp.float32)
        score_ref[unit] = scores
        peak = [scores[:, at : at + 128] for at in range(0, span, 128)]
        while len(peak) > 1:
            peak = [jnp.maximum(*peak[i : i + 2]) for i in range(0, len(peak) - 1, 2)] + (
                peak[-1:] if len(peak) % 2 else []
            )
        peak = jnp.max(peak[0], axis=1, keepdims=True) * LOG2_SCALE
        peak = jnp.maximum(jnp.ceil(peak * (1.0 / STEP)), FLOOR / STEP)
        peaks.append(jnp.broadcast_to(peak, (plan.piece, 128)))
    same = lax.broadcasted_iota(jnp.int32, (plan.piece, 128), 0) == lax.broadcasted_iota(
        jnp.int32, (plan.piece, 128), 1
    )
    stats = []
    at = side * plan.side if part != 0 else 0
    for unit, group in enumerate(groups):
        shift = jnp.concatenate([peaks[unit] * STEP] * (span // 128), axis=1)
        weights = jnp.exp2(score_ref[unit] * LOG2_SCALE - shift)
        value_at = pl.multiple_of((KVH + group) * HD, HD)
        values = jnp.concatenate([cache_ref[:, pl.ds(value_at, HD)], ones], axis=1)
        both = jnp.dot(weights.astype(jnp.bfloat16), values, preferred_element_type=jnp.float32)
        outs[0][at : at + plan.piece, :] = both[:, :HD].astype(outs[0].dtype)
        at += plan.piece
        for wide in (peaks[unit], both[:, HD:]):
            stats.append(jnp.sum(jnp.where(same, wide, 0.0), axis=0, keepdims=True))
    if part == 0:
        kept = earlier[0][...] if earlier else None
        write_stats(outs[1], 0, stats, side * plan.units, kept)
    else:
        kept = None
        if earlier:
            outs[0][: plan.side, :] = earlier[0][: plan.side, :]
            kept = earlier[0][plan.side :, :]
        write_stats(outs[0], at, stats, side * plan.units, kept)


def attend(plan, part, side, queries, *tables):
    span = tables[1].shape[0]
    if part == 0:
        out_shape = [
            jax.ShapeDtypeStruct((plan.side, HD), jnp.float32),
            jax.ShapeDtypeStruct((plan.stats, HD), jnp.bfloat16),
        ]
    else:
        out_shape = [jax.ShapeDtypeStruct(((side + 1) * plan.side + plan.stats, HD), jnp.bfloat16)]
    return local(
        functools.partial(attend_kernel, plan, part, side),
        out_shape,
        [pltpu.VMEM] * (len(queries) + len(tables)),
        "attend",
        [pltpu.VMEM((plan.units, plan.piece, span), jnp.float32)],
        pl.CostEstimate(
            flops=4 * plan.side * span * HD,
            bytes_accessed=2 * plan.units * span * HD * 2,
            transcendentals=plan.side * span,
        ),
    )(*queries, *tables)


def columns(plan, rows):
    index = lax.broadcasted_iota(jnp.int32, (128, 128), 0)
    table = jnp.zeros((128, 128), jnp.float32)
    for i, row in enumerate(rows):
        table = jnp.where(index == i, row, table)
    turned = jnp.transpose(table)[: plan.piece]
    return [turned[:, i : i + 1] for i in range(len(rows))]


def factors(stats, pieces):
    parts = [[stat[3 * piece + i : 3 * piece + i + 1] for i in range(3)] for stat, piece in zip(stats, pieces)]
    joint = functools.reduce(jnp.maximum, [peak for peak, _, _ in parts])
    scale = [jnp.exp2((peak - joint) * STEP) for peak, _, _ in parts]
    total = functools.reduce(jnp.add, [f * (high + low) for f, (_, high, low) in zip(scale, parts)])
    return joint, scale, total


def mix(parts, scale):
    terms = [f * part.astype(jnp.float32) for part, f in zip(parts, scale)]
    return functools.reduce(jnp.add, terms)


def merge_kernel(plan, first_ref, second_ref, stat_ref, *refs):
    *parts, out_ref, wide_ref = refs
    stats = [stat_ref[...].astype(jnp.float32)]
    stats += [ref[plan.share_rows :, :].astype(jnp.float32) for ref in parts]
    rows = []
    for piece in range(2 * plan.units):
        joint, scale, total = factors(stats, [piece] * len(stats))
        rows += [joint, total]
        at, own_at = piece * plan.piece, piece % plan.units * plan.piece
        own_ref = (first_ref, second_ref)[piece // plan.units]
        values = [own_ref[own_at : own_at + plan.piece, :]]
        values += [ref[at : at + plan.piece, :] for ref in parts]
        mixed = mix(values, columns(plan, scale))
        wide_ref[at : at + plan.piece, :] = mixed
        out_ref[at : at + plan.piece, :] = mixed.astype(jnp.bfloat16)
    write_stats(out_ref, plan.share_rows, rows, 0)


def merge(plan, first, second, stats, parts):
    return local(
        functools.partial(merge_kernel, plan),
        [
            jax.ShapeDtypeStruct((plan.share_rows + plan.stats, HD), jnp.bfloat16),
            jax.ShapeDtypeStruct((plan.share_rows, HD), jnp.float32),
        ],
        [pltpu.VMEM] * (len(parts) + 3),
        "merge",
    )(first, second, stats, *parts)


def settle_kernel(plan, wide_ref, own_ref, other_ref, out_ref):
    stats = [ref[plan.share_rows :, :].astype(jnp.float32) for ref in (own_ref, other_ref)]
    high = lax.axis_index("ctx") // plan.half
    for piece in range(2 * plan.units):
        swapped = (piece + plan.units) % (2 * plan.units)
        _, scale, total = factors(stats, [piece, swapped])
        at, other_at = piece * plan.piece, swapped * plan.piece
        values = [wide_ref[at : at + plan.piece, :], other_ref[other_at : other_at + plan.piece, :]]
        done = mix(values, columns(plan, [f / total for f in scale])).astype(jnp.bfloat16)
        side, unit = piece // plan.units, piece % plan.units
        row_at = pl.multiple_of((high ^ side) * plan.side_rows, plan.side_rows)
        for head in range(plan.unit_heads):
            to = (unit * plan.unit_heads + head) * HD
            rows = done[head * plan.side_rows : (head + 1) * plan.side_rows, :]
            out_ref[pl.ds(row_at, plan.side_rows), to : to + HD] = rows


def settle(plan, wide, own, other):
    return local(
        functools.partial(settle_kernel, plan),
        jax.ShapeDtypeStruct((plan.rows, plan.heads * HD), jnp.bfloat16),
        [pltpu.VMEM] * 3,
        "settle",
    )(wide, own, other)


def project_kernel(plan, part, *refs):
    block_ref, weight_ref, *before, out_ref = refs
    depth = plan.heads * HD
    at = pl.multiple_of(plan.share(part) * depth, depth)
    total = jnp.dot(block_ref[...], weight_ref[pl.ds(at, depth), :], preferred_element_type=jnp.float32)
    for ref in before:
        total = total + ref[...]
    out_ref[...] = total.astype(out_ref.dtype)


def project(plan, part, block, weight, before, dtype):
    operands = [block, weight] + ([] if before is None else [before])
    return local(
        functools.partial(project_kernel, plan, part),
        jax.ShapeDtypeStruct((plan.rows, weight.shape[1]), dtype),
        [pltpu.VMEM] * len(operands),
        "project",
    )(*operands)


def per_device(queries, cache, out_weight, offsets, starts):
    plan = Plan(lax.axis_size("ctx"), queries.shape[0])
    half = plan.half
    out_weight = pltpu.with_memory_space_constraint(out_weight, pltpu.VMEM)

    own = queries.reshape(plan.rows_here, KVH, GROUP, HD)
    own = own.transpose(1, 2, 0, 3).reshape(KVH, GROUP * plan.rows_here, HD)
    far = swap(own, "ctx", half)
    sides = [[block] + [swap(block, "ctx", k) for k in range(1, half)] for block in (own, far)]
    order, one_hot, bias = ready(plan, cache.shape[0], offsets, starts, sides[0][-1])
    keys = pltpu.with_memory_space_constraint(turn(cache, sides[0][-1]), pltpu.VMEM)
    cache = pltpu.with_memory_space_constraint(cache, pltpu.VMEM)
    tables = (keys, cache, bias, order, one_hot)
    if own.shape[1] % 16 != 0:
        sides = [[jnp.concatenate(blocks, axis=1)] for blocks in sides]

    parts = list(reversed(range(half)))
    begun = {part: attend(plan, part, 0, sides[0], *tables) for part in parts}
    received = []
    for part in parts[:-1]:
        (piece,) = attend(plan, part, 1, sides[1], *tables, *begun[part])
        received.append(swap(piece, "ctx", part))
    first, stats = begun[0]
    second, stats = attend(plan, 0, 1, sides[1], *tables, stats)

    near, wide = merge(plan, first, second, stats, received)
    block = settle(plan, wide, near, swap(near, "ctx", plan.across))

    total = project(plan, 0, block, out_weight, None, jnp.float32)
    blocks = [swap(block, "ctx", k) for k in range(1, half)]
    for k in range(1, half):
        dtype = jnp.float32 if k < half - 1 else jnp.bfloat16
        total = project(plan, k, blocks[k - 1], out_weight, total, dtype)
    return from_behind(total, "segment", 1)


def solution(mesh):
    in_specs = (
        P(("segment", "ctx"), None),
        P(("segment", "ctx"), None),
        P("segment", "ctx"),
        P("segment"),
        P("segment"),
    )
    out_specs = P("segment", "ctx")
    return jax.shard_map(
        per_device, mesh=mesh, in_specs=in_specs, out_specs=out_specs, check_vma=False
    )
```

```python
import functools
import math

import jax
import jax.numpy as jnp
from jax import lax
from jax.experimental import pallas as pl
from jax.experimental.pallas import tpu as pltpu
from jax.sharding import PartitionSpec as P

H = 64
KVH = 8
HD = 128
GROUP = H // KVH
LOG2_SCALE = HD ** (-0.5) * math.log2(math.e)
STEP = 8.0
FLOOR = -4096.0
HIDDEN = -1e30
STATS = 16
VMEM_LIMIT = 12 * 1024 * 1024


def swap(value, axis, bits):
    devices = lax.axis_size(axis)
    return lax.ppermute(value, axis, [(i, i ^ bits) for i in range(devices)])


def from_behind(value, axis, by):
    devices = lax.axis_size(axis)
    return lax.ppermute(value, axis, [(i, (i + by) % devices) for i in range(devices)])


class Plan:
    def __init__(self, ctx, rows_here):
        self.ctx = ctx
        self.half = ctx // 2
        self.fold = self.half // 2
        self.across = self.half | self.fold
        self.rows_here = rows_here
        self.rows = ctx * rows_here
        self.group_rows = GROUP * self.rows
        self.heads = H // self.half
        self.unit_heads = min(self.heads, GROUP)
        self.units = self.heads // self.unit_heads
        self.unit_rows = self.unit_heads * self.rows
        self.blocks = self.unit_rows // 128
        self.share_rows = self.units * self.unit_rows
        self.by_device = self.unit_heads == GROUP and GROUP * rows_here % 16 == 0

    def share(self, part):
        me = lax.axis_index("ctx")
        return (me % self.half) ^ (me // self.half * self.fold) ^ part


def stat_rows(blocks):
    return -(-3 * blocks // 16) * 16


def local(kernel, out_shape, spaces, name, scratch=(), cost=None):
    return pl.pallas_call(
        kernel,
        out_shape=out_shape,
        in_specs=[pl.BlockSpec(memory_space=space) for space in spaces],
        out_specs=jax.tree.map(lambda _: pl.BlockSpec(memory_space=pltpu.VMEM), out_shape),
        scratch_shapes=list(scratch),
        compiler_params=pltpu.CompilerParams(vmem_limit_bytes=VMEM_LIMIT),
        cost_estimate=cost,
        name=name,
    )


def ready_kernel(plan, offset_ref, start_ref, after_ref, order_ref, one_hot_ref, bias_ref):
    del after_ref
    me = lax.axis_index("ctx")
    low, high = me % plan.half, me // plan.half
    row = lax.broadcasted_iota(jnp.int32, (plan.group_rows, 128), 0)
    lane = lax.broadcasted_iota(jnp.int32, (plan.group_rows, 128), 1)
    query = lax.rem(row, plan.rows)
    device = lax.div(query, plan.rows_here)
    block = device
    if not plan.by_device:
        block = 2 * (lax.rem(device, plan.half) ^ low) + (lax.div(device, plan.half) ^ high)
    origin = (block * GROUP + lax.div(row, plan.rows)) * plan.rows_here + lax.rem(query, plan.rows_here)
    for at in range(0, plan.group_rows, 128):
        order_ref[:, at : at + 128] = jnp.where(lane + at == origin, 1.0, 0.0).astype(jnp.bfloat16)
    if plan.by_device:
        query = lax.div(row, GROUP * plan.rows_here) * plan.rows_here + lax.rem(row, plan.rows_here)
    one_hot_ref[...] = jnp.where(query == lane, 1.0, 0.0).astype(jnp.bfloat16)
    span = bias_ref.shape[0]
    position = me * span + lax.broadcasted_iota(jnp.int32, (span, 128), 0)
    asked = lax.broadcasted_iota(jnp.int32, (span, 128), 1)
    shown = (position >= start_ref[0]) & (position <= offset_ref[0] + asked)
    bias_ref[...] = jnp.where(shown, 0.0, HIDDEN).astype(jnp.bfloat16)


def ready(plan, span, offsets, starts, after):
    return local(
        functools.partial(ready_kernel, plan),
        [
            jax.ShapeDtypeStruct((plan.group_rows, plan.group_rows), jnp.bfloat16),
            jax.ShapeDtypeStruct((plan.group_rows, 128), jnp.bfloat16),
            jax.ShapeDtypeStruct((span, 128), jnp.bfloat16),
        ],
        [pltpu.SMEM, pltpu.SMEM, pl.ANY],
        "ready",
        cost=pl.CostEstimate(flops=8_000_000_000, bytes_accessed=4 * span * HD, transcendentals=0),
    )(offsets, starts, after)


def write_stats(ref, at, rows):
    values = []
    for peak, total in zip(rows[::2], rows[1::2]):
        high = total.astype(jnp.bfloat16).astype(jnp.float32)
        values += [peak, high, total - high]
    size = stat_rows(len(rows) // 2)
    index = lax.broadcasted_iota(jnp.int32, (size, 128), 0)
    table = jnp.zeros((size, 128), jnp.float32)
    for i, value in enumerate(values):
        table = jnp.where(index == i, value, table)
    ref[at : at + size, :] = table.astype(jnp.bfloat16)


def attend_kernel(plan, part, *refs):
    *refs, score_ref, held_ref = refs
    if part == 0:
        *refs, value_ref, stat_ref = refs
        stat_at = 0
    else:
        *refs, value_ref = refs
        stat_ref, stat_at = value_ref, plan.share_rows
    *query_refs, cache_ref, bias_ref, order_ref, one_hot_ref = refs
    span = cache_ref.shape[0]
    me = lax.axis_index("ctx")
    mine = plan.share(part)
    row_at = pl.multiple_of((mine * plan.heads) % GROUP * plan.rows, plan.unit_rows)
    order = order_ref[pl.ds(row_at, plan.unit_rows), :]
    one_hot = one_hot_ref[pl.ds(row_at, plan.unit_rows), :]
    ones = jnp.ones((span, HD), jnp.bfloat16)
    groups = [(mine * plan.heads + unit * plan.unit_heads) // GROUP for unit in range(plan.units)]
    peaks = []
    for unit, group in enumerate(groups):
        if plan.by_device:
            for block, ref in enumerate(query_refs):
                device = me ^ (block // 2) ^ (block % 2 * plan.half)
                to = pl.multiple_of(device * GROUP * plan.rows_here, GROUP * plan.rows_here)
                held_ref[unit, pl.ds(to, GROUP * plan.rows_here), :] = ref[group]
            queries = held_ref[unit]
        else:
            stacked = jnp.concatenate([ref[group] for ref in query_refs], axis=0)
            queries = jnp.dot(order, stacked, preferred_element_type=jnp.float32).astype(jnp.bfloat16)
        queries = jnp.concatenate([queries, one_hot], axis=1)
        key_at = pl.multiple_of(group * HD, HD)
        keys = jnp.concatenate([cache_ref[:, pl.ds(key_at, HD)], bias_ref[...]], axis=1)
        scores = lax.dot_general(queries, keys, (((1,), (1,)), ((), ())), preferred_element_type=jnp.float32)
        score_ref[unit] = scores
        peak = [scores[:, at : at + 128] for at in range(0, span, 128)]
        while len(peak) > 1:
            peak = [jnp.maximum(*peak[i : i + 2]) for i in range(0, len(peak) - 1, 2)] + (
                peak[-1:] if len(peak) % 2 else []
            )
        peak = jnp.max(peak[0], axis=1, keepdims=True) * LOG2_SCALE
        peak = jnp.maximum(jnp.ceil(peak * (1.0 / STEP)), FLOOR / STEP)
        peaks.append(jnp.broadcast_to(peak, (plan.unit_rows, 128)))
    same = lax.broadcasted_iota(jnp.int32, (128, 128), 0) == lax.broadcasted_iota(jnp.int32, (128, 128), 1)
    stats = []
    for unit, group in enumerate(groups):
        shift = jnp.concatenate([peaks[unit] * STEP] * (span // 128), axis=1)
        weights = jnp.exp2(score_ref[unit] * LOG2_SCALE - shift)
        value_at = pl.multiple_of((KVH + group) * HD, HD)
        values = jnp.concatenate([cache_ref[:, pl.ds(value_at, HD)], ones], axis=1)
        both = jnp.dot(weights.astype(jnp.bfloat16), values, preferred_element_type=jnp.float32)
        at = unit * plan.unit_rows
        value_ref[at : at + plan.unit_rows, :] = both[:, :HD].astype(value_ref.dtype)
        for block in range(0, plan.unit_rows, 128):
            for wide in (peaks[unit], both[:, HD:]):
                chosen = jnp.where(same, wide[block : block + 128, :], 0.0)
                stats.append(jnp.sum(chosen, axis=0, keepdims=True))
    write_stats(stat_ref, stat_at, stats)


def attend(plan, part, queries, cache, *tables):
    span = cache.shape[0]
    size = stat_rows(plan.units * plan.blocks)
    if part == 0:
        out_shape = [
            jax.ShapeDtypeStruct((plan.share_rows, HD), jnp.float32),
            jax.ShapeDtypeStruct((size, HD), jnp.bfloat16),
        ]
    else:
        out_shape = [jax.ShapeDtypeStruct((plan.share_rows + size, HD), jnp.bfloat16)]
    return local(
        functools.partial(attend_kernel, plan, part),
        out_shape,
        [pltpu.VMEM] * (len(queries) + 1 + len(tables)),
        "attend",
        [
            pltpu.VMEM((plan.units, plan.unit_rows, span), jnp.float32),
            pltpu.VMEM((plan.units, plan.unit_rows, HD), jnp.bfloat16),
        ],
        pl.CostEstimate(
            flops=4 * plan.share_rows * span * HD,
            bytes_accessed=2 * plan.units * span * HD * 2,
            transcendentals=plan.share_rows * span,
        ),
    )(*queries, cache, *tables)


def columns(rows):
    index = lax.broadcasted_iota(jnp.int32, (128, 128), 0)
    table = jnp.zeros((128, 128), jnp.float32)
    for i, row in enumerate(rows):
        table = jnp.where(index == i, row, table)
    turned = jnp.transpose(table)
    return [turned[:, i : i + 1] for i in range(len(rows))]


def factors(stats, block):
    parts = []
    for ref, at in stats:
        base = 3 * block // 16 * 16
        tile = ref[at + base : at + min(base + 32, stat_rows(block + 1)), :].astype(jnp.float32)
        begin = 3 * block - base
        parts.append([tile[begin + i : begin + i + 1] for i in range(3)])
    joint = functools.reduce(jnp.maximum, [peak for peak, _, _ in parts])
    scale = [jnp.exp2((peak - joint) * STEP) for peak, _, _ in parts]
    total = functools.reduce(jnp.add, [f * (high + low) for f, (_, high, low) in zip(scale, parts)])
    return joint, scale, total


def mix(refs, at, scale):
    terms = [f * ref[at : at + 128, :].astype(jnp.float32) for ref, f in zip(refs, scale)]
    return functools.reduce(jnp.add, terms)


def merge_kernel(plan, wide_ref, stat_ref, *refs):
    *parts, out_ref, wide_out_ref = refs
    stats = [(stat_ref, 0)] + [(ref, plan.share_rows) for ref in parts]
    rows = []
    for block in range(plan.units * plan.blocks):
        joint, scale, total = factors(stats, block)
        rows += [joint, total]
        at = block * 128
        mixed = mix([wide_ref] + parts, at, columns(scale))
        wide_out_ref[at : at + 128, :] = mixed
        out_ref[at : at + 128, :] = mixed.astype(jnp.bfloat16)
    write_stats(out_ref, plan.share_rows, rows)


def merge(plan, wide, stats, parts):
    rows = plan.share_rows + stat_rows(plan.units * plan.blocks)
    return local(
        functools.partial(merge_kernel, plan),
        [
            jax.ShapeDtypeStruct((rows, HD), jnp.bfloat16),
            jax.ShapeDtypeStruct((plan.share_rows, HD), jnp.float32),
        ],
        [pltpu.VMEM] * (len(parts) + 2),
        "merge",
    )(wide, stats, *parts)


def settle_kernel(plan, wide_ref, own_ref, other_ref, order_ref, out_ref):
    stats = [(own_ref, plan.share_rows), (other_ref, plan.share_rows)]
    for unit in range(plan.units):
        done = []
        for block in range(unit * plan.blocks, (unit + 1) * plan.blocks):
            _, scale, total = factors(stats, block)
            mixed = mix([wide_ref, other_ref], block * 128, columns([f / total for f in scale]))
            done.append(mixed.astype(jnp.bfloat16))
        done = jnp.concatenate(done, axis=0)
        if plan.by_device:
            done = jnp.dot(order_ref[...], done, preferred_element_type=jnp.float32).astype(jnp.bfloat16)
        for head in range(plan.unit_heads):
            to = (unit * plan.unit_heads + head) * HD
            out_ref[:, to : to + HD] = done[head * plan.rows : (head + 1) * plan.rows, :]


def settle(plan, wide, own, other, order):
    return local(
        functools.partial(settle_kernel, plan),
        jax.ShapeDtypeStruct((plan.rows, plan.heads * HD), jnp.bfloat16),
        [pltpu.VMEM] * 4,
        "settle",
    )(wide, own, other, order)


def project_kernel(plan, part, *refs):
    block_ref, weight_ref, *before, out_ref = refs
    depth = plan.heads * HD
    at = pl.multiple_of(plan.share(part) * depth, depth)
    total = jnp.dot(block_ref[...], weight_ref[pl.ds(at, depth), :], preferred_element_type=jnp.float32)
    for ref in before:
        total = total + ref[...]
    out_ref[...] = total.astype(out_ref.dtype)


def project(plan, part, block, weight, before, dtype):
    operands = [block, weight] + ([] if before is None else [before])
    return local(
        functools.partial(project_kernel, plan, part),
        jax.ShapeDtypeStruct((plan.rows, weight.shape[1]), dtype),
        [pltpu.VMEM] * len(operands),
        "project",
    )(*operands)


def per_device(queries, cache, out_weight, offsets, starts):
    plan = Plan(lax.axis_size("ctx"), queries.shape[0])
    half = plan.half
    cache = pltpu.with_memory_space_constraint(cache, pltpu.VMEM)
    out_weight = pltpu.with_memory_space_constraint(out_weight, pltpu.VMEM)

    own = queries.reshape(plan.rows_here, KVH, GROUP, HD)
    own = own.transpose(1, 2, 0, 3).reshape(KVH, GROUP * plan.rows_here, HD)
    far = swap(own, "ctx", half)
    near = [swap(own, "ctx", k) for k in range(1, half)]
    order, one_hot, bias = ready(plan, cache.shape[0], offsets, starts, near[-1])
    if plan.by_device:
        gathered = [own, far]
        for k in range(1, half):
            gathered += [near[k - 1], swap(far, "ctx", k)]
    else:
        pair = jnp.concatenate([own, far], axis=1)
        gathered = [pair] + [swap(pair, "ctx", k) for k in range(1, half)]

    received = []
    for part in reversed(range(1, half)):
        (piece,) = attend(plan, part, gathered, cache, bias, order, one_hot)
        received.append(swap(piece, "ctx", part))
    wide, stats = attend(plan, 0, gathered, cache, bias, order, one_hot)

    near, near_wide = merge(plan, wide, stats, received)
    block = settle(plan, near_wide, near, swap(near, "ctx", plan.across), order)

    total = project(plan, 0, block, out_weight, None, jnp.float32)
    blocks = [swap(block, "ctx", k) for k in range(1, half)]
    for k in range(1, half):
        dtype = jnp.float32 if k < half - 1 else jnp.bfloat16
        total = project(plan, k, blocks[k - 1], out_weight, total, dtype)
    return from_behind(total, "segment", 1)


def solution(mesh):
    in_specs = (
        P(("segment", "ctx"), None),
        P(("segment", "ctx"), None),
        P("segment", "ctx"),
        P("segment"),
        P("segment"),
    )
    out_specs = P("segment", "ctx")
    return jax.shard_map(
        per_device, mesh=mesh, in_specs=in_specs, out_specs=out_specs, check_vma=False
    )
```

```python
import functools
import math

import jax
import jax.numpy as jnp
from jax import lax
from jax.experimental import pallas as pl
from jax.experimental.pallas import tpu as pltpu
from jax.sharding import PartitionSpec as P

H = 64
KVH = 8
HD = 128
GROUP = H // KVH
LOG2_SCALE = HD ** (-0.5) * math.log2(math.e)
STEP = 8.0
FLOOR = -4096.0
HIDDEN = -1e30
STATS = 16
VMEM_LIMIT = 12 * 1024 * 1024


def swap(value, axis, bits):
    devices = lax.axis_size(axis)
    return lax.ppermute(value, axis, [(i, i ^ bits) for i in range(devices)])


def from_behind(value, axis, by):
    devices = lax.axis_size(axis)
    return lax.ppermute(value, axis, [(i, (i + by) % devices) for i in range(devices)])


class Plan:
    def __init__(self, ctx, rows_here):
        self.ctx = ctx
        self.half = ctx // 2
        self.fold = self.half // 2
        self.across = self.half | self.fold
        self.rows_here = rows_here
        self.rows = ctx * rows_here
        self.group_rows = GROUP * self.rows
        self.heads = H // self.half
        self.unit_heads = min(self.heads, GROUP)
        self.units = self.heads // self.unit_heads
        self.unit_rows = self.unit_heads * self.rows
        self.blocks = self.unit_rows // 128
        self.share_rows = self.units * self.unit_rows
        self.by_device = self.unit_heads == GROUP and GROUP * rows_here % 16 == 0

    def share(self, part):
        me = lax.axis_index("ctx")
        return (me % self.half) ^ (me // self.half * self.fold) ^ part


def stat_rows(blocks):
    return -(-3 * blocks // 16) * 16


def local(kernel, out_shape, spaces, name, scratch=(), cost=None):
    return pl.pallas_call(
        kernel,
        out_shape=out_shape,
        in_specs=[pl.BlockSpec(memory_space=space) for space in spaces],
        out_specs=jax.tree.map(lambda _: pl.BlockSpec(memory_space=pltpu.VMEM), out_shape),
        scratch_shapes=list(scratch),
        compiler_params=pltpu.CompilerParams(vmem_limit_bytes=VMEM_LIMIT),
        cost_estimate=cost,
        name=name,
    )


def order_kernel(plan, order_ref, one_hot_ref):
    low = lax.axis_index("ctx") % plan.half
    high = lax.axis_index("ctx") // plan.half
    row = lax.broadcasted_iota(jnp.int32, (plan.group_rows, 128), 0)
    lane = lax.broadcasted_iota(jnp.int32, (plan.group_rows, 128), 1)
    query = lax.rem(row, plan.rows)
    device = lax.div(query, plan.rows_here)
    block = device
    if not plan.by_device:
        block = 2 * (lax.rem(device, plan.half) ^ low) + (lax.div(device, plan.half) ^ high)
    origin = (block * GROUP + lax.div(row, plan.rows)) * plan.rows_here + lax.rem(query, plan.rows_here)
    for at in range(0, plan.group_rows, 128):
        order_ref[:, at : at + 128] = jnp.where(lane + at == origin, 1.0, 0.0).astype(jnp.bfloat16)
    if plan.by_device:
        query = lax.div(row, GROUP * plan.rows_here) * plan.rows_here + lax.rem(row, plan.rows_here)
    one_hot_ref[...] = jnp.where(query == lane, 1.0, 0.0).astype(jnp.bfloat16)


def row_order(plan):
    return local(
        functools.partial(order_kernel, plan),
        [
            jax.ShapeDtypeStruct((plan.group_rows, plan.group_rows), jnp.bfloat16),
            jax.ShapeDtypeStruct((plan.group_rows, 128), jnp.bfloat16),
        ],
        [],
        "order",
        cost=pl.CostEstimate(flops=8_000_000_000, bytes_accessed=0, transcendentals=0),
    )()


def mask_kernel(offset_ref, start_ref, after_ref, bias_ref):
    del after_ref
    span = bias_ref.shape[0]
    position = lax.axis_index("ctx") * span + lax.broadcasted_iota(jnp.int32, (span, 128), 0)
    asked = lax.broadcasted_iota(jnp.int32, (span, 128), 1)
    shown = (position >= start_ref[0]) & (position <= offset_ref[0] + asked)
    bias_ref[...] = jnp.where(shown, 0.0, HIDDEN).astype(jnp.bfloat16)


def mask(span, offsets, starts, after):
    return local(
        mask_kernel,
        jax.ShapeDtypeStruct((span, 128), jnp.bfloat16),
        [pltpu.SMEM, pltpu.SMEM, pl.ANY],
        "mask",
        cost=pl.CostEstimate(flops=1_000_000, bytes_accessed=256 * span, transcendentals=0),
    )(offsets, starts, after)


def write_stats(ref, at, rows):
    values = []
    for peak, total in zip(rows[::2], rows[1::2]):
        high = total.astype(jnp.bfloat16).astype(jnp.float32)
        values += [peak, high, total - high]
    size = stat_rows(len(rows) // 2)
    index = lax.broadcasted_iota(jnp.int32, (size, 128), 0)
    table = jnp.zeros((size, 128), jnp.float32)
    for i, value in enumerate(values):
        table = jnp.where(index == i, value, table)
    ref[at : at + size, :] = table.astype(jnp.bfloat16)


def attend_kernel(plan, part, *refs):
    *refs, score_ref, held_ref = refs
    if part == 0:
        *refs, value_ref, stat_ref = refs
        stat_at = 0
    else:
        *refs, value_ref = refs
        stat_ref, stat_at = value_ref, plan.share_rows
    *query_refs, cache_ref, bias_ref, order_ref, one_hot_ref = refs
    span = cache_ref.shape[0]
    me = lax.axis_index("ctx")
    mine = plan.share(part)
    row_at = pl.multiple_of((mine * plan.heads) % GROUP * plan.rows, plan.unit_rows)
    order = order_ref[pl.ds(row_at, plan.unit_rows), :]
    one_hot = one_hot_ref[pl.ds(row_at, plan.unit_rows), :]
    ones = jnp.ones((span, HD), jnp.bfloat16)
    groups = [(mine * plan.heads + unit * plan.unit_heads) // GROUP for unit in range(plan.units)]
    peaks = []
    for unit, group in enumerate(groups):
        if plan.by_device:
            for block, ref in enumerate(query_refs):
                device = me ^ (block // 2) ^ (block % 2 * plan.half)
                to = pl.multiple_of(device * GROUP * plan.rows_here, GROUP * plan.rows_here)
                held_ref[unit, pl.ds(to, GROUP * plan.rows_here), :] = ref[group]
            queries = held_ref[unit]
        else:
            stacked = jnp.concatenate([ref[group] for ref in query_refs], axis=0)
            queries = jnp.dot(order, stacked, preferred_element_type=jnp.float32).astype(jnp.bfloat16)
        queries = jnp.concatenate([queries, one_hot], axis=1)
        key_at = pl.multiple_of(group * HD, HD)
        keys = jnp.concatenate([cache_ref[:, pl.ds(key_at, HD)], bias_ref[...]], axis=1)
        scores = lax.dot_general(queries, keys, (((1,), (1,)), ((), ())), preferred_element_type=jnp.float32)
        score_ref[unit] = scores
        peak = [scores[:, at : at + 128] for at in range(0, span, 128)]
        while len(peak) > 1:
            peak = [jnp.maximum(*peak[i : i + 2]) for i in range(0, len(peak) - 1, 2)] + (
                peak[-1:] if len(peak) % 2 else []
            )
        peak = jnp.max(peak[0], axis=1, keepdims=True) * LOG2_SCALE
        peak = jnp.maximum(jnp.ceil(peak * (1.0 / STEP)), FLOOR / STEP)
        peaks.append(jnp.broadcast_to(peak, (plan.unit_rows, 128)))
    same = lax.broadcasted_iota(jnp.int32, (128, 128), 0) == lax.broadcasted_iota(jnp.int32, (128, 128), 1)
    stats = []
    for unit, group in enumerate(groups):
        shift = jnp.concatenate([peaks[unit] * STEP] * (span // 128), axis=1)
        weights = jnp.exp2(score_ref[unit] * LOG2_SCALE - shift)
        value_at = pl.multiple_of((KVH + group) * HD, HD)
        values = jnp.concatenate([cache_ref[:, pl.ds(value_at, HD)], ones], axis=1)
        both = jnp.dot(weights.astype(jnp.bfloat16), values, preferred_element_type=jnp.float32)
        at = unit * plan.unit_rows
        value_ref[at : at + plan.unit_rows, :] = both[:, :HD].astype(value_ref.dtype)
        for block in range(0, plan.unit_rows, 128):
            for wide in (peaks[unit], both[:, HD:]):
                chosen = jnp.where(same, wide[block : block + 128, :], 0.0)
                stats.append(jnp.sum(chosen, axis=0, keepdims=True))
    write_stats(stat_ref, stat_at, stats)


def attend(plan, part, queries, cache, *tables):
    span = cache.shape[0]
    size = stat_rows(plan.units * plan.blocks)
    if part == 0:
        out_shape = [
            jax.ShapeDtypeStruct((plan.share_rows, HD), jnp.float32),
            jax.ShapeDtypeStruct((size, HD), jnp.bfloat16),
        ]
    else:
        out_shape = [jax.ShapeDtypeStruct((plan.share_rows + size, HD), jnp.bfloat16)]
    return local(
        functools.partial(attend_kernel, plan, part),
        out_shape,
        [pltpu.VMEM] * (len(queries) + 1 + len(tables)),
        "attend",
        [
            pltpu.VMEM((plan.units, plan.unit_rows, span), jnp.float32),
            pltpu.VMEM((plan.units, plan.unit_rows, HD), jnp.bfloat16),
        ],
        pl.CostEstimate(
            flops=4 * plan.share_rows * span * HD,
            bytes_accessed=2 * plan.units * span * HD * 2,
            transcendentals=plan.share_rows * span,
        ),
    )(*queries, cache, *tables)


def columns(rows):
    index = lax.broadcasted_iota(jnp.int32, (128, 128), 0)
    table = jnp.zeros((128, 128), jnp.float32)
    for i, row in enumerate(rows):
        table = jnp.where(index == i, row, table)
    turned = jnp.transpose(table)
    return [turned[:, i : i + 1] for i in range(len(rows))]


def factors(stats, block):
    parts = []
    for ref, at in stats:
        base = 3 * block // 16 * 16
        tile = ref[at + base : at + min(base + 32, stat_rows(block + 1)), :].astype(jnp.float32)
        begin = 3 * block - base
        parts.append([tile[begin + i : begin + i + 1] for i in range(3)])
    joint = functools.reduce(jnp.maximum, [peak for peak, _, _ in parts])
    scale = [jnp.exp2((peak - joint) * STEP) for peak, _, _ in parts]
    total = functools.reduce(jnp.add, [f * (high + low) for f, (_, high, low) in zip(scale, parts)])
    return joint, scale, total


def mix(refs, at, scale):
    terms = [f * ref[at : at + 128, :].astype(jnp.float32) for ref, f in zip(refs, scale)]
    return functools.reduce(jnp.add, terms)


def merge_kernel(plan, wide_ref, stat_ref, *refs):
    *parts, out_ref, wide_out_ref = refs
    stats = [(stat_ref, 0)] + [(ref, plan.share_rows) for ref in parts]
    rows = []
    for block in range(plan.units * plan.blocks):
        joint, scale, total = factors(stats, block)
        rows += [joint, total]
        at = block * 128
        mixed = mix([wide_ref] + parts, at, columns(scale))
        wide_out_ref[at : at + 128, :] = mixed
        out_ref[at : at + 128, :] = mixed.astype(jnp.bfloat16)
    write_stats(out_ref, plan.share_rows, rows)


def merge(plan, wide, stats, parts):
    rows = plan.share_rows + stat_rows(plan.units * plan.blocks)
    return local(
        functools.partial(merge_kernel, plan),
        [
            jax.ShapeDtypeStruct((rows, HD), jnp.bfloat16),
            jax.ShapeDtypeStruct((plan.share_rows, HD), jnp.float32),
        ],
        [pltpu.VMEM] * (len(parts) + 2),
        "merge",
    )(wide, stats, *parts)


def settle_kernel(plan, wide_ref, own_ref, other_ref, order_ref, out_ref):
    stats = [(own_ref, plan.share_rows), (other_ref, plan.share_rows)]
    for unit in range(plan.units):
        done = []
        for block in range(unit * plan.blocks, (unit + 1) * plan.blocks):
            _, scale, total = factors(stats, block)
            mixed = mix([wide_ref, other_ref], block * 128, columns([f / total for f in scale]))
            done.append(mixed.astype(jnp.bfloat16))
        done = jnp.concatenate(done, axis=0)
        if plan.by_device:
            done = jnp.dot(order_ref[...], done, preferred_element_type=jnp.float32).astype(jnp.bfloat16)
        for head in range(plan.unit_heads):
            to = (unit * plan.unit_heads + head) * HD
            out_ref[:, to : to + HD] = done[head * plan.rows : (head + 1) * plan.rows, :]


def settle(plan, wide, own, other, order):
    return local(
        functools.partial(settle_kernel, plan),
        jax.ShapeDtypeStruct((plan.rows, plan.heads * HD), jnp.bfloat16),
        [pltpu.VMEM] * 4,
        "settle",
    )(wide, own, other, order)


def project_kernel(plan, part, *refs):
    block_ref, weight_ref, *before, out_ref = refs
    depth = plan.heads * HD
    at = pl.multiple_of(plan.share(part) * depth, depth)
    total = jnp.dot(block_ref[...], weight_ref[pl.ds(at, depth), :], preferred_element_type=jnp.float32)
    for ref in before:
        total = total + ref[...]
    out_ref[...] = total.astype(out_ref.dtype)


def project(plan, part, block, weight, before, dtype):
    operands = [block, weight] + ([] if before is None else [before])
    return local(
        functools.partial(project_kernel, plan, part),
        jax.ShapeDtypeStruct((plan.rows, weight.shape[1]), dtype),
        [pltpu.VMEM] * len(operands),
        "project",
    )(*operands)


def per_device(queries, cache, out_weight, offsets, starts):
    plan = Plan(lax.axis_size("ctx"), queries.shape[0])
    half = plan.half
    cache = pltpu.with_memory_space_constraint(cache, pltpu.VMEM)
    out_weight = pltpu.with_memory_space_constraint(out_weight, pltpu.VMEM)

    own = queries.reshape(plan.rows_here, KVH, GROUP, HD)
    own = own.transpose(1, 2, 0, 3).reshape(KVH, GROUP * plan.rows_here, HD)
    far = swap(own, "ctx", half)
    near = [swap(own, "ctx", k) for k in range(1, half)]
    order, one_hot = row_order(plan)
    bias = mask(cache.shape[0], offsets, starts, near[-1])
    if plan.by_device:
        gathered = [own, far]
        for k in range(1, half):
            gathered += [near[k - 1], swap(far, "ctx", k)]
    else:
        pair = jnp.concatenate([own, far], axis=1)
        gathered = [pair] + [swap(pair, "ctx", k) for k in range(1, half)]

    received = []
    for part in reversed(range(1, half)):
        (piece,) = attend(plan, part, gathered, cache, bias, order, one_hot)
        received.append(swap(piece, "ctx", part))
    wide, stats = attend(plan, 0, gathered, cache, bias, order, one_hot)

    near, near_wide = merge(plan, wide, stats, received)
    block = settle(plan, near_wide, near, swap(near, "ctx", plan.across), order)

    total = project(plan, 0, block, out_weight, None, jnp.float32)
    blocks = [swap(block, "ctx", k) for k in range(1, half)]
    for k in range(1, half):
        dtype = jnp.float32 if k < half - 1 else jnp.bfloat16
        total = project(plan, k, blocks[k - 1], out_weight, total, dtype)
    return from_behind(total, "segment", 1)


def solution(mesh):
    in_specs = (
        P(("segment", "ctx"), None),
        P(("segment", "ctx"), None),
        P("segment", "ctx"),
        P("segment"),
        P("segment"),
    )
    out_specs = P("segment", "ctx")
    return jax.shard_map(
        per_device, mesh=mesh, in_specs=in_specs, out_specs=out_specs, check_vma=False
    )
```

```python
import functools
import math

import jax
import jax.numpy as jnp
from jax import lax
from jax.experimental import pallas as pl
from jax.experimental.pallas import tpu as pltpu
from jax.sharding import PartitionSpec as P

H = 64
KVH = 8
HD = 128
GROUP = H // KVH
LOG2_SCALE = HD ** (-0.5) * math.log2(math.e)
STEP = 8.0
FLOOR = -4096.0
HIDDEN = -1e30
STATS = 16
VMEM_LIMIT = 12 * 1024 * 1024


def swap(value, axis, bits):
    devices = lax.axis_size(axis)
    return lax.ppermute(value, axis, [(i, i ^ bits) for i in range(devices)])


def from_behind(value, axis, by):
    devices = lax.axis_size(axis)
    return lax.ppermute(value, axis, [(i, (i + by) % devices) for i in range(devices)])


class Plan:
    def __init__(self, ctx, rows_here):
        self.ctx = ctx
        self.half = ctx // 2
        self.fold = self.half // 2
        self.across = self.half | self.fold
        self.rows_here = rows_here
        self.rows = ctx * rows_here
        self.group_rows = GROUP * self.rows
        self.heads = H // self.half
        self.unit_heads = min(self.heads, GROUP)
        self.units = self.heads // self.unit_heads
        self.unit_rows = self.unit_heads * self.rows
        self.blocks = self.unit_rows // 128
        self.share_rows = self.units * self.unit_rows
        self.by_device = self.unit_heads == GROUP and GROUP * rows_here % 16 == 0

    def share(self, part):
        me = lax.axis_index("ctx")
        return (me % self.half) ^ (me // self.half * self.fold) ^ part


def stat_rows(blocks):
    return -(-3 * blocks // 16) * 16


def local(kernel, out_shape, spaces, name, scratch=(), cost=None):
    return pl.pallas_call(
        kernel,
        out_shape=out_shape,
        in_specs=[pl.BlockSpec(memory_space=space) for space in spaces],
        out_specs=jax.tree.map(lambda _: pl.BlockSpec(memory_space=pltpu.VMEM), out_shape),
        scratch_shapes=list(scratch),
        compiler_params=pltpu.CompilerParams(vmem_limit_bytes=VMEM_LIMIT),
        cost_estimate=cost,
        name=name,
    )


def order_kernel(plan, order_ref, one_hot_ref):
    low = lax.axis_index("ctx") % plan.half
    high = lax.axis_index("ctx") // plan.half
    row = lax.broadcasted_iota(jnp.int32, (plan.group_rows, 128), 0)
    lane = lax.broadcasted_iota(jnp.int32, (plan.group_rows, 128), 1)
    query = lax.rem(row, plan.rows)
    device = lax.div(query, plan.rows_here)
    block = device
    if not plan.by_device:
        block = 2 * (lax.rem(device, plan.half) ^ low) + (lax.div(device, plan.half) ^ high)
    origin = (block * GROUP + lax.div(row, plan.rows)) * plan.rows_here + lax.rem(query, plan.rows_here)
    for at in range(0, plan.group_rows, 128):
        order_ref[:, at : at + 128] = jnp.where(lane + at == origin, 1.0, 0.0).astype(jnp.bfloat16)
    if plan.by_device:
        query = lax.div(row, GROUP * plan.rows_here) * plan.rows_here + lax.rem(row, plan.rows_here)
    one_hot_ref[...] = jnp.where(query == lane, 1.0, 0.0).astype(jnp.bfloat16)


def row_order(plan):
    return local(
        functools.partial(order_kernel, plan),
        [
            jax.ShapeDtypeStruct((plan.group_rows, plan.group_rows), jnp.bfloat16),
            jax.ShapeDtypeStruct((plan.group_rows, 128), jnp.bfloat16),
        ],
        [],
        "order",
        cost=pl.CostEstimate(flops=8_000_000_000, bytes_accessed=0, transcendentals=0),
    )()


def mask_kernel(offset_ref, start_ref, after_ref, bias_ref):
    del after_ref
    span = bias_ref.shape[0]
    position = lax.axis_index("ctx") * span + lax.broadcasted_iota(jnp.int32, (span, 128), 0)
    asked = lax.broadcasted_iota(jnp.int32, (span, 128), 1)
    shown = (position >= start_ref[0]) & (position <= offset_ref[0] + asked)
    bias_ref[...] = jnp.where(shown, 0.0, HIDDEN).astype(jnp.bfloat16)


def mask(span, offsets, starts, after):
    return local(
        mask_kernel,
        jax.ShapeDtypeStruct((span, 128), jnp.bfloat16),
        [pltpu.SMEM, pltpu.SMEM, pl.ANY],
        "mask",
        cost=pl.CostEstimate(flops=1_000_000, bytes_accessed=256 * span, transcendentals=0),
    )(offsets, starts, after)


def write_stats(ref, at, rows):
    values = []
    for peak, total in zip(rows[::2], rows[1::2]):
        high = total.astype(jnp.bfloat16).astype(jnp.float32)
        values += [peak, high, total - high]
    size = stat_rows(len(rows) // 2)
    index = lax.broadcasted_iota(jnp.int32, (size, 128), 0)
    table = jnp.zeros((size, 128), jnp.float32)
    for i, value in enumerate(values):
        table = jnp.where(index == i, value, table)
    ref[at : at + size, :] = table.astype(jnp.bfloat16)


def attend_kernel(plan, part, *refs):
    *refs, score_ref, held_ref = refs
    if part == 0:
        *refs, value_ref, stat_ref = refs
        stat_at = 0
    else:
        *refs, value_ref = refs
        stat_ref, stat_at = value_ref, plan.share_rows
    *query_refs, cache_ref, bias_ref, order_ref, one_hot_ref = refs
    span = cache_ref.shape[0]
    me = lax.axis_index("ctx")
    mine = plan.share(part)
    row_at = pl.multiple_of((mine * plan.heads) % GROUP * plan.rows, plan.unit_rows)
    order = order_ref[pl.ds(row_at, plan.unit_rows), :]
    one_hot = one_hot_ref[pl.ds(row_at, plan.unit_rows), :]
    ones = jnp.ones((span, HD), jnp.bfloat16)
    groups = [(mine * plan.heads + unit * plan.unit_heads) // GROUP for unit in range(plan.units)]
    peaks = []
    for unit, group in enumerate(groups):
        if plan.by_device:
            for block, ref in enumerate(query_refs):
                device = me ^ (block // 2) ^ (block % 2 * plan.half)
                to = pl.multiple_of(device * GROUP * plan.rows_here, GROUP * plan.rows_here)
                held_ref[unit, pl.ds(to, GROUP * plan.rows_here), :] = ref[group]
            queries = held_ref[unit]
        else:
            stacked = jnp.concatenate([ref[group] for ref in query_refs], axis=0)
            queries = jnp.dot(order, stacked, preferred_element_type=jnp.float32).astype(jnp.bfloat16)
        queries = jnp.concatenate([queries, one_hot], axis=1)
        key_at = pl.multiple_of(group * HD, HD)
        keys = jnp.concatenate([cache_ref[:, pl.ds(key_at, HD)], bias_ref[...]], axis=1)
        scores = lax.dot_general(queries, keys, (((1,), (1,)), ((), ())), preferred_element_type=jnp.float32)
        score_ref[unit] = scores
        peak = [scores[:, at : at + 128] for at in range(0, span, 128)]
        while len(peak) > 1:
            peak = [jnp.maximum(*peak[i : i + 2]) for i in range(0, len(peak) - 1, 2)] + (
                peak[-1:] if len(peak) % 2 else []
            )
        peak = jnp.max(peak[0], axis=1, keepdims=True) * LOG2_SCALE
        peak = jnp.maximum(jnp.ceil(peak * (1.0 / STEP)), FLOOR / STEP)
        peaks.append(jnp.broadcast_to(peak, (plan.unit_rows, 128)))
    same = lax.broadcasted_iota(jnp.int32, (128, 128), 0) == lax.broadcasted_iota(jnp.int32, (128, 128), 1)
    stats = []
    for unit, group in enumerate(groups):
        shift = jnp.concatenate([peaks[unit] * STEP] * (span // 128), axis=1)
        weights = jnp.exp2(score_ref[unit] * LOG2_SCALE - shift)
        value_at = pl.multiple_of((KVH + group) * HD, HD)
        values = jnp.concatenate([cache_ref[:, pl.ds(value_at, HD)], ones], axis=1)
        both = jnp.dot(weights.astype(jnp.bfloat16), values, preferred_element_type=jnp.float32)
        at = unit * plan.unit_rows
        value_ref[at : at + plan.unit_rows, :] = both[:, :HD].astype(value_ref.dtype)
        for block in range(0, plan.unit_rows, 128):
            for wide in (peaks[unit], both[:, HD:]):
                chosen = jnp.where(same, wide[block : block + 128, :], 0.0)
                stats.append(jnp.sum(chosen, axis=0, keepdims=True))
    write_stats(stat_ref, stat_at, stats)


def attend(plan, part, queries, cache, *tables):
    span = cache.shape[0]
    size = stat_rows(plan.units * plan.blocks)
    if part == 0:
        out_shape = [
            jax.ShapeDtypeStruct((plan.share_rows, HD), jnp.float32),
            jax.ShapeDtypeStruct((size, HD), jnp.bfloat16),
        ]
    else:
        out_shape = [jax.ShapeDtypeStruct((plan.share_rows + size, HD), jnp.bfloat16)]
    return local(
        functools.partial(attend_kernel, plan, part),
        out_shape,
        [pltpu.VMEM] * (len(queries) + 1 + len(tables)),
        "attend",
        [
            pltpu.VMEM((plan.units, plan.unit_rows, span), jnp.float32),
            pltpu.VMEM((plan.units, plan.unit_rows, HD), jnp.bfloat16),
        ],
        pl.CostEstimate(
            flops=4 * plan.share_rows * span * HD,
            bytes_accessed=2 * plan.units * span * HD * 2,
            transcendentals=plan.share_rows * span,
        ),
    )(*queries, cache, *tables)


def columns(rows):
    size = -(-len(rows) // 8) * 8
    index = lax.broadcasted_iota(jnp.int32, (size, 128), 0)
    table = jnp.zeros((size, 128), jnp.float32)
    for i, row in enumerate(rows):
        table = jnp.where(index == i, row, table)
    turned = jnp.transpose(jnp.concatenate([table, jnp.zeros((128 - size, 128), jnp.float32)], axis=0))
    return [turned[:, i : i + 1] for i in range(len(rows))]


def factors(stats, block):
    parts = []
    for ref, at in stats:
        base = 3 * block // 16 * 16
        tile = ref[at + base : at + min(base + 32, stat_rows(block + 1)), :].astype(jnp.float32)
        begin = 3 * block - base
        parts.append([tile[begin + i : begin + i + 1] for i in range(3)])
    joint = functools.reduce(jnp.maximum, [peak for peak, _, _ in parts])
    scale = [jnp.exp2((peak - joint) * STEP) for peak, _, _ in parts]
    total = functools.reduce(jnp.add, [f * (high + low) for f, (_, high, low) in zip(scale, parts)])
    return joint, scale, total


def mix(refs, at, scale):
    terms = [f * ref[at : at + 128, :].astype(jnp.float32) for ref, f in zip(refs, scale)]
    return functools.reduce(jnp.add, terms)


def merge_kernel(plan, wide_ref, stat_ref, *refs):
    *parts, out_ref, wide_out_ref = refs
    stats = [(stat_ref, 0)] + [(ref, plan.share_rows) for ref in parts]
    rows, scales = [], []
    for block in range(plan.units * plan.blocks):
        joint, scale, total = factors(stats, block)
        rows += [joint, total]
        scales += scale
    scales = columns(scales)
    for block in range(plan.units * plan.blocks):
        at = block * 128
        mixed = mix([wide_ref] + parts, at, scales[block * len(stats) : (block + 1) * len(stats)])
        wide_out_ref[at : at + 128, :] = mixed
        out_ref[at : at + 128, :] = mixed.astype(jnp.bfloat16)
    write_stats(out_ref, plan.share_rows, rows)


def merge(plan, wide, stats, parts):
    rows = plan.share_rows + stat_rows(plan.units * plan.blocks)
    return local(
        functools.partial(merge_kernel, plan),
        [
            jax.ShapeDtypeStruct((rows, HD), jnp.bfloat16),
            jax.ShapeDtypeStruct((plan.share_rows, HD), jnp.float32),
        ],
        [pltpu.VMEM] * (len(parts) + 2),
        "merge",
    )(wide, stats, *parts)


def settle_kernel(plan, wide_ref, own_ref, other_ref, order_ref, out_ref):
    stats = [(own_ref, plan.share_rows), (other_ref, plan.share_rows)]
    scales = []
    for block in range(plan.units * plan.blocks):
        _, scale, total = factors(stats, block)
        scales += [f / total for f in scale]
    scales = columns(scales)
    for unit in range(plan.units):
        done = []
        for block in range(unit * plan.blocks, (unit + 1) * plan.blocks):
            mixed = mix([wide_ref, other_ref], block * 128, scales[2 * block : 2 * block + 2])
            done.append(mixed.astype(jnp.bfloat16))
        done = jnp.concatenate(done, axis=0)
        if plan.by_device:
            done = jnp.dot(order_ref[...], done, preferred_element_type=jnp.float32).astype(jnp.bfloat16)
        for head in range(plan.unit_heads):
            to = (unit * plan.unit_heads + head) * HD
            out_ref[:, to : to + HD] = done[head * plan.rows : (head + 1) * plan.rows, :]


def settle(plan, wide, own, other, order):
    return local(
        functools.partial(settle_kernel, plan),
        jax.ShapeDtypeStruct((plan.rows, plan.heads * HD), jnp.bfloat16),
        [pltpu.VMEM] * 4,
        "settle",
    )(wide, own, other, order)


def project_kernel(plan, part, *refs):
    block_ref, weight_ref, *before, out_ref = refs
    depth = plan.heads * HD
    at = pl.multiple_of(plan.share(part) * depth, depth)
    total = jnp.dot(block_ref[...], weight_ref[pl.ds(at, depth), :], preferred_element_type=jnp.float32)
    for ref in before:
        total = total + ref[...]
    out_ref[...] = total.astype(out_ref.dtype)


def project(plan, part, block, weight, before, dtype):
    operands = [block, weight] + ([] if before is None else [before])
    return local(
        functools.partial(project_kernel, plan, part),
        jax.ShapeDtypeStruct((plan.rows, weight.shape[1]), dtype),
        [pltpu.VMEM] * len(operands),
        "project",
    )(*operands)


def deliver_kernel(value_ref, out_ref, sem):
    copy = pltpu.make_async_copy(value_ref, out_ref, sem)
    copy.start()
    copy.wait()


def deliver(value):
    return pl.pallas_call(
        deliver_kernel,
        out_shape=pltpu.HBM(value.shape, value.dtype),
        in_specs=[pl.BlockSpec(memory_space=pltpu.VMEM)],
        out_specs=pl.BlockSpec(memory_space=pltpu.HBM),
        scratch_shapes=[pltpu.SemaphoreType.DMA],
        name="deliver",
    )(value)


def per_device(queries, cache, out_weight, offsets, starts):
    plan = Plan(lax.axis_size("ctx"), queries.shape[0])
    half = plan.half
    cache = pltpu.with_memory_space_constraint(cache, pltpu.VMEM)
    out_weight = pltpu.with_memory_space_constraint(out_weight, pltpu.VMEM)

    own = queries.reshape(plan.rows_here, KVH, GROUP, HD)
    own = own.transpose(1, 2, 0, 3).reshape(KVH, GROUP * plan.rows_here, HD)
    far = swap(own, "ctx", half)
    near = [swap(own, "ctx", k) for k in range(1, half)]
    order, one_hot = row_order(plan)
    bias = mask(cache.shape[0], offsets, starts, near[-1])
    if plan.by_device:
        gathered = [own, far]
        for k in range(1, half):
            gathered += [near[k - 1], swap(far, "ctx", k)]
    else:
        pair = jnp.concatenate([own, far], axis=1)
        gathered = [pair] + [swap(pair, "ctx", k) for k in range(1, half)]

    received = []
    for part in reversed(range(1, half)):
        (piece,) = attend(plan, part, gathered, cache, bias, order, one_hot)
        received.append(swap(piece, "ctx", part))
    wide, stats = attend(plan, 0, gathered, cache, bias, order, one_hot)

    near, near_wide = merge(plan, wide, stats, received)
    block = settle(plan, near_wide, near, swap(near, "ctx", plan.across), order)

    total = project(plan, 0, block, out_weight, None, jnp.float32)
    blocks = [swap(block, "ctx", k) for k in range(1, half)]
    for k in range(1, half):
        dtype = jnp.float32 if k < half - 1 else jnp.bfloat16
        total = project(plan, k, blocks[k - 1], out_weight, total, dtype)
    return deliver(from_behind(total, "segment", 1))


def solution(mesh):
    in_specs = (
        P(("segment", "ctx"), None),
        P(("segment", "ctx"), None),
        P("segment", "ctx"),
        P("segment"),
        P("segment"),
    )
    out_specs = P("segment", "ctx")
    return jax.shard_map(
        per_device, mesh=mesh, in_specs=in_specs, out_specs=out_specs, check_vma=False
    )
```

```python
import functools
import math

import jax
import jax.numpy as jnp
from jax import lax
from jax.experimental import pallas as pl
from jax.experimental.pallas import tpu as pltpu
from jax.sharding import PartitionSpec as P

H = 64
KVH = 8
HD = 128
GROUP = H // KVH
LOG2_SCALE = HD ** (-0.5) * math.log2(math.e)
STEP = 8.0
FLOOR = -4096.0
HIDDEN = -1e30
STATS = 16
VMEM_LIMIT = 12 * 1024 * 1024


def swap(value, axis, bits):
    devices = lax.axis_size(axis)
    return lax.ppermute(value, axis, [(i, i ^ bits) for i in range(devices)])


def from_behind(value, axis, by):
    devices = lax.axis_size(axis)
    return lax.ppermute(value, axis, [(i, (i + by) % devices) for i in range(devices)])


class Plan:
    def __init__(self, ctx, rows_here):
        self.ctx = ctx
        self.half = ctx // 2
        self.fold = self.half // 2
        self.across = self.half | self.fold
        self.rows_here = rows_here
        self.rows = ctx * rows_here
        self.group_rows = GROUP * self.rows
        self.heads = H // self.half
        self.unit_heads = min(self.heads, GROUP)
        self.units = self.heads // self.unit_heads
        self.unit_rows = self.unit_heads * self.rows
        self.blocks = self.unit_rows // 128
        self.share_rows = self.units * self.unit_rows
        self.by_device = self.unit_heads == GROUP and GROUP * rows_here % 16 == 0

        far = [self.half ^ k for k in range(0, self.half, 2)]
        self.sources = list(range(self.half)) + far + [k ^ 1 for k in far]

    def share(self, part):
        me = lax.axis_index("ctx")
        return (me % self.half) ^ (me // self.half * self.fold) ^ part


def stat_rows(blocks):
    return -(-3 * blocks // 16) * 16


def local(kernel, out_shape, spaces, name, scratch=(), cost=None):
    return pl.pallas_call(
        kernel,
        out_shape=out_shape,
        in_specs=[pl.BlockSpec(memory_space=space) for space in spaces],
        out_specs=jax.tree.map(lambda _: pl.BlockSpec(memory_space=pltpu.VMEM), out_shape),
        scratch_shapes=list(scratch),
        compiler_params=pltpu.CompilerParams(vmem_limit_bytes=VMEM_LIMIT),
        cost_estimate=cost,
        name=name,
    )


def order_kernel(plan, order_ref, one_hot_ref):
    low = lax.axis_index("ctx") % plan.half
    high = lax.axis_index("ctx") // plan.half
    row = lax.broadcasted_iota(jnp.int32, (plan.group_rows, 128), 0)
    lane = lax.broadcasted_iota(jnp.int32, (plan.group_rows, 128), 1)
    query = lax.rem(row, plan.rows)
    device = lax.div(query, plan.rows_here)
    block = device
    if not plan.by_device:
        away = lax.rem(device, plan.half) ^ low
        beyond = plan.half + lax.rem(away, 2) * (plan.half // 2) + lax.div(away, 2)
        block = jnp.where(lax.div(device, plan.half) == high, away, beyond)
    origin = (block * GROUP + lax.div(row, plan.rows)) * plan.rows_here + lax.rem(query, plan.rows_here)
    for at in range(0, plan.group_rows, 128):
        order_ref[:, at : at + 128] = jnp.where(lane + at == origin, 1.0, 0.0).astype(jnp.bfloat16)
    if plan.by_device:
        query = lax.div(row, GROUP * plan.rows_here) * plan.rows_here + lax.rem(row, plan.rows_here)
    one_hot_ref[...] = jnp.where(query == lane, 1.0, 0.0).astype(jnp.bfloat16)


def row_order(plan):
    return local(
        functools.partial(order_kernel, plan),
        [
            jax.ShapeDtypeStruct((plan.group_rows, plan.group_rows), jnp.bfloat16),
            jax.ShapeDtypeStruct((plan.group_rows, 128), jnp.bfloat16),
        ],
        [],
        "order",
        cost=pl.CostEstimate(flops=8_000_000_000, bytes_accessed=0, transcendentals=0),
    )()


def mask_kernel(offset_ref, start_ref, after_ref, bias_ref):
    del after_ref
    span = bias_ref.shape[0]
    position = lax.axis_index("ctx") * span + lax.broadcasted_iota(jnp.int32, (span, 128), 0)
    asked = lax.broadcasted_iota(jnp.int32, (span, 128), 1)
    shown = (position >= start_ref[0]) & (position <= offset_ref[0] + asked)
    bias_ref[...] = jnp.where(shown, 0.0, HIDDEN).astype(jnp.bfloat16)


def mask(span, offsets, starts, after):
    return local(
        mask_kernel,
        jax.ShapeDtypeStruct((span, 128), jnp.bfloat16),
        [pltpu.SMEM, pltpu.SMEM, pl.ANY],
        "mask",
        cost=pl.CostEstimate(flops=1_000_000, bytes_accessed=256 * span, transcendentals=0),
    )(offsets, starts, after)


def join_kernel(*refs):
    *parts, out_ref = refs
    rows = parts[0].shape[1]
    for i, part in enumerate(parts):
        out_ref[:, i * rows : (i + 1) * rows, :] = part[...]


def join(blocks):
    groups, rows, width = blocks[0].shape
    return local(
        join_kernel,
        jax.ShapeDtypeStruct((groups, len(blocks) * rows, width), blocks[0].dtype),
        [pltpu.VMEM] * len(blocks),
        "join",
    )(*blocks)


def write_stats(ref, at, rows):
    values = []
    for peak, total in zip(rows[::2], rows[1::2]):
        high = total.astype(jnp.bfloat16).astype(jnp.float32)
        values += [peak, high, total - high]
    size = stat_rows(len(rows) // 2)
    index = lax.broadcasted_iota(jnp.int32, (size, 128), 0)
    table = jnp.zeros((size, 128), jnp.float32)
    for i, value in enumerate(values):
        table = jnp.where(index == i, value, table)
    ref[at : at + size, :] = table.astype(jnp.bfloat16)


def attend_kernel(plan, part, *refs):
    *refs, score_ref, held_ref = refs
    if part == 0:
        *refs, value_ref, stat_ref = refs
        stat_at = 0
    else:
        *refs, value_ref = refs
        stat_ref, stat_at = value_ref, plan.share_rows
    *query_refs, cache_ref, bias_ref, order_ref, one_hot_ref = refs
    span = cache_ref.shape[0]
    me = lax.axis_index("ctx")
    mine = plan.share(part)
    row_at = pl.multiple_of((mine * plan.heads) % GROUP * plan.rows, plan.unit_rows)
    order = order_ref[pl.ds(row_at, plan.unit_rows), :]
    one_hot = one_hot_ref[pl.ds(row_at, plan.unit_rows), :]
    ones = jnp.ones((span, HD), jnp.bfloat16)
    groups = [(mine * plan.heads + unit * plan.unit_heads) // GROUP for unit in range(plan.units)]
    peaks = []
    for unit, group in enumerate(groups):
        if plan.by_device:
            rows = GROUP * plan.rows_here
            sources = [(ref, 0) for ref in query_refs[:-2]]
            sources += [(ref, at) for ref in query_refs[-2:] for at in range(0, ref.shape[1], rows)]
            for away, (ref, at) in zip(plan.sources, sources):
                to = pl.multiple_of((me ^ away) * rows, rows)
                held_ref[unit, pl.ds(to, rows), :] = ref[group, at : at + rows, :]
            queries = held_ref[unit]
        else:
            stacked = jnp.concatenate([ref[group] for ref in query_refs], axis=0)
            queries = jnp.dot(order, stacked, preferred_element_type=jnp.float32).astype(jnp.bfloat16)
        queries = jnp.concatenate([queries, one_hot], axis=1)
        key_at = pl.multiple_of(group * HD, HD)
        keys = jnp.concatenate([cache_ref[:, pl.ds(key_at, HD)], bias_ref[...]], axis=1)
        scores = lax.dot_general(queries, keys, (((1,), (1,)), ((), ())), preferred_element_type=jnp.float32)
        score_ref[unit] = scores
        peak = [scores[:, at : at + 128] for at in range(0, span, 128)]
        while len(peak) > 1:
            peak = [jnp.maximum(*peak[i : i + 2]) for i in range(0, len(peak) - 1, 2)] + (
                peak[-1:] if len(peak) % 2 else []
            )
        peak = jnp.max(peak[0], axis=1, keepdims=True) * LOG2_SCALE
        peak = jnp.maximum(jnp.ceil(peak * (1.0 / STEP)), FLOOR / STEP)
        peaks.append(jnp.broadcast_to(peak, (plan.unit_rows, 128)))
    same = lax.broadcasted_iota(jnp.int32, (128, 128), 0) == lax.broadcasted_iota(jnp.int32, (128, 128), 1)
    stats = []
    for unit, group in enumerate(groups):
        shift = jnp.concatenate([peaks[unit] * STEP] * (span // 128), axis=1)
        weights = jnp.exp2(score_ref[unit] * LOG2_SCALE - shift)
        value_at = pl.multiple_of((KVH + group) * HD, HD)
        values = jnp.concatenate([cache_ref[:, pl.ds(value_at, HD)], ones], axis=1)
        both = jnp.dot(weights.astype(jnp.bfloat16), values, preferred_element_type=jnp.float32)
        at = unit * plan.unit_rows
        value_ref[at : at + plan.unit_rows, :] = both[:, :HD].astype(value_ref.dtype)
        for block in range(0, plan.unit_rows, 128):
            for wide in (peaks[unit], both[:, HD:]):
                chosen = jnp.where(same, wide[block : block + 128, :], 0.0)
                stats.append(jnp.sum(chosen, axis=0, keepdims=True))
    write_stats(stat_ref, stat_at, stats)


def attend(plan, part, queries, cache, *tables):
    span = cache.shape[0]
    size = stat_rows(plan.units * plan.blocks)
    if part == 0:
        out_shape = [
            jax.ShapeDtypeStruct((plan.share_rows, HD), jnp.float32),
            jax.ShapeDtypeStruct((size, HD), jnp.bfloat16),
        ]
    else:
        out_shape = [jax.ShapeDtypeStruct((plan.share_rows + size, HD), jnp.bfloat16)]
    return local(
        functools.partial(attend_kernel, plan, part),
        out_shape,
        [pltpu.VMEM] * (len(queries) + 1 + len(tables)),
        "attend",
        [
            pltpu.VMEM((plan.units, plan.unit_rows, span), jnp.float32),
            pltpu.VMEM((plan.units, plan.unit_rows, HD), jnp.bfloat16),
        ],
        pl.CostEstimate(
            flops=4 * plan.share_rows * span * HD,
            bytes_accessed=2 * plan.units * span * HD * 2,
            transcendentals=plan.share_rows * span,
        ),
    )(*queries, cache, *tables)


def columns(rows):
    size = -(-len(rows) // 8) * 8
    index = lax.broadcasted_iota(jnp.int32, (size, 128), 0)
    table = jnp.zeros((size, 128), jnp.float32)
    for i, row in enumerate(rows):
        table = jnp.where(index == i, row, table)
    turned = jnp.transpose(jnp.concatenate([table, jnp.zeros((128 - size, 128), jnp.float32)], axis=0))
    return [turned[:, i : i + 1] for i in range(len(rows))]


def factors(stats, block):
    parts = []
    for ref, at in stats:
        base = 3 * block // 16 * 16
        tile = ref[at + base : at + min(base + 32, stat_rows(block + 1)), :].astype(jnp.float32)
        begin = 3 * block - base
        parts.append([tile[begin + i : begin + i + 1] for i in range(3)])
    joint = functools.reduce(jnp.maximum, [peak for peak, _, _ in parts])
    scale = [jnp.exp2((peak - joint) * STEP) for peak, _, _ in parts]
    total = functools.reduce(jnp.add, [f * (high + low) for f, (_, high, low) in zip(scale, parts)])
    return joint, scale, total


def mix(refs, at, scale):
    terms = [f * ref[at : at + 128, :].astype(jnp.float32) for ref, f in zip(refs, scale)]
    return functools.reduce(jnp.add, terms)


def merge_kernel(plan, wide_ref, stat_ref, *refs):
    *parts, out_ref, wide_out_ref = refs
    stats = [(stat_ref, 0)] + [(ref, plan.share_rows) for ref in parts]
    rows, scales = [], []
    for block in range(plan.units * plan.blocks):
        joint, scale, total = factors(stats, block)
        rows += [joint, total]
        scales += scale
    scales = columns(scales)
    for block in range(plan.units * plan.blocks):
        at = block * 128
        mixed = mix([wide_ref] + parts, at, scales[block * len(stats) : (block + 1) * len(stats)])
        wide_out_ref[at : at + 128, :] = mixed
        out_ref[at : at + 128, :] = mixed.astype(jnp.bfloat16)
    write_stats(out_ref, plan.share_rows, rows)


def merge(plan, wide, stats, parts):
    rows = plan.share_rows + stat_rows(plan.units * plan.blocks)
    return local(
        functools.partial(merge_kernel, plan),
        [
            jax.ShapeDtypeStruct((rows, HD), jnp.bfloat16),
            jax.ShapeDtypeStruct((plan.share_rows, HD), jnp.float32),
        ],
        [pltpu.VMEM] * (len(parts) + 2),
        "merge",
    )(wide, stats, *parts)


def settle_kernel(plan, wide_ref, own_ref, other_ref, order_ref, out_ref):
    stats = [(own_ref, plan.share_rows), (other_ref, plan.share_rows)]
    scales = []
    for block in range(plan.units * plan.blocks):
        _, scale, total = factors(stats, block)
        scales += [f / total for f in scale]
    scales = columns(scales)
    for unit in range(plan.units):
        done = []
        for block in range(unit * plan.blocks, (unit + 1) * plan.blocks):
            mixed = mix([wide_ref, other_ref], block * 128, scales[2 * block : 2 * block + 2])
            done.append(mixed.astype(jnp.bfloat16))
        done = jnp.concatenate(done, axis=0)
        if plan.by_device:
            done = jnp.dot(order_ref[...], done, preferred_element_type=jnp.float32).astype(jnp.bfloat16)
        for head in range(plan.unit_heads):
            to = (unit * plan.unit_heads + head) * HD
            out_ref[:, to : to + HD] = done[head * plan.rows : (head + 1) * plan.rows, :]


def settle(plan, wide, own, other, order):
    return local(
        functools.partial(settle_kernel, plan),
        jax.ShapeDtypeStruct((plan.rows, plan.heads * HD), jnp.bfloat16),
        [pltpu.VMEM] * 4,
        "settle",
    )(wide, own, other, order)


def project_kernel(plan, part, *refs):
    block_ref, weight_ref, *before, out_ref = refs
    depth = plan.heads * HD
    at = pl.multiple_of(plan.share(part) * depth, depth)
    total = jnp.dot(block_ref[...], weight_ref[pl.ds(at, depth), :], preferred_element_type=jnp.float32)
    for ref in before:
        total = total + ref[...]
    out_ref[...] = total.astype(out_ref.dtype)


def project(plan, part, block, weight, before, dtype):
    operands = [block, weight] + ([] if before is None else [before])
    return local(
        functools.partial(project_kernel, plan, part),
        jax.ShapeDtypeStruct((plan.rows, weight.shape[1]), dtype),
        [pltpu.VMEM] * len(operands),
        "project",
    )(*operands)


def per_device(queries, cache, out_weight, offsets, starts):
    plan = Plan(lax.axis_size("ctx"), queries.shape[0])
    half = plan.half
    cache = pltpu.with_memory_space_constraint(cache, pltpu.VMEM)
    out_weight = pltpu.with_memory_space_constraint(out_weight, pltpu.VMEM)

    own = queries.reshape(plan.rows_here, KVH, GROUP, HD)
    own = own.transpose(1, 2, 0, 3).reshape(KVH, GROUP * plan.rows_here, HD)
    far = [swap(own, "ctx", k) for k in plan.sources[half : half + half // 2]]
    near = [swap(own, "ctx", k) for k in range(1, half)]
    order, one_hot = row_order(plan)
    bias = mask(cache.shape[0], offsets, starts, near[-1])
    if plan.by_device:
        far = join(far)
        gathered = [own] + near + [far, swap(far, "ctx", 1)]
    else:
        far = jnp.concatenate(far, axis=1)
        gathered = [jnp.concatenate([own] + near + [far, swap(far, "ctx", 1)], axis=1)]

    received = []
    for part in reversed(range(1, half)):
        (piece,) = attend(plan, part, gathered, cache, bias, order, one_hot)
        received.append(swap(piece, "ctx", part))
    wide, stats = attend(plan, 0, gathered, cache, bias, order, one_hot)

    near, near_wide = merge(plan, wide, stats, received)
    block = settle(plan, near_wide, near, swap(near, "ctx", plan.across), order)

    total = project(plan, 0, block, out_weight, None, jnp.float32)
    blocks = [swap(block, "ctx", k) for k in range(1, half)]
    for k in range(1, half):
        dtype = jnp.float32 if k < half - 1 else jnp.bfloat16
        total = project(plan, k, blocks[k - 1], out_weight, total, dtype)
    return from_behind(total, "segment", 1)


def solution(mesh):
    in_specs = (
        P(("segment", "ctx"), None),
        P(("segment", "ctx"), None),
        P("segment", "ctx"),
        P("segment"),
        P("segment"),
    )
    out_specs = P("segment", "ctx")
    return jax.shard_map(
        per_device, mesh=mesh, in_specs=in_specs, out_specs=out_specs, check_vma=False
    )
```

```python
import functools
import math

import jax
import jax.numpy as jnp
from jax import lax
from jax.experimental import pallas as pl
from jax.experimental.pallas import tpu as pltpu
from jax.sharding import PartitionSpec as P

H = 64
KVH = 8
HD = 128
GROUP = H // KVH
LOG2_SCALE = HD ** (-0.5) * math.log2(math.e)
STEP = 8.0
FLOOR = -4096.0
HIDDEN = -1e30
STATS = 16
VMEM_LIMIT = 12 * 1024 * 1024


def swap(value, axis, bits):
    devices = lax.axis_size(axis)
    return lax.ppermute(value, axis, [(i, i ^ bits) for i in range(devices)])


def from_behind(value, axis, by):
    devices = lax.axis_size(axis)
    return lax.ppermute(value, axis, [(i, (i + by) % devices) for i in range(devices)])


class Plan:
    def __init__(self, ctx, rows_here):
        self.ctx = ctx
        self.half = ctx // 2
        self.fold = self.half // 2
        self.across = self.half | self.fold
        self.rows_here = rows_here
        self.rows = ctx * rows_here
        self.group_rows = GROUP * self.rows
        self.heads = H // self.half
        self.unit_heads = min(self.heads, GROUP)
        self.units = self.heads // self.unit_heads
        self.unit_rows = self.unit_heads * self.rows
        self.blocks = self.unit_rows // 128
        self.share_rows = self.units * self.unit_rows
        self.by_device = self.unit_heads == GROUP and GROUP * rows_here % 16 == 0

    def share(self, part):
        me = lax.axis_index("ctx")
        return (me % self.half) ^ (me // self.half * self.fold) ^ part


def stat_rows(blocks):
    return -(-3 * blocks // 16) * 16


def local(kernel, out_shape, spaces, name, scratch=(), cost=None):
    return pl.pallas_call(
        kernel,
        out_shape=out_shape,
        in_specs=[pl.BlockSpec(memory_space=space) for space in spaces],
        out_specs=jax.tree.map(lambda _: pl.BlockSpec(memory_space=pltpu.VMEM), out_shape),
        scratch_shapes=list(scratch),
        compiler_params=pltpu.CompilerParams(vmem_limit_bytes=VMEM_LIMIT),
        cost_estimate=cost,
        name=name,
    )


def order_kernel(plan, order_ref, one_hot_ref):
    low = lax.axis_index("ctx") % plan.half
    high = lax.axis_index("ctx") // plan.half
    row = lax.broadcasted_iota(jnp.int32, (plan.group_rows, 128), 0)
    lane = lax.broadcasted_iota(jnp.int32, (plan.group_rows, 128), 1)
    query = lax.rem(row, plan.rows)
    device = lax.div(query, plan.rows_here)
    block = device
    if not plan.by_device:
        block = 2 * (lax.rem(device, plan.half) ^ low) + (lax.div(device, plan.half) ^ high)
    origin = (block * GROUP + lax.div(row, plan.rows)) * plan.rows_here + lax.rem(query, plan.rows_here)
    for at in range(0, plan.group_rows, 128):
        order_ref[:, at : at + 128] = jnp.where(lane + at == origin, 1.0, 0.0).astype(jnp.bfloat16)
    if plan.by_device:
        query = lax.div(row, GROUP * plan.rows_here) * plan.rows_here + lax.rem(row, plan.rows_here)
    one_hot_ref[...] = jnp.where(query == lane, 1.0, 0.0).astype(jnp.bfloat16)


def row_order(plan):
    return local(
        functools.partial(order_kernel, plan),
        [
            jax.ShapeDtypeStruct((plan.group_rows, plan.group_rows), jnp.bfloat16),
            jax.ShapeDtypeStruct((plan.group_rows, 128), jnp.bfloat16),
        ],
        [],
        "order",
        cost=pl.CostEstimate(flops=8_000_000_000, bytes_accessed=0, transcendentals=0),
    )()


def mask_kernel(offset_ref, start_ref, after_ref, bias_ref):
    del after_ref
    span = bias_ref.shape[0]
    position = lax.axis_index("ctx") * span + lax.broadcasted_iota(jnp.int32, (span, 128), 0)
    asked = lax.broadcasted_iota(jnp.int32, (span, 128), 1)
    shown = (position >= start_ref[0]) & (position <= offset_ref[0] + asked)
    bias_ref[...] = jnp.where(shown, 0.0, HIDDEN).astype(jnp.bfloat16)


def mask(span, offsets, starts, after):
    return local(
        mask_kernel,
        jax.ShapeDtypeStruct((span, 128), jnp.bfloat16),
        [pltpu.SMEM, pltpu.SMEM, pl.ANY],
        "mask",
        cost=pl.CostEstimate(flops=1_000_000, bytes_accessed=256 * span, transcendentals=0),
    )(offsets, starts, after)


def write_stats(ref, at, rows):
    values = []
    for peak, total in zip(rows[::2], rows[1::2]):
        high = total.astype(jnp.bfloat16).astype(jnp.float32)
        values += [peak, high, total - high]
    size = stat_rows(len(rows) // 2)
    index = lax.broadcasted_iota(jnp.int32, (size, 128), 0)
    table = jnp.zeros((size, 128), jnp.float32)
    for i, value in enumerate(values):
        table = jnp.where(index == i, value, table)
    ref[at : at + size, :] = table.astype(jnp.bfloat16)


def attend_kernel(plan, part, *refs):
    *refs, score_ref, held_ref = refs
    if part == 0:
        *refs, value_ref, stat_ref = refs
        stat_at = 0
    else:
        *refs, value_ref = refs
        stat_ref, stat_at = value_ref, plan.share_rows
    *query_refs, cache_ref, bias_ref, order_ref, one_hot_ref = refs
    span = cache_ref.shape[0]
    me = lax.axis_index("ctx")
    mine = plan.share(part)
    row_at = pl.multiple_of((mine * plan.heads) % GROUP * plan.rows, plan.unit_rows)
    order = order_ref[pl.ds(row_at, plan.unit_rows), :]
    one_hot = one_hot_ref[pl.ds(row_at, plan.unit_rows), :]
    ones = jnp.ones((span, HD), jnp.bfloat16)
    groups = [(mine * plan.heads + unit * plan.unit_heads) // GROUP for unit in range(plan.units)]
    peaks = []
    for unit, group in enumerate(groups):
        if plan.by_device:
            for block, ref in enumerate(query_refs):
                device = me ^ (block // 2) ^ (block % 2 * plan.half)
                to = pl.multiple_of(device * GROUP * plan.rows_here, GROUP * plan.rows_here)
                held_ref[unit, pl.ds(to, GROUP * plan.rows_here), :] = ref[group]
            queries = held_ref[unit]
        else:
            stacked = jnp.concatenate([ref[group] for ref in query_refs], axis=0)
            queries = jnp.dot(order, stacked, preferred_element_type=jnp.float32).astype(jnp.bfloat16)
        queries = jnp.concatenate([queries, one_hot], axis=1)
        key_at = pl.multiple_of(group * HD, HD)
        keys = jnp.concatenate([cache_ref[:, pl.ds(key_at, HD)], bias_ref[...]], axis=1)
        scores = lax.dot_general(queries, keys, (((1,), (1,)), ((), ())), preferred_element_type=jnp.float32)
        score_ref[unit] = scores
        peak = [scores[:, at : at + 128] for at in range(0, span, 128)]
        while len(peak) > 1:
            peak = [jnp.maximum(*peak[i : i + 2]) for i in range(0, len(peak) - 1, 2)] + (
                peak[-1:] if len(peak) % 2 else []
            )
        peak = jnp.max(peak[0], axis=1, keepdims=True) * LOG2_SCALE
        peak = jnp.maximum(jnp.ceil(peak * (1.0 / STEP)), FLOOR / STEP)
        peaks.append(jnp.broadcast_to(peak, (plan.unit_rows, 128)))
    same = lax.broadcasted_iota(jnp.int32, (128, 128), 0) == lax.broadcasted_iota(jnp.int32, (128, 128), 1)
    stats = []
    for unit, group in enumerate(groups):
        shift = jnp.concatenate([peaks[unit] * STEP] * (span // 128), axis=1)
        weights = jnp.exp2(score_ref[unit] * LOG2_SCALE - shift)
        value_at = pl.multiple_of((KVH + group) * HD, HD)
        values = jnp.concatenate([cache_ref[:, pl.ds(value_at, HD)], ones], axis=1)
        both = jnp.dot(weights.astype(jnp.bfloat16), values, preferred_element_type=jnp.float32)
        at = unit * plan.unit_rows
        value_ref[at : at + plan.unit_rows, :] = both[:, :HD].astype(value_ref.dtype)
        for block in range(0, plan.unit_rows, 128):
            for wide in (peaks[unit], both[:, HD:]):
                chosen = jnp.where(same, wide[block : block + 128, :], 0.0)
                stats.append(jnp.sum(chosen, axis=0, keepdims=True))
    write_stats(stat_ref, stat_at, stats)


def attend(plan, part, queries, cache, *tables):
    span = cache.shape[0]
    size = stat_rows(plan.units * plan.blocks)
    if part == 0:
        out_shape = [
            jax.ShapeDtypeStruct((plan.share_rows, HD), jnp.float32),
            jax.ShapeDtypeStruct((size, HD), jnp.bfloat16),
        ]
    else:
        out_shape = [jax.ShapeDtypeStruct((plan.share_rows + size, HD), jnp.bfloat16)]
    return local(
        functools.partial(attend_kernel, plan, part),
        out_shape,
        [pltpu.VMEM] * (len(queries) + 1 + len(tables)),
        "attend",
        [
            pltpu.VMEM((plan.units, plan.unit_rows, span), jnp.float32),
            pltpu.VMEM((plan.units, plan.unit_rows, HD), jnp.bfloat16),
        ],
        pl.CostEstimate(
            flops=4 * plan.share_rows * span * HD,
            bytes_accessed=2 * plan.units * span * HD * 2,
            transcendentals=plan.share_rows * span,
        ),
    )(*queries, cache, *tables)


def columns(rows):
    size = -(-len(rows) // 8) * 8
    index = lax.broadcasted_iota(jnp.int32, (size, 128), 0)
    table = jnp.zeros((size, 128), jnp.float32)
    for i, row in enumerate(rows):
        table = jnp.where(index == i, row, table)
    turned = jnp.transpose(jnp.concatenate([table, jnp.zeros((128 - size, 128), jnp.float32)], axis=0))
    return [turned[:, i : i + 1] for i in range(len(rows))]


def factors(stats, block):
    parts = []
    for ref, at in stats:
        base = 3 * block // 16 * 16
        tile = ref[at + base : at + min(base + 32, stat_rows(block + 1)), :].astype(jnp.float32)
        begin = 3 * block - base
        parts.append([tile[begin + i : begin + i + 1] for i in range(3)])
    joint = functools.reduce(jnp.maximum, [peak for peak, _, _ in parts])
    scale = [jnp.exp2((peak - joint) * STEP) for peak, _, _ in parts]
    total = functools.reduce(jnp.add, [f * (high + low) for f, (_, high, low) in zip(scale, parts)])
    return joint, scale, total


def mix(refs, at, scale):
    terms = [f * ref[at : at + 128, :].astype(jnp.float32) for ref, f in zip(refs, scale)]
    return functools.reduce(jnp.add, terms)


def merge_kernel(plan, wide_ref, stat_ref, *refs):
    *parts, out_ref, wide_out_ref = refs
    stats = [(stat_ref, 0)] + [(ref, plan.share_rows) for ref in parts]
    rows, scales = [], []
    for block in range(plan.units * plan.blocks):
        joint, scale, total = factors(stats, block)
        rows += [joint, total]
        scales += scale
    scales = columns(scales)
    for block in range(plan.units * plan.blocks):
        at = block * 128
        mixed = mix([wide_ref] + parts, at, scales[block * len(stats) : (block + 1) * len(stats)])
        wide_out_ref[at : at + 128, :] = mixed
        out_ref[at : at + 128, :] = mixed.astype(jnp.bfloat16)
    write_stats(out_ref, plan.share_rows, rows)


def merge(plan, wide, stats, parts):
    rows = plan.share_rows + stat_rows(plan.units * plan.blocks)
    return local(
        functools.partial(merge_kernel, plan),
        [
            jax.ShapeDtypeStruct((rows, HD), jnp.bfloat16),
            jax.ShapeDtypeStruct((plan.share_rows, HD), jnp.float32),
        ],
        [pltpu.VMEM] * (len(parts) + 2),
        "merge",
    )(wide, stats, *parts)


def settle_kernel(plan, wide_ref, own_ref, other_ref, order_ref, out_ref):
    stats = [(own_ref, plan.share_rows), (other_ref, plan.share_rows)]
    scales = []
    for block in range(plan.units * plan.blocks):
        _, scale, total = factors(stats, block)
        scales += [f / total for f in scale]
    scales = columns(scales)
    for unit in range(plan.units):
        done = []
        for block in range(unit * plan.blocks, (unit + 1) * plan.blocks):
            mixed = mix([wide_ref, other_ref], block * 128, scales[2 * block : 2 * block + 2])
            done.append(mixed.astype(jnp.bfloat16))
        done = jnp.concatenate(done, axis=0)
        if plan.by_device:
            done = jnp.dot(order_ref[...], done, preferred_element_type=jnp.float32).astype(jnp.bfloat16)
        for head in range(plan.unit_heads):
            to = (unit * plan.unit_heads + head) * HD
            out_ref[:, to : to + HD] = done[head * plan.rows : (head + 1) * plan.rows, :]


def settle(plan, wide, own, other, order):
    return local(
        functools.partial(settle_kernel, plan),
        jax.ShapeDtypeStruct((plan.rows, plan.heads * HD), jnp.bfloat16),
        [pltpu.VMEM] * 4,
        "settle",
    )(wide, own, other, order)


def project_kernel(plan, part, *refs):
    block_ref, weight_ref, *before, out_ref = refs
    depth = plan.heads * HD
    at = pl.multiple_of(plan.share(part) * depth, depth)
    total = jnp.dot(block_ref[...], weight_ref[pl.ds(at, depth), :], preferred_element_type=jnp.float32)
    for ref in before:
        total = total + ref[...]
    out_ref[...] = total.astype(out_ref.dtype)


def project(plan, part, block, weight, before, dtype):
    operands = [block, weight] + ([] if before is None else [before])
    return local(
        functools.partial(project_kernel, plan, part),
        jax.ShapeDtypeStruct((plan.rows, weight.shape[1]), dtype),
        [pltpu.VMEM] * len(operands),
        "project",
    )(*operands)


def per_device(queries, cache, out_weight, offsets, starts):
    plan = Plan(lax.axis_size("ctx"), queries.shape[0])
    half = plan.half
    cache = pltpu.with_memory_space_constraint(cache, pltpu.VMEM)
    out_weight = pltpu.with_memory_space_constraint(out_weight, pltpu.VMEM)

    own = queries.reshape(plan.rows_here, KVH, GROUP, HD)
    own = own.transpose(1, 2, 0, 3).reshape(KVH, GROUP * plan.rows_here, HD)
    far = swap(own, "ctx", half)
    near = [swap(own, "ctx", k) for k in range(1, half)]
    order, one_hot = row_order(plan)
    bias = mask(cache.shape[0], offsets, starts, near[-1])
    if plan.by_device:
        gathered = [own, far]
        for k in range(1, half):
            gathered += [near[k - 1], swap(far, "ctx", k)]
    else:
        pair = jnp.concatenate([own, far], axis=1)
        gathered = [pair] + [swap(pair, "ctx", k) for k in range(1, half)]

    received = []
    for part in sorted(range(1, half), key=lambda k: (k % 2 == 0, -k)):
        (piece,) = attend(plan, part, gathered, cache, bias, order, one_hot)
        received.append(swap(piece, "ctx", part))
    wide, stats = attend(plan, 0, gathered, cache, bias, order, one_hot)

    near, near_wide = merge(plan, wide, stats, received)
    block = settle(plan, near_wide, near, swap(near, "ctx", plan.across), order)

    total = project(plan, 0, block, out_weight, None, jnp.float32)
    blocks = [swap(block, "ctx", k) for k in range(1, half)]
    for k in range(1, half):
        dtype = jnp.float32 if k < half - 1 else jnp.bfloat16
        total = project(plan, k, blocks[k - 1], out_weight, total, dtype)
    return from_behind(total, "segment", 1)


def solution(mesh):
    in_specs = (
        P(("segment", "ctx"), None),
        P(("segment", "ctx"), None),
        P("segment", "ctx"),
        P("segment"),
        P("segment"),
    )
    out_specs = P("segment", "ctx")
    return jax.shard_map(
        per_device, mesh=mesh, in_specs=in_specs, out_specs=out_specs, check_vma=False
    )
```

```python
import functools
import math

import jax
import jax.numpy as jnp
from jax import lax
from jax.experimental import pallas as pl
from jax.experimental.pallas import tpu as pltpu
from jax.sharding import PartitionSpec as P

H = 64
KVH = 8
HD = 128
GROUP = H // KVH
LOG2_SCALE = HD ** (-0.5) * math.log2(math.e)
STEP = 8.0
FLOOR = -4096.0
HIDDEN = -1e30
STATS = 16
VMEM_LIMIT = 12 * 1024 * 1024


def swap(value, axis, bits):
    devices = lax.axis_size(axis)
    return lax.ppermute(value, axis, [(i, i ^ bits) for i in range(devices)])


def from_behind(value, axis, by):
    devices = lax.axis_size(axis)
    return lax.ppermute(value, axis, [(i, (i + by) % devices) for i in range(devices)])


class Plan:
    def __init__(self, ctx, rows_here):
        self.ctx = ctx
        self.half = ctx // 2
        self.fold = self.half // 2
        self.across = self.half | self.fold
        self.rows_here = rows_here
        self.rows = ctx * rows_here
        self.group_rows = GROUP * self.rows
        self.heads = H // self.half
        self.unit_heads = min(self.heads, GROUP)
        self.units = self.heads // self.unit_heads
        self.unit_rows = self.unit_heads * self.rows
        self.blocks = self.unit_rows // 128
        self.share_rows = self.units * self.unit_rows
        self.by_device = self.unit_heads == GROUP and GROUP * rows_here % 16 == 0

    def share(self, part):
        me = lax.axis_index("ctx")
        return (me % self.half) ^ (me // self.half * self.fold) ^ part


def stat_rows(blocks):
    return -(-3 * blocks // 16) * 16


def local(kernel, out_shape, spaces, name, scratch=(), cost=None):
    return pl.pallas_call(
        kernel,
        out_shape=out_shape,
        in_specs=[pl.BlockSpec(memory_space=space) for space in spaces],
        out_specs=jax.tree.map(lambda _: pl.BlockSpec(memory_space=pltpu.VMEM), out_shape),
        scratch_shapes=list(scratch),
        compiler_params=pltpu.CompilerParams(vmem_limit_bytes=VMEM_LIMIT),
        cost_estimate=cost,
        name=name,
    )


def order_kernel(plan, order_ref, one_hot_ref):
    low = lax.axis_index("ctx") % plan.half
    high = lax.axis_index("ctx") // plan.half
    row = lax.broadcasted_iota(jnp.int32, (plan.group_rows, 128), 0)
    lane = lax.broadcasted_iota(jnp.int32, (plan.group_rows, 128), 1)
    query = lax.rem(row, plan.rows)
    device = lax.div(query, plan.rows_here)
    block = device
    if not plan.by_device:
        block = 2 * (lax.rem(device, plan.half) ^ low) + (lax.div(device, plan.half) ^ high)
    origin = (block * GROUP + lax.div(row, plan.rows)) * plan.rows_here + lax.rem(query, plan.rows_here)
    for at in range(0, plan.group_rows, 128):
        order_ref[:, at : at + 128] = jnp.where(lane + at == origin, 1.0, 0.0).astype(jnp.bfloat16)
    if plan.by_device:
        query = lax.div(row, GROUP * plan.rows_here) * plan.rows_here + lax.rem(row, plan.rows_here)
    one_hot_ref[...] = jnp.where(query == lane, 1.0, 0.0).astype(jnp.bfloat16)


def row_order(plan):
    return local(
        functools.partial(order_kernel, plan),
        [
            jax.ShapeDtypeStruct((plan.group_rows, plan.group_rows), jnp.bfloat16),
            jax.ShapeDtypeStruct((plan.group_rows, 128), jnp.bfloat16),
        ],
        [],
        "order",
        cost=pl.CostEstimate(flops=8_000_000_000, bytes_accessed=0, transcendentals=0),
    )()


def mask_kernel(offset_ref, start_ref, after_ref, bias_ref):
    del after_ref
    span = bias_ref.shape[0]
    position = lax.axis_index("ctx") * span + lax.broadcasted_iota(jnp.int32, (span, 128), 0)
    asked = lax.broadcasted_iota(jnp.int32, (span, 128), 1)
    shown = (position >= start_ref[0]) & (position <= offset_ref[0] + asked)
    bias_ref[...] = jnp.where(shown, 0.0, HIDDEN).astype(jnp.bfloat16)


def mask(span, offsets, starts, after):
    return local(
        mask_kernel,
        jax.ShapeDtypeStruct((span, 128), jnp.bfloat16),
        [pltpu.SMEM, pltpu.SMEM, pl.ANY],
        "mask",
        cost=pl.CostEstimate(flops=1_000_000, bytes_accessed=256 * span, transcendentals=0),
    )(offsets, starts, after)


def write_stats(ref, at, rows):
    values = []
    for peak, total in zip(rows[::2], rows[1::2]):
        high = total.astype(jnp.bfloat16).astype(jnp.float32)
        values += [peak, high, total - high]
    size = stat_rows(len(rows) // 2)
    index = lax.broadcasted_iota(jnp.int32, (size, 128), 0)
    table = jnp.zeros((size, 128), jnp.float32)
    for i, value in enumerate(values):
        table = jnp.where(index == i, value, table)
    ref[at : at + size, :] = table.astype(jnp.bfloat16)


def attend_kernel(plan, part, *refs):
    *refs, score_ref, held_ref = refs
    if part == 0:
        *refs, value_ref, stat_ref = refs
        stat_at = 0
    else:
        *refs, value_ref = refs
        stat_ref, stat_at = value_ref, plan.share_rows
    *query_refs, cache_ref, bias_ref, order_ref, one_hot_ref = refs
    span = cache_ref.shape[0]
    me = lax.axis_index("ctx")
    mine = plan.share(part)
    row_at = pl.multiple_of((mine * plan.heads) % GROUP * plan.rows, plan.unit_rows)
    order = order_ref[pl.ds(row_at, plan.unit_rows), :]
    one_hot = one_hot_ref[pl.ds(row_at, plan.unit_rows), :]
    ones = jnp.ones((span, HD), jnp.bfloat16)
    groups = [(mine * plan.heads + unit * plan.unit_heads) // GROUP for unit in range(plan.units)]
    peaks = []
    for unit, group in enumerate(groups):
        if plan.by_device:
            for block, ref in enumerate(query_refs):
                device = me ^ (block // 2) ^ (block % 2 * plan.half)
                to = pl.multiple_of(device * GROUP * plan.rows_here, GROUP * plan.rows_here)
                held_ref[unit, pl.ds(to, GROUP * plan.rows_here), :] = ref[group]
            queries = held_ref[unit]
        else:
            stacked = jnp.concatenate([ref[group] for ref in query_refs], axis=0)
            queries = jnp.dot(order, stacked, preferred_element_type=jnp.float32).astype(jnp.bfloat16)
        queries = jnp.concatenate([queries, one_hot], axis=1)
        key_at = pl.multiple_of(group * HD, HD)
        keys = jnp.concatenate([cache_ref[:, pl.ds(key_at, HD)], bias_ref[...]], axis=1)
        scores = lax.dot_general(queries, keys, (((1,), (1,)), ((), ())), preferred_element_type=jnp.float32)
        score_ref[unit] = scores
        peak = [scores[:, at : at + 128] for at in range(0, span, 128)]
        while len(peak) > 1:
            peak = [jnp.maximum(*peak[i : i + 2]) for i in range(0, len(peak) - 1, 2)] + (
                peak[-1:] if len(peak) % 2 else []
            )
        peak = jnp.max(peak[0], axis=1, keepdims=True) * LOG2_SCALE
        peak = jnp.maximum(jnp.ceil(peak * (1.0 / STEP)), FLOOR / STEP)
        peaks.append(jnp.broadcast_to(peak, (plan.unit_rows, 128)))
    same = lax.broadcasted_iota(jnp.int32, (128, 128), 0) == lax.broadcasted_iota(jnp.int32, (128, 128), 1)
    stats = []
    for unit, group in enumerate(groups):
        shift = jnp.concatenate([peaks[unit] * STEP] * (span // 128), axis=1)
        weights = jnp.exp2(score_ref[unit] * LOG2_SCALE - shift)
        value_at = pl.multiple_of((KVH + group) * HD, HD)
        values = jnp.concatenate([cache_ref[:, pl.ds(value_at, HD)], ones], axis=1)
        both = jnp.dot(weights.astype(jnp.bfloat16), values, preferred_element_type=jnp.float32)
        at = unit * plan.unit_rows
        value_ref[at : at + plan.unit_rows, :] = both[:, :HD].astype(value_ref.dtype)
        for block in range(0, plan.unit_rows, 128):
            for wide in (peaks[unit], both[:, HD:]):
                chosen = jnp.where(same, wide[block : block + 128, :], 0.0)
                stats.append(jnp.sum(chosen, axis=0, keepdims=True))
    write_stats(stat_ref, stat_at, stats)


def attend(plan, part, queries, cache, *tables):
    span = cache.shape[0]
    size = stat_rows(plan.units * plan.blocks)
    if part == 0:
        out_shape = [
            jax.ShapeDtypeStruct((plan.share_rows, HD), jnp.float32),
            jax.ShapeDtypeStruct((size, HD), jnp.bfloat16),
        ]
    else:
        out_shape = [jax.ShapeDtypeStruct((plan.share_rows + size, HD), jnp.bfloat16)]
    return local(
        functools.partial(attend_kernel, plan, part),
        out_shape,
        [pltpu.VMEM] * (len(queries) + 1 + len(tables)),
        "attend",
        [
            pltpu.VMEM((plan.units, plan.unit_rows, span), jnp.float32),
            pltpu.VMEM((plan.units, plan.unit_rows, HD), jnp.bfloat16),
        ],
        pl.CostEstimate(
            flops=4 * plan.share_rows * span * HD,
            bytes_accessed=2 * plan.units * span * HD * 2,
            transcendentals=plan.share_rows * span,
        ),
    )(*queries, cache, *tables)


def columns(rows):
    size = -(-len(rows) // 8) * 8
    index = lax.broadcasted_iota(jnp.int32, (size, 128), 0)
    table = jnp.zeros((size, 128), jnp.float32)
    for i, row in enumerate(rows):
        table = jnp.where(index == i, row, table)
    turned = jnp.transpose(jnp.concatenate([table, jnp.zeros((128 - size, 128), jnp.float32)], axis=0))
    return [turned[:, i : i + 1] for i in range(len(rows))]


def factors(stats, block):
    parts = []
    for ref, at in stats:
        base = 3 * block // 16 * 16
        tile = ref[at + base : at + min(base + 32, stat_rows(block + 1)), :].astype(jnp.float32)
        begin = 3 * block - base
        parts.append([tile[begin + i : begin + i + 1] for i in range(3)])
    joint = functools.reduce(jnp.maximum, [peak for peak, _, _ in parts])
    scale = [jnp.exp2((peak - joint) * STEP) for peak, _, _ in parts]
    total = functools.reduce(jnp.add, [f * (high + low) for f, (_, high, low) in zip(scale, parts)])
    return joint, scale, total


def mix(refs, at, scale):
    terms = [f * ref[at : at + 128, :].astype(jnp.float32) for ref, f in zip(refs, scale)]
    return functools.reduce(jnp.add, terms)


def merge_kernel(plan, wide_ref, stat_ref, *refs):
    *parts, out_ref, wide_out_ref = refs
    size = stat_rows(plan.units * plan.blocks)
    stats = [(stat_ref, stat_ref.shape[0] - size)] + [(ref, plan.share_rows) for ref in parts]
    rows, scales = [], []
    for block in range(plan.units * plan.blocks):
        joint, scale, total = factors(stats, block)
        rows += [joint, total]
        scales += scale
    scales = columns(scales)
    for block in range(plan.units * plan.blocks):
        at = block * 128
        mixed = mix([wide_ref] + parts, at, scales[block * len(stats) : (block + 1) * len(stats)])
        wide_out_ref[at : at + 128, :] = mixed
        out_ref[at : at + 128, :] = mixed.astype(jnp.bfloat16)
    write_stats(out_ref, plan.share_rows, rows)


def merge(plan, wide, stats, parts):
    rows = plan.share_rows + stat_rows(plan.units * plan.blocks)
    return local(
        functools.partial(merge_kernel, plan),
        [
            jax.ShapeDtypeStruct((rows, HD), jnp.bfloat16),
            jax.ShapeDtypeStruct((plan.share_rows, HD), jnp.float32),
        ],
        [pltpu.VMEM] * (len(parts) + 2),
        "merge",
    )(wide, stats, *parts)


def settle_kernel(plan, wide_ref, own_ref, other_ref, order_ref, out_ref):
    stats = [(own_ref, plan.share_rows), (other_ref, plan.share_rows)]
    scales = []
    for block in range(plan.units * plan.blocks):
        _, scale, total = factors(stats, block)
        scales += [f / total for f in scale]
    scales = columns(scales)
    done = []
    for block in range(plan.units * plan.blocks):
        mixed = mix([wide_ref, other_ref], block * 128, scales[2 * block : 2 * block + 2])
        done.append(mixed.astype(jnp.bfloat16))
    done = [done[unit * plan.blocks : (unit + 1) * plan.blocks] for unit in range(plan.units)]
    done = jnp.concatenate([jnp.concatenate(blocks, axis=0) for blocks in done], axis=1)
    if plan.by_device:
        done = jnp.dot(order_ref[...], done, preferred_element_type=jnp.float32).astype(jnp.bfloat16)
    for unit in range(plan.units):
        for head in range(plan.unit_heads):
            to = (unit * plan.unit_heads + head) * HD
            rows = slice(head * plan.rows, (head + 1) * plan.rows)
            out_ref[:, to : to + HD] = done[rows, unit * HD : (unit + 1) * HD]


def settle(plan, wide, own, other, order):
    return local(
        functools.partial(settle_kernel, plan),
        jax.ShapeDtypeStruct((plan.rows, plan.heads * HD), jnp.bfloat16),
        [pltpu.VMEM] * 4,
        "settle",
    )(wide, own, other, order)


def project_kernel(plan, part, *refs):
    block_ref, weight_ref, *before, out_ref = refs
    depth = plan.heads * HD
    at = pl.multiple_of(plan.share(part) * depth, depth)
    total = jnp.dot(block_ref[...], weight_ref[pl.ds(at, depth), :], preferred_element_type=jnp.float32)
    for ref in before:
        total = total + ref[...]
    out_ref[...] = total.astype(out_ref.dtype)


def project(plan, part, block, weight, before, dtype):
    operands = [block, weight] + ([] if before is None else [before])
    return local(
        functools.partial(project_kernel, plan, part),
        jax.ShapeDtypeStruct((plan.rows, weight.shape[1]), dtype),
        [pltpu.VMEM] * len(operands),
        "project",
    )(*operands)


def per_device(queries, cache, out_weight, offsets, starts):
    plan = Plan(lax.axis_size("ctx"), queries.shape[0])
    half = plan.half
    cache = pltpu.with_memory_space_constraint(cache, pltpu.VMEM)
    out_weight = pltpu.with_memory_space_constraint(out_weight, pltpu.VMEM)

    own = queries.reshape(plan.rows_here, KVH, GROUP, HD)
    own = own.transpose(1, 2, 0, 3).reshape(KVH, GROUP * plan.rows_here, HD)
    far = swap(own, "ctx", half)
    near = [swap(own, "ctx", k) for k in range(1, half)]
    order, one_hot = row_order(plan)
    bias = mask(cache.shape[0], offsets, starts, near[-1])
    if plan.by_device:
        gathered = [own, far]
        for k in range(1, half):
            gathered += [near[k - 1], swap(far, "ctx", k)]
    else:
        pair = jnp.concatenate([own, far], axis=1)
        gathered = [pair] + [swap(pair, "ctx", k) for k in range(1, half)]

    received = []
    for part in reversed(range(1, half)):
        (piece,) = attend(plan, part, gathered, cache, bias, order, one_hot)
        received.append(swap(piece, "ctx", part))
    wide, stats = attend(plan, 0, gathered, cache, bias, order, one_hot)

    near, wide = merge(plan, wide, stats, received[:-1])
    near, wide = merge(plan, wide, near, received[-1:])
    block = settle(plan, wide, near, swap(near, "ctx", plan.across), order)

    total = project(plan, 0, block, out_weight, None, jnp.float32)
    blocks = [swap(block, "ctx", k) for k in range(1, half)]
    for k in range(1, half):
        dtype = jnp.float32 if k < half - 1 else jnp.bfloat16
        total = project(plan, k, blocks[k - 1], out_weight, total, dtype)
    return from_behind(total, "segment", 1)


def solution(mesh):
    in_specs = (
        P(("segment", "ctx"), None),
        P(("segment", "ctx"), None),
        P("segment", "ctx"),
        P("segment"),
        P("segment"),
    )
    out_specs = P("segment", "ctx")
    return jax.shard_map(
        per_device, mesh=mesh, in_specs=in_specs, out_specs=out_specs, check_vma=False
    )
```

```python
import functools
import math

import jax
import jax.numpy as jnp
from jax import lax
from jax.experimental import pallas as pl
from jax.experimental.pallas import tpu as pltpu
from jax.sharding import PartitionSpec as P

H = 64
KVH = 8
HD = 128
GROUP = H // KVH
LOG2_SCALE = HD ** (-0.5) * math.log2(math.e)
STEP = 8.0
FLOOR = -4096.0
HIDDEN = -1e30
STATS = 16
VMEM_LIMIT = 12 * 1024 * 1024


def swap(value, axis, bits):
    devices = lax.axis_size(axis)
    return lax.ppermute(value, axis, [(i, i ^ bits) for i in range(devices)])


def from_behind(value, axis, by):
    devices = lax.axis_size(axis)
    return lax.ppermute(value, axis, [(i, (i + by) % devices) for i in range(devices)])


class Plan:
    def __init__(self, ctx, rows_here):
        self.ctx = ctx
        self.half = ctx // 2
        self.across = self.half
        self.rows_here = rows_here
        self.rows = ctx * rows_here
        self.group_rows = GROUP * self.rows
        self.heads = H // self.half
        self.unit_heads = min(self.heads, GROUP)
        self.units = self.heads // self.unit_heads
        self.unit_rows = self.unit_heads * self.rows
        self.blocks = self.unit_rows // 128
        self.share_rows = self.units * self.unit_rows
        self.by_device = self.unit_heads == GROUP and GROUP * rows_here % 16 == 0

    def share(self, part):
        me = lax.axis_index("ctx")
        return (me % self.half) ^ part


def stat_rows(blocks):
    return -(-3 * blocks // 16) * 16


def local(kernel, out_shape, spaces, name, scratch=(), cost=None):
    return pl.pallas_call(
        kernel,
        out_shape=out_shape,
        in_specs=[pl.BlockSpec(memory_space=space) for space in spaces],
        out_specs=jax.tree.map(lambda _: pl.BlockSpec(memory_space=pltpu.VMEM), out_shape),
        scratch_shapes=list(scratch),
        compiler_params=pltpu.CompilerParams(vmem_limit_bytes=VMEM_LIMIT),
        cost_estimate=cost,
        name=name,
    )


def order_kernel(plan, order_ref, one_hot_ref):
    low = lax.axis_index("ctx") % plan.half
    high = lax.axis_index("ctx") // plan.half
    row = lax.broadcasted_iota(jnp.int32, (plan.group_rows, 128), 0)
    lane = lax.broadcasted_iota(jnp.int32, (plan.group_rows, 128), 1)
    query = lax.rem(row, plan.rows)
    device = lax.div(query, plan.rows_here)
    block = device
    if not plan.by_device:
        block = 2 * (lax.rem(device, plan.half) ^ low) + (lax.div(device, plan.half) ^ high)
    origin = (block * GROUP + lax.div(row, plan.rows)) * plan.rows_here + lax.rem(query, plan.rows_here)
    for at in range(0, plan.group_rows, 128):
        order_ref[:, at : at + 128] = jnp.where(lane + at == origin, 1.0, 0.0).astype(jnp.bfloat16)
    if plan.by_device:
        query = lax.div(row, GROUP * plan.rows_here) * plan.rows_here + lax.rem(row, plan.rows_here)
    one_hot_ref[...] = jnp.where(query == lane, 1.0, 0.0).astype(jnp.bfloat16)


def row_order(plan):
    return local(
        functools.partial(order_kernel, plan),
        [
            jax.ShapeDtypeStruct((plan.group_rows, plan.group_rows), jnp.bfloat16),
            jax.ShapeDtypeStruct((plan.group_rows, 128), jnp.bfloat16),
        ],
        [],
        "order",
        cost=pl.CostEstimate(flops=8_000_000_000, bytes_accessed=0, transcendentals=0),
    )()


def mask_kernel(offset_ref, start_ref, after_ref, bias_ref):
    del after_ref
    span = bias_ref.shape[0]
    position = lax.axis_index("ctx") * span + lax.broadcasted_iota(jnp.int32, (span, 128), 0)
    asked = lax.broadcasted_iota(jnp.int32, (span, 128), 1)
    shown = (position >= start_ref[0]) & (position <= offset_ref[0] + asked)
    bias_ref[...] = jnp.where(shown, 0.0, HIDDEN).astype(jnp.bfloat16)


def mask(span, offsets, starts, after):
    return local(
        mask_kernel,
        jax.ShapeDtypeStruct((span, 128), jnp.bfloat16),
        [pltpu.SMEM, pltpu.SMEM, pl.ANY],
        "mask",
        cost=pl.CostEstimate(flops=1_000_000, bytes_accessed=256 * span, transcendentals=0),
    )(offsets, starts, after)


def write_stats(ref, at, rows):
    values = []
    for peak, total in zip(rows[::2], rows[1::2]):
        high = total.astype(jnp.bfloat16).astype(jnp.float32)
        values += [peak, high, total - high]
    size = stat_rows(len(rows) // 2)
    index = lax.broadcasted_iota(jnp.int32, (size, 128), 0)
    table = jnp.zeros((size, 128), jnp.float32)
    for i, value in enumerate(values):
        table = jnp.where(index == i, value, table)
    ref[at : at + size, :] = table.astype(jnp.bfloat16)


def attend_kernel(plan, part, *refs):
    *refs, score_ref, held_ref = refs
    if part == 0:
        *refs, value_ref, stat_ref = refs
        stat_at = 0
    else:
        *refs, value_ref = refs
        stat_ref, stat_at = value_ref, plan.share_rows
    *query_refs, cache_ref, bias_ref, order_ref, one_hot_ref = refs
    span = cache_ref.shape[0]
    me = lax.axis_index("ctx")
    mine = plan.share(part)
    row_at = pl.multiple_of((mine * plan.heads) % GROUP * plan.rows, plan.unit_rows)
    order = order_ref[pl.ds(row_at, plan.unit_rows), :]
    one_hot = one_hot_ref[pl.ds(row_at, plan.unit_rows), :]
    ones = jnp.ones((span, HD), jnp.bfloat16)
    groups = [(mine * plan.heads + unit * plan.unit_heads) // GROUP for unit in range(plan.units)]
    peaks = []
    for unit, group in enumerate(groups):
        if plan.by_device:
            for block, ref in enumerate(query_refs):
                device = me ^ (block // 2) ^ (block % 2 * plan.half)
                to = pl.multiple_of(device * GROUP * plan.rows_here, GROUP * plan.rows_here)
                held_ref[unit, pl.ds(to, GROUP * plan.rows_here), :] = ref[group]
            queries = held_ref[unit]
        else:
            stacked = jnp.concatenate([ref[group] for ref in query_refs], axis=0)
            queries = jnp.dot(order, stacked, preferred_element_type=jnp.float32).astype(jnp.bfloat16)
        queries = jnp.concatenate([queries, one_hot], axis=1)
        key_at = pl.multiple_of(group * HD, HD)
        keys = jnp.concatenate([cache_ref[:, pl.ds(key_at, HD)], bias_ref[...]], axis=1)
        scores = lax.dot_general(queries, keys, (((1,), (1,)), ((), ())), preferred_element_type=jnp.float32)
        score_ref[unit] = scores
        peak = [scores[:, at : at + 128] for at in range(0, span, 128)]
        while len(peak) > 1:
            peak = [jnp.maximum(*peak[i : i + 2]) for i in range(0, len(peak) - 1, 2)] + (
                peak[-1:] if len(peak) % 2 else []
            )
        peak = jnp.max(peak[0], axis=1, keepdims=True) * LOG2_SCALE
        peak = jnp.maximum(jnp.ceil(peak * (1.0 / STEP)), FLOOR / STEP)
        peaks.append(jnp.broadcast_to(peak, (plan.unit_rows, 128)))
    same = lax.broadcasted_iota(jnp.int32, (128, 128), 0) == lax.broadcasted_iota(jnp.int32, (128, 128), 1)
    stats = []
    for unit, group in enumerate(groups):
        shift = jnp.concatenate([peaks[unit] * STEP] * (span // 128), axis=1)
        weights = jnp.exp2(score_ref[unit] * LOG2_SCALE - shift)
        value_at = pl.multiple_of((KVH + group) * HD, HD)
        values = jnp.concatenate([cache_ref[:, pl.ds(value_at, HD)], ones], axis=1)
        both = jnp.dot(weights.astype(jnp.bfloat16), values, preferred_element_type=jnp.float32)
        at = unit * plan.unit_rows
        value_ref[at : at + plan.unit_rows, :] = both[:, :HD].astype(value_ref.dtype)
        for block in range(0, plan.unit_rows, 128):
            for wide in (peaks[unit], both[:, HD:]):
                chosen = jnp.where(same, wide[block : block + 128, :], 0.0)
                stats.append(jnp.sum(chosen, axis=0, keepdims=True))
    write_stats(stat_ref, stat_at, stats)


def attend(plan, part, queries, cache, *tables):
    span = cache.shape[0]
    size = stat_rows(plan.units * plan.blocks)
    if part == 0:
        out_shape = [
            jax.ShapeDtypeStruct((plan.share_rows, HD), jnp.float32),
            jax.ShapeDtypeStruct((size, HD), jnp.bfloat16),
        ]
    else:
        out_shape = [jax.ShapeDtypeStruct((plan.share_rows + size, HD), jnp.bfloat16)]
    return local(
        functools.partial(attend_kernel, plan, part),
        out_shape,
        [pltpu.VMEM] * (len(queries) + 1 + len(tables)),
        "attend",
        [
            pltpu.VMEM((plan.units, plan.unit_rows, span), jnp.float32),
            pltpu.VMEM((plan.units, plan.unit_rows, HD), jnp.bfloat16),
        ],
        pl.CostEstimate(
            flops=4 * plan.share_rows * span * HD,
            bytes_accessed=2 * plan.units * span * HD * 2,
            transcendentals=plan.share_rows * span,
        ),
    )(*queries, cache, *tables)


def columns(rows):
    size = -(-len(rows) // 8) * 8
    index = lax.broadcasted_iota(jnp.int32, (size, 128), 0)
    table = jnp.zeros((size, 128), jnp.float32)
    for i, row in enumerate(rows):
        table = jnp.where(index == i, row, table)
    turned = jnp.transpose(jnp.concatenate([table, jnp.zeros((128 - size, 128), jnp.float32)], axis=0))
    return [turned[:, i : i + 1] for i in range(len(rows))]


def factors(stats, block):
    parts = []
    for ref, at in stats:
        base = 3 * block // 16 * 16
        tile = ref[at + base : at + min(base + 32, stat_rows(block + 1)), :].astype(jnp.float32)
        begin = 3 * block - base
        parts.append([tile[begin + i : begin + i + 1] for i in range(3)])
    joint = functools.reduce(jnp.maximum, [peak for peak, _, _ in parts])
    scale = [jnp.exp2((peak - joint) * STEP) for peak, _, _ in parts]
    total = functools.reduce(jnp.add, [f * (high + low) for f, (_, high, low) in zip(scale, parts)])
    return joint, scale, total


def mix(refs, at, scale):
    terms = [f * ref[at : at + 128, :].astype(jnp.float32) for ref, f in zip(refs, scale)]
    return functools.reduce(jnp.add, terms)


def merge_kernel(plan, wide_ref, stat_ref, *refs):
    *parts, out_ref, wide_out_ref = refs
    size = stat_rows(plan.units * plan.blocks)
    stats = [(stat_ref, stat_ref.shape[0] - size)] + [(ref, plan.share_rows) for ref in parts]
    rows, scales = [], []
    for block in range(plan.units * plan.blocks):
        joint, scale, total = factors(stats, block)
        rows += [joint, total]
        scales += scale
    scales = columns(scales)
    for block in range(plan.units * plan.blocks):
        at = block * 128
        mixed = mix([wide_ref] + parts, at, scales[block * len(stats) : (block + 1) * len(stats)])
        wide_out_ref[at : at + 128, :] = mixed
        out_ref[at : at + 128, :] = mixed.astype(jnp.bfloat16)
    write_stats(out_ref, plan.share_rows, rows)


def merge(plan, wide, stats, parts):
    rows = plan.share_rows + stat_rows(plan.units * plan.blocks)
    return local(
        functools.partial(merge_kernel, plan),
        [
            jax.ShapeDtypeStruct((rows, HD), jnp.bfloat16),
            jax.ShapeDtypeStruct((plan.share_rows, HD), jnp.float32),
        ],
        [pltpu.VMEM] * (len(parts) + 2),
        "merge",
    )(wide, stats, *parts)


def settle_kernel(plan, wide_ref, own_ref, other_ref, order_ref, out_ref):
    stats = [(own_ref, plan.share_rows), (other_ref, plan.share_rows)]
    scales = []
    for block in range(plan.units * plan.blocks):
        _, scale, total = factors(stats, block)
        scales += [f / total for f in scale]
    scales = columns(scales)
    done = []
    for block in range(plan.units * plan.blocks):
        mixed = mix([wide_ref, other_ref], block * 128, scales[2 * block : 2 * block + 2])
        done.append(mixed.astype(jnp.bfloat16))
    done = [done[unit * plan.blocks : (unit + 1) * plan.blocks] for unit in range(plan.units)]
    done = jnp.concatenate([jnp.concatenate(blocks, axis=0) for blocks in done], axis=1)
    if plan.by_device:
        done = jnp.dot(order_ref[...], done, preferred_element_type=jnp.float32).astype(jnp.bfloat16)
    for unit in range(plan.units):
        for head in range(plan.unit_heads):
            to = (unit * plan.unit_heads + head) * HD
            rows = slice(head * plan.rows, (head + 1) * plan.rows)
            out_ref[:, to : to + HD] = done[rows, unit * HD : (unit + 1) * HD]


def settle(plan, wide, own, other, order):
    return local(
        functools.partial(settle_kernel, plan),
        jax.ShapeDtypeStruct((plan.rows, plan.heads * HD), jnp.bfloat16),
        [pltpu.VMEM] * 4,
        "settle",
    )(wide, own, other, order)


def project_kernel(plan, part, *refs):
    block_ref, weight_ref, *before, out_ref = refs
    depth = plan.heads * HD
    at = pl.multiple_of(plan.share(part) * depth, depth)
    total = jnp.dot(block_ref[...], weight_ref[pl.ds(at, depth), :], preferred_element_type=jnp.float32)
    for ref in before:
        total = total + ref[...]
    out_ref[...] = total.astype(out_ref.dtype)


def project(plan, part, block, weight, before, dtype):
    operands = [block, weight] + ([] if before is None else [before])
    return local(
        functools.partial(project_kernel, plan, part),
        jax.ShapeDtypeStruct((plan.rows, weight.shape[1]), dtype),
        [pltpu.VMEM] * len(operands),
        "project",
    )(*operands)


def per_device(queries, cache, out_weight, offsets, starts):
    plan = Plan(lax.axis_size("ctx"), queries.shape[0])
    half = plan.half
    cache = pltpu.with_memory_space_constraint(cache, pltpu.VMEM)
    out_weight = pltpu.with_memory_space_constraint(out_weight, pltpu.VMEM)

    own = queries.reshape(plan.rows_here, KVH, GROUP, HD)
    own = own.transpose(1, 2, 0, 3).reshape(KVH, GROUP * plan.rows_here, HD)
    far = swap(own, "ctx", half)
    near = [swap(own, "ctx", k) for k in range(1, half)]
    order, one_hot = row_order(plan)
    bias = mask(cache.shape[0], offsets, starts, near[-1])
    if plan.by_device:
        gathered = [own, far]
        for k in range(1, half):
            gathered += [near[k - 1], swap(far, "ctx", k)]
    else:
        pair = jnp.concatenate([own, far], axis=1)
        gathered = [pair] + [swap(pair, "ctx", k) for k in range(1, half)]

    received = []
    for part in reversed(range(1, half)):
        (piece,) = attend(plan, part, gathered, cache, bias, order, one_hot)
        received.append(swap(piece, "ctx", part))
    wide, stats = attend(plan, 0, gathered, cache, bias, order, one_hot)

    near, wide = merge(plan, wide, stats, received[:-1])
    near, wide = merge(plan, wide, near, received[-1:])
    block = settle(plan, wide, near, swap(near, "ctx", plan.across), order)

    total = project(plan, 0, block, out_weight, None, jnp.float32)
    blocks = [swap(block, "ctx", k) for k in range(1, half)]
    for k in range(1, half):
        dtype = jnp.float32 if k < half - 1 else jnp.bfloat16
        total = project(plan, k, blocks[k - 1], out_weight, total, dtype)
    return from_behind(total, "segment", 1)


def solution(mesh):
    in_specs = (
        P(("segment", "ctx"), None),
        P(("segment", "ctx"), None),
        P("segment", "ctx"),
        P("segment"),
        P("segment"),
    )
    out_specs = P("segment", "ctx")
    return jax.shard_map(
        per_device, mesh=mesh, in_specs=in_specs, out_specs=out_specs, check_vma=False
    )
```

```python
import functools
import math

import jax
import jax.numpy as jnp
from jax import lax
from jax.experimental import pallas as pl
from jax.experimental.pallas import tpu as pltpu
from jax.sharding import PartitionSpec as P

H = 64
KVH = 8
HD = 128
GROUP = H // KVH
LOG2_SCALE = HD ** (-0.5) * math.log2(math.e)
STEP = 8.0
FLOOR = -4096.0
HIDDEN = -1e30
STATS = 16
VMEM_LIMIT = 12 * 1024 * 1024


def swap(value, axis, bits):
    devices = lax.axis_size(axis)
    return lax.ppermute(value, axis, [(i, i ^ bits) for i in range(devices)])


def from_behind(value, axis, by):
    devices = lax.axis_size(axis)
    return lax.ppermute(value, axis, [(i, (i + by) % devices) for i in range(devices)])


class Plan:
    def __init__(self, ctx, rows_here):
        self.ctx = ctx
        self.half = ctx // 2
        self.fold = self.half // 2
        self.across = self.half | self.fold
        self.rows_here = rows_here
        self.rows = ctx * rows_here
        self.group_rows = GROUP * self.rows
        self.heads = H // self.half
        self.unit_heads = min(self.heads, GROUP)
        self.units = self.heads // self.unit_heads
        self.unit_rows = self.unit_heads * self.rows
        self.blocks = self.unit_rows // 128
        self.share_rows = self.units * self.unit_rows
        self.by_device = self.unit_heads == GROUP and GROUP * rows_here % 16 == 0

    def share(self, part):
        me = lax.axis_index("ctx")
        return (me % self.half) ^ (me // self.half * self.fold) ^ part


def stat_rows(blocks):
    return -(-3 * blocks // 16) * 16


def local(kernel, out_shape, spaces, name, scratch=(), cost=None):
    return pl.pallas_call(
        kernel,
        out_shape=out_shape,
        in_specs=[pl.BlockSpec(memory_space=space) for space in spaces],
        out_specs=jax.tree.map(lambda _: pl.BlockSpec(memory_space=pltpu.VMEM), out_shape),
        scratch_shapes=list(scratch),
        compiler_params=pltpu.CompilerParams(vmem_limit_bytes=VMEM_LIMIT),
        cost_estimate=cost,
        name=name,
    )


def order_kernel(plan, order_ref, one_hot_ref):
    low = lax.axis_index("ctx") % plan.half
    high = lax.axis_index("ctx") // plan.half
    row = lax.broadcasted_iota(jnp.int32, (plan.group_rows, 128), 0)
    lane = lax.broadcasted_iota(jnp.int32, (plan.group_rows, 128), 1)
    query = lax.rem(row, plan.rows)
    device = lax.div(query, plan.rows_here)
    block = device
    if not plan.by_device:
        block = 2 * (lax.rem(device, plan.half) ^ low) + (lax.div(device, plan.half) ^ high)
    origin = (block * GROUP + lax.div(row, plan.rows)) * plan.rows_here + lax.rem(query, plan.rows_here)
    for at in range(0, plan.group_rows, 128):
        order_ref[:, at : at + 128] = jnp.where(lane + at == origin, 1.0, 0.0).astype(jnp.bfloat16)
    if plan.by_device:
        query = lax.div(row, GROUP * plan.rows_here) * plan.rows_here + lax.rem(row, plan.rows_here)
    one_hot_ref[...] = jnp.where(query == lane, 1.0, 0.0).astype(jnp.bfloat16)


def row_order(plan):
    return local(
        functools.partial(order_kernel, plan),
        [
            jax.ShapeDtypeStruct((plan.group_rows, plan.group_rows), jnp.bfloat16),
            jax.ShapeDtypeStruct((plan.group_rows, 128), jnp.bfloat16),
        ],
        [],
        "order",
        cost=pl.CostEstimate(flops=8_000_000_000, bytes_accessed=0, transcendentals=0),
    )()


def mask_kernel(offset_ref, start_ref, after_ref, bias_ref):
    del after_ref
    span = bias_ref.shape[0]
    position = lax.axis_index("ctx") * span + lax.broadcasted_iota(jnp.int32, (span, 128), 0)
    asked = lax.broadcasted_iota(jnp.int32, (span, 128), 1)
    shown = (position >= start_ref[0]) & (position <= offset_ref[0] + asked)
    bias_ref[...] = jnp.where(shown, 0.0, HIDDEN).astype(jnp.bfloat16)


def mask(span, offsets, starts, after):
    return local(
        mask_kernel,
        jax.ShapeDtypeStruct((span, 128), jnp.bfloat16),
        [pltpu.SMEM, pltpu.SMEM, pl.ANY],
        "mask",
        cost=pl.CostEstimate(flops=1_000_000, bytes_accessed=256 * span, transcendentals=0),
    )(offsets, starts, after)


def write_stats(ref, at, rows):
    values = []
    for peak, total in zip(rows[::2], rows[1::2]):
        high = total.astype(jnp.bfloat16).astype(jnp.float32)
        values += [peak, high, total - high]
    size = stat_rows(len(rows) // 2)
    index = lax.broadcasted_iota(jnp.int32, (size, 128), 0)
    table = jnp.zeros((size, 128), jnp.float32)
    for i, value in enumerate(values):
        table = jnp.where(index == i, value, table)
    ref[at : at + size, :] = table.astype(jnp.bfloat16)


def attend_kernel(plan, part, *refs):
    *refs, score_ref, held_ref = refs
    if part == 0:
        *refs, value_ref, stat_ref = refs
        stat_at = 0
    else:
        *refs, value_ref = refs
        stat_ref, stat_at = value_ref, plan.share_rows
    *query_refs, cache_ref, bias_ref, order_ref, one_hot_ref = refs
    span = cache_ref.shape[0]
    me = lax.axis_index("ctx")
    mine = plan.share(part)
    row_at = pl.multiple_of((mine * plan.heads) % GROUP * plan.rows, plan.unit_rows)
    order = order_ref[pl.ds(row_at, plan.unit_rows), :]
    one_hot = one_hot_ref[pl.ds(row_at, plan.unit_rows), :]
    ones = jnp.ones((span, HD), jnp.bfloat16)
    groups = [(mine * plan.heads + unit * plan.unit_heads) // GROUP for unit in range(plan.units)]
    peaks = []
    for unit, group in enumerate(groups):
        if plan.by_device:
            for block, ref in enumerate(query_refs):
                device = me ^ (block // 2) ^ (block % 2 * plan.half)
                to = pl.multiple_of(device * GROUP * plan.rows_here, GROUP * plan.rows_here)
                held_ref[unit, pl.ds(to, GROUP * plan.rows_here), :] = ref[group]
            queries = held_ref[unit]
        else:
            stacked = jnp.concatenate([ref[group] for ref in query_refs], axis=0)
            queries = jnp.dot(order, stacked, preferred_element_type=jnp.float32).astype(jnp.bfloat16)
        queries = jnp.concatenate([queries, one_hot], axis=1)
        key_at = pl.multiple_of(group * HD, HD)
        keys = jnp.concatenate([cache_ref[:, pl.ds(key_at, HD)], bias_ref[...]], axis=1)
        scores = lax.dot_general(queries, keys, (((1,), (1,)), ((), ())), preferred_element_type=jnp.float32)
        score_ref[unit] = scores
        peak = [scores[:, at : at + 128] for at in range(0, span, 128)]
        while len(peak) > 1:
            peak = [jnp.maximum(*peak[i : i + 2]) for i in range(0, len(peak) - 1, 2)] + (
                peak[-1:] if len(peak) % 2 else []
            )
        peak = jnp.max(peak[0], axis=1, keepdims=True) * LOG2_SCALE
        peak = jnp.maximum(jnp.ceil(peak * (1.0 / STEP)), FLOOR / STEP)
        peaks.append(jnp.broadcast_to(peak, (plan.unit_rows, 128)))
    same = lax.broadcasted_iota(jnp.int32, (128, 128), 0) == lax.broadcasted_iota(jnp.int32, (128, 128), 1)
    stats = []
    for unit, group in enumerate(groups):
        shift = jnp.concatenate([peaks[unit] * STEP] * (span // 128), axis=1)
        weights = jnp.exp2(score_ref[unit] * LOG2_SCALE - shift)
        value_at = pl.multiple_of((KVH + group) * HD, HD)
        values = jnp.concatenate([cache_ref[:, pl.ds(value_at, HD)], ones], axis=1)
        both = jnp.dot(weights.astype(jnp.bfloat16), values, preferred_element_type=jnp.float32)
        at = unit * plan.unit_rows
        value_ref[at : at + plan.unit_rows, :] = both[:, :HD].astype(value_ref.dtype)
        for block in range(0, plan.unit_rows, 128):
            for wide in (peaks[unit], both[:, HD:]):
                chosen = jnp.where(same, wide[block : block + 128, :], 0.0)
                stats.append(jnp.sum(chosen, axis=0, keepdims=True))
    write_stats(stat_ref, stat_at, stats)


def attend(plan, part, queries, cache, *tables):
    span = cache.shape[0]
    size = stat_rows(plan.units * plan.blocks)
    if part == 0:
        out_shape = [
            jax.ShapeDtypeStruct((plan.share_rows, HD), jnp.float32),
            jax.ShapeDtypeStruct((size, HD), jnp.bfloat16),
        ]
    else:
        out_shape = [jax.ShapeDtypeStruct((plan.share_rows + size, HD), jnp.bfloat16)]
    return local(
        functools.partial(attend_kernel, plan, part),
        out_shape,
        [pltpu.VMEM] * (len(queries) + 1 + len(tables)),
        "attend",
        [
            pltpu.VMEM((plan.units, plan.unit_rows, span), jnp.float32),
            pltpu.VMEM((plan.units, plan.unit_rows, HD), jnp.bfloat16),
        ],
        pl.CostEstimate(
            flops=4 * plan.share_rows * span * HD,
            bytes_accessed=2 * plan.units * span * HD * 2,
            transcendentals=plan.share_rows * span,
        ),
    )(*queries, cache, *tables)


def columns(rows):
    size = -(-len(rows) // 8) * 8
    index = lax.broadcasted_iota(jnp.int32, (size, 128), 0)
    table = jnp.zeros((size, 128), jnp.float32)
    for i, row in enumerate(rows):
        table = jnp.where(index == i, row, table)
    turned = jnp.transpose(jnp.concatenate([table, jnp.zeros((128 - size, 128), jnp.float32)], axis=0))
    return [turned[:, i : i + 1] for i in range(len(rows))]


def factors(stats, block):
    parts = []
    for ref, at in stats:
        base = 3 * block // 16 * 16
        tile = ref[at + base : at + min(base + 32, stat_rows(block + 1)), :].astype(jnp.float32)
        begin = 3 * block - base
        parts.append([tile[begin + i : begin + i + 1] for i in range(3)])
    joint = functools.reduce(jnp.maximum, [peak for peak, _, _ in parts])
    scale = [jnp.exp2((peak - joint) * STEP) for peak, _, _ in parts]
    total = functools.reduce(jnp.add, [f * (high + low) for f, (_, high, low) in zip(scale, parts)])
    return joint, scale, total


def mix(refs, at, scale):
    terms = [f * ref[at : at + 128, :].astype(jnp.float32) for ref, f in zip(refs, scale)]
    return functools.reduce(jnp.add, terms)


def merge_kernel(plan, wide_ref, stat_ref, *refs):
    *parts, out_ref, wide_out_ref = refs
    size = stat_rows(plan.units * plan.blocks)
    stats = [(stat_ref, stat_ref.shape[0] - size)] + [(ref, plan.share_rows) for ref in parts]
    rows, scales = [], []
    for block in range(plan.units * plan.blocks):
        joint, scale, total = factors(stats, block)
        rows += [joint, total]
        scales += scale
    scales = columns(scales)
    for block in range(plan.units * plan.blocks):
        at = block * 128
        mixed = mix([wide_ref] + parts, at, scales[block * len(stats) : (block + 1) * len(stats)])
        wide_out_ref[at : at + 128, :] = mixed
        out_ref[at : at + 128, :] = mixed.astype(jnp.bfloat16)
    write_stats(out_ref, plan.share_rows, rows)


def merge(plan, wide, stats, parts):
    rows = plan.share_rows + stat_rows(plan.units * plan.blocks)
    return local(
        functools.partial(merge_kernel, plan),
        [
            jax.ShapeDtypeStruct((rows, HD), jnp.bfloat16),
            jax.ShapeDtypeStruct((plan.share_rows, HD), jnp.float32),
        ],
        [pltpu.VMEM] * (len(parts) + 2),
        "merge",
    )(wide, stats, *parts)


def settle_kernel(plan, wide_ref, own_ref, other_ref, order_ref, out_ref):
    stats = [(own_ref, plan.share_rows), (other_ref, plan.share_rows)]
    scales = []
    for block in range(plan.units * plan.blocks):
        _, scale, total = factors(stats, block)
        scales += [f / total for f in scale]
    scales = columns(scales)
    done = []
    for block in range(plan.units * plan.blocks):
        mixed = mix([wide_ref, other_ref], block * 128, scales[2 * block : 2 * block + 2])
        done.append(mixed.astype(jnp.bfloat16))
    done = [done[unit * plan.blocks : (unit + 1) * plan.blocks] for unit in range(plan.units)]
    done = jnp.concatenate([jnp.concatenate(blocks, axis=0) for blocks in done], axis=1)
    if plan.by_device:
        done = jnp.dot(order_ref[...], done, preferred_element_type=jnp.float32).astype(jnp.bfloat16)
    for unit in range(plan.units):
        for head in range(plan.unit_heads):
            to = (unit * plan.unit_heads + head) * HD
            rows = slice(head * plan.rows, (head + 1) * plan.rows)
            out_ref[:, to : to + HD] = done[rows, unit * HD : (unit + 1) * HD]


def settle(plan, wide, own, other, order):
    return local(
        functools.partial(settle_kernel, plan),
        jax.ShapeDtypeStruct((plan.rows, plan.heads * HD), jnp.bfloat16),
        [pltpu.VMEM] * 4,
        "settle",
    )(wide, own, other, order)


def project_kernel(plan, part, *refs):
    block_ref, weight_ref, *before, out_ref = refs
    depth = plan.heads * HD
    at = pl.multiple_of(plan.share(part) * depth, depth)
    total = jnp.dot(block_ref[...], weight_ref[pl.ds(at, depth), :], preferred_element_type=jnp.float32)
    for ref in before:
        total = total + ref[...]
    out_ref[...] = total.astype(out_ref.dtype)


def project(plan, part, block, weight, before, dtype):
    operands = [block, weight] + ([] if before is None else [before])
    return local(
        functools.partial(project_kernel, plan, part),
        jax.ShapeDtypeStruct((plan.rows, weight.shape[1]), dtype),
        [pltpu.VMEM] * len(operands),
        "project",
    )(*operands)


def per_device(queries, cache, out_weight, offsets, starts):
    plan = Plan(lax.axis_size("ctx"), queries.shape[0])
    half = plan.half
    cache = pltpu.with_memory_space_constraint(cache, pltpu.VMEM)
    out_weight = pltpu.with_memory_space_constraint(out_weight, pltpu.VMEM)

    own = queries.reshape(plan.rows_here, KVH, GROUP, HD)
    own = own.transpose(1, 2, 0, 3).reshape(KVH, GROUP * plan.rows_here, HD)
    far = swap(own, "ctx", half)
    near = [swap(own, "ctx", k) for k in range(1, half)]
    order, one_hot = row_order(plan)
    bias = mask(cache.shape[0], offsets, starts, near[-1])
    if plan.by_device:
        gathered = [own, far]
        for k in range(1, half):
            gathered += [near[k - 1], swap(far, "ctx", k)]
    else:
        pair = jnp.concatenate([own, far], axis=1)
        gathered = [pair] + [swap(pair, "ctx", k) for k in range(1, half)]

    received = []
    for part in reversed(range(1, half)):
        (piece,) = attend(plan, part, gathered, cache, bias, order, one_hot)
        received.append(swap(piece, "ctx", part))
    wide, stats = attend(plan, 0, gathered, cache, bias, order, one_hot)

    near, wide = merge(plan, wide, stats, received[:-1])
    near, wide = merge(plan, wide, near, received[-1:])
    block = settle(plan, wide, near, swap(near, "ctx", plan.across), order)

    total = project(plan, 0, block, out_weight, None, jnp.float32)
    for k in reversed(range(1, half)):
        dtype = jnp.float32 if k > 1 else jnp.bfloat16
        total = project(plan, k, swap(block, "ctx", k), out_weight, total, dtype)
    return from_behind(total, "segment", 1)


def solution(mesh):
    in_specs = (
        P(("segment", "ctx"), None),
        P(("segment", "ctx"), None),
        P("segment", "ctx"),
        P("segment"),
        P("segment"),
    )
    out_specs = P("segment", "ctx")
    return jax.shard_map(
        per_device, mesh=mesh, in_specs=in_specs, out_specs=out_specs, check_vma=False
    )
```

```python
import functools
import math

import jax
import jax.numpy as jnp
from jax import lax
from jax.experimental import pallas as pl
from jax.experimental.pallas import tpu as pltpu
from jax.sharding import PartitionSpec as P

H = 64
KVH = 8
HD = 128
GROUP = H // KVH
LOG2_SCALE = HD ** (-0.5) * math.log2(math.e)
STEP = 8.0
FLOOR = -4096.0
HIDDEN = -1e30
STATS = 16
VMEM_LIMIT = 12 * 1024 * 1024


def swap(value, axis, bits):
    devices = lax.axis_size(axis)
    return lax.ppermute(value, axis, [(i, i ^ bits) for i in range(devices)])


def from_behind(value, axis, by):
    devices = lax.axis_size(axis)
    return lax.ppermute(value, axis, [(i, (i + by) % devices) for i in range(devices)])


class Plan:
    def __init__(self, ctx, rows_here):
        self.ctx = ctx
        self.half = ctx // 2
        self.fold = self.half // 2
        self.across = self.half | self.fold
        self.rows_here = rows_here
        self.rows = ctx * rows_here
        self.group_rows = GROUP * self.rows
        self.heads = H // self.half
        self.unit_heads = min(self.heads, GROUP)
        self.units = self.heads // self.unit_heads
        self.unit_rows = self.unit_heads * self.rows
        self.blocks = self.unit_rows // 128
        self.share_rows = self.units * self.unit_rows
        self.by_device = self.unit_heads == GROUP and GROUP * rows_here % 16 == 0

    def share(self, part):
        me = lax.axis_index("ctx")
        return (me % self.half) ^ (me // self.half * self.fold) ^ part


def stat_rows(blocks):
    return -(-3 * blocks // 16) * 16


def local(kernel, out_shape, spaces, name, scratch=(), cost=None):
    return pl.pallas_call(
        kernel,
        out_shape=out_shape,
        in_specs=[pl.BlockSpec(memory_space=space) for space in spaces],
        out_specs=jax.tree.map(lambda _: pl.BlockSpec(memory_space=pltpu.VMEM), out_shape),
        scratch_shapes=list(scratch),
        compiler_params=pltpu.CompilerParams(vmem_limit_bytes=VMEM_LIMIT),
        cost_estimate=cost,
        name=name,
    )


def order_kernel(plan, order_ref, one_hot_ref):
    low = lax.axis_index("ctx") % plan.half
    high = lax.axis_index("ctx") // plan.half
    row = lax.broadcasted_iota(jnp.int32, (plan.group_rows, 128), 0)
    lane = lax.broadcasted_iota(jnp.int32, (plan.group_rows, 128), 1)
    query = lax.rem(row, plan.rows)
    device = lax.div(query, plan.rows_here)
    block = device
    if not plan.by_device:
        block = 2 * (lax.rem(device, plan.half) ^ low) + (lax.div(device, plan.half) ^ high)
    origin = (block * GROUP + lax.div(row, plan.rows)) * plan.rows_here + lax.rem(query, plan.rows_here)
    for at in range(0, plan.group_rows, 128):
        order_ref[:, at : at + 128] = jnp.where(lane + at == origin, 1.0, 0.0).astype(jnp.bfloat16)
    if plan.by_device:
        query = lax.div(row, GROUP * plan.rows_here) * plan.rows_here + lax.rem(row, plan.rows_here)
    one_hot_ref[...] = jnp.where(query == lane, 1.0, 0.0).astype(jnp.bfloat16)


def row_order(plan):
    return local(
        functools.partial(order_kernel, plan),
        [
            jax.ShapeDtypeStruct((plan.group_rows, plan.group_rows), jnp.bfloat16),
            jax.ShapeDtypeStruct((plan.group_rows, 128), jnp.bfloat16),
        ],
        [],
        "order",
        cost=pl.CostEstimate(flops=8_000_000_000, bytes_accessed=0, transcendentals=0),
    )()


def mask_kernel(offset_ref, start_ref, after_ref, bias_ref):
    del after_ref
    span = bias_ref.shape[0]
    position = lax.axis_index("ctx") * span + lax.broadcasted_iota(jnp.int32, (span, 128), 0)
    asked = lax.broadcasted_iota(jnp.int32, (span, 128), 1)
    shown = (position >= start_ref[0]) & (position <= offset_ref[0] + asked)
    bias_ref[...] = jnp.where(shown, 0.0, HIDDEN).astype(jnp.bfloat16)


def mask(span, offsets, starts, after):
    return local(
        mask_kernel,
        jax.ShapeDtypeStruct((span, 128), jnp.bfloat16),
        [pltpu.SMEM, pltpu.SMEM, pl.ANY],
        "mask",
        cost=pl.CostEstimate(flops=1_000_000, bytes_accessed=256 * span, transcendentals=0),
    )(offsets, starts, after)


def write_stats(ref, at, rows):
    values = []
    for peak, total in zip(rows[::2], rows[1::2]):
        high = total.astype(jnp.bfloat16).astype(jnp.float32)
        values += [peak, high, total - high]
    size = stat_rows(len(rows) // 2)
    index = lax.broadcasted_iota(jnp.int32, (size, 128), 0)
    table = jnp.zeros((size, 128), jnp.float32)
    for i, value in enumerate(values):
        table = jnp.where(index == i, value, table)
    ref[at : at + size, :] = table.astype(jnp.bfloat16)


def attend_kernel(plan, part, given, onward, *refs):
    *refs, score_ref, held_ref = refs
    if onward is not None:
        *refs, next_score_ref, next_peak_ref = refs
    if part == 0:
        *refs, value_ref, stat_ref = refs
        stat_at = 0
    else:
        *refs, value_ref = refs
        stat_ref, stat_at = value_ref, plan.share_rows
    if given:
        *refs, given_score_ref, given_peak_ref = refs
    *query_refs, cache_ref, bias_ref, order_ref, one_hot_ref = refs
    span = cache_ref.shape[0]
    me = lax.axis_index("ctx")
    ones = jnp.ones((span, HD), jnp.bfloat16)

    def group_of(share, unit):
        return (share * plan.heads + unit * plan.unit_heads) // GROUP

    def first(share, unit, slot, to_ref):
        group = group_of(share, unit)
        row_at = pl.multiple_of((share * plan.heads) % GROUP * plan.rows, plan.unit_rows)
        if plan.by_device:
            for block, ref in enumerate(query_refs):
                device = me ^ (block // 2) ^ (block % 2 * plan.half)
                to = pl.multiple_of(device * GROUP * plan.rows_here, GROUP * plan.rows_here)
                held_ref[slot, pl.ds(to, GROUP * plan.rows_here), :] = ref[group]
            queries = held_ref[slot]
        else:
            stacked = jnp.concatenate([ref[group] for ref in query_refs], axis=0)
            order = order_ref[pl.ds(row_at, plan.unit_rows), :]
            queries = jnp.dot(order, stacked, preferred_element_type=jnp.float32).astype(jnp.bfloat16)
        queries = jnp.concatenate([queries, one_hot_ref[pl.ds(row_at, plan.unit_rows), :]], axis=1)
        key_at = pl.multiple_of(group * HD, HD)
        keys = jnp.concatenate([cache_ref[:, pl.ds(key_at, HD)], bias_ref[...]], axis=1)
        scores = lax.dot_general(queries, keys, (((1,), (1,)), ((), ())), preferred_element_type=jnp.float32)
        to_ref[...] = scores
        peak = [scores[:, at : at + 128] for at in range(0, span, 128)]
        while len(peak) > 1:
            peak = [jnp.maximum(*peak[i : i + 2]) for i in range(0, len(peak) - 1, 2)] + (
                peak[-1:] if len(peak) % 2 else []
            )
        peak = jnp.max(peak[0], axis=1, keepdims=True) * LOG2_SCALE
        peak = jnp.maximum(jnp.ceil(peak * (1.0 / STEP)), FLOOR / STEP)
        return jnp.broadcast_to(peak, (plan.unit_rows, 128))

    mine = plan.share(part)
    scores, peaks = [], []
    for unit in range(plan.units):
        if unit == 0 and given:
            scores.append(given_score_ref)
            peaks.append(given_peak_ref[...])
        else:
            scores.append(score_ref.at[unit])
            peaks.append(first(mine, unit, unit, score_ref.at[unit]))
    same = lax.broadcasted_iota(jnp.int32, (128, 128), 0) == lax.broadcasted_iota(jnp.int32, (128, 128), 1)
    stats = []
    for unit in range(plan.units):
        if unit == plan.units - 1 and onward is not None:
            next_peak_ref[...] = first(plan.share(onward), 0, plan.units, next_score_ref)
        shift = jnp.concatenate([peaks[unit] * STEP] * (span // 128), axis=1)
        weights = jnp.exp2(scores[unit][...] * LOG2_SCALE - shift)
        value_at = pl.multiple_of((KVH + group_of(mine, unit)) * HD, HD)
        values = jnp.concatenate([cache_ref[:, pl.ds(value_at, HD)], ones], axis=1)
        both = jnp.dot(weights.astype(jnp.bfloat16), values, preferred_element_type=jnp.float32)
        at = unit * plan.unit_rows
        value_ref[at : at + plan.unit_rows, :] = both[:, :HD].astype(value_ref.dtype)
        for block in range(0, plan.unit_rows, 128):
            for wide in (peaks[unit], both[:, HD:]):
                chosen = jnp.where(same, wide[block : block + 128, :], 0.0)
                stats.append(jnp.sum(chosen, axis=0, keepdims=True))
    write_stats(stat_ref, stat_at, stats)


def attend(plan, part, onward, queries, cache, tables, given):
    span = cache.shape[0]
    size = stat_rows(plan.units * plan.blocks)
    if part == 0:
        out_shape = [
            jax.ShapeDtypeStruct((plan.share_rows, HD), jnp.float32),
            jax.ShapeDtypeStruct((size, HD), jnp.bfloat16),
        ]
    else:
        out_shape = [jax.ShapeDtypeStruct((plan.share_rows + size, HD), jnp.bfloat16)]
    if onward is not None:
        out_shape += [
            pltpu.VMEM((plan.unit_rows, span), jnp.float32),
            pltpu.VMEM((plan.unit_rows, 128), jnp.float32),
        ]
    given = [pltpu.with_memory_space_constraint(value, pltpu.VMEM) for value in given]
    return local(
        functools.partial(attend_kernel, plan, part, bool(given), onward),
        out_shape,
        [pltpu.VMEM] * (len(queries) + 1 + len(tables) + len(given)),
        "attend",
        [
            pltpu.VMEM((plan.units, plan.unit_rows, span), jnp.float32),
            pltpu.VMEM((plan.units + 1, plan.unit_rows, HD), jnp.bfloat16),
        ],
        pl.CostEstimate(
            flops=4 * plan.share_rows * span * HD,
            bytes_accessed=2 * plan.units * span * HD * 2,
            transcendentals=plan.share_rows * span,
        ),
    )(*queries, cache, *tables, *given)


def columns(rows):
    size = -(-len(rows) // 8) * 8
    index = lax.broadcasted_iota(jnp.int32, (size, 128), 0)
    table = jnp.zeros((size, 128), jnp.float32)
    for i, row in enumerate(rows):
        table = jnp.where(index == i, row, table)
    turned = jnp.transpose(jnp.concatenate([table, jnp.zeros((128 - size, 128), jnp.float32)], axis=0))
    return [turned[:, i : i + 1] for i in range(len(rows))]


def factors(stats, block):
    parts = []
    for ref, at in stats:
        base = 3 * block // 16 * 16
        tile = ref[at + base : at + min(base + 32, stat_rows(block + 1)), :].astype(jnp.float32)
        begin = 3 * block - base
        parts.append([tile[begin + i : begin + i + 1] for i in range(3)])
    joint = functools.reduce(jnp.maximum, [peak for peak, _, _ in parts])
    scale = [jnp.exp2((peak - joint) * STEP) for peak, _, _ in parts]
    total = functools.reduce(jnp.add, [f * (high + low) for f, (_, high, low) in zip(scale, parts)])
    return joint, scale, total


def mix(refs, at, scale):
    terms = [f * ref[at : at + 128, :].astype(jnp.float32) for ref, f in zip(refs, scale)]
    return functools.reduce(jnp.add, terms)


def merge_kernel(plan, wide_ref, stat_ref, *refs):
    *parts, out_ref, wide_out_ref = refs
    size = stat_rows(plan.units * plan.blocks)
    stats = [(stat_ref, stat_ref.shape[0] - size)] + [(ref, plan.share_rows) for ref in parts]
    rows, scales = [], []
    for block in range(plan.units * plan.blocks):
        joint, scale, total = factors(stats, block)
        rows += [joint, total]
        scales += scale
    scales = columns(scales)
    for block in range(plan.units * plan.blocks):
        at = block * 128
        mixed = mix([wide_ref] + parts, at, scales[block * len(stats) : (block + 1) * len(stats)])
        wide_out_ref[at : at + 128, :] = mixed
        out_ref[at : at + 128, :] = mixed.astype(jnp.bfloat16)
    write_stats(out_ref, plan.share_rows, rows)


def merge(plan, wide, stats, parts):
    rows = plan.share_rows + stat_rows(plan.units * plan.blocks)
    return local(
        functools.partial(merge_kernel, plan),
        [
            jax.ShapeDtypeStruct((rows, HD), jnp.bfloat16),
            jax.ShapeDtypeStruct((plan.share_rows, HD), jnp.float32),
        ],
        [pltpu.VMEM] * (len(parts) + 2),
        "merge",
    )(wide, stats, *parts)


def settle_kernel(plan, wide_ref, own_ref, other_ref, order_ref, out_ref):
    stats = [(own_ref, plan.share_rows), (other_ref, plan.share_rows)]
    scales = []
    for block in range(plan.units * plan.blocks):
        _, scale, total = factors(stats, block)
        scales += [f / total for f in scale]
    scales = columns(scales)
    done = []
    for block in range(plan.units * plan.blocks):
        mixed = mix([wide_ref, other_ref], block * 128, scales[2 * block : 2 * block + 2])
        done.append(mixed.astype(jnp.bfloat16))
    done = [done[unit * plan.blocks : (unit + 1) * plan.blocks] for unit in range(plan.units)]
    done = jnp.concatenate([jnp.concatenate(blocks, axis=0) for blocks in done], axis=1)
    if plan.by_device:
        done = jnp.dot(order_ref[...], done, preferred_element_type=jnp.float32).astype(jnp.bfloat16)
    for unit in range(plan.units):
        for head in range(plan.unit_heads):
            to = (unit * plan.unit_heads + head) * HD
            rows = slice(head * plan.rows, (head + 1) * plan.rows)
            out_ref[:, to : to + HD] = done[rows, unit * HD : (unit + 1) * HD]


def settle(plan, wide, own, other, order):
    return local(
        functools.partial(settle_kernel, plan),
        jax.ShapeDtypeStruct((plan.rows, plan.heads * HD), jnp.bfloat16),
        [pltpu.VMEM] * 4,
        "settle",
    )(wide, own, other, order)


def project_kernel(plan, part, *refs):
    block_ref, weight_ref, *before, out_ref = refs
    depth = plan.heads * HD
    at = pl.multiple_of(plan.share(part) * depth, depth)
    total = jnp.dot(block_ref[...], weight_ref[pl.ds(at, depth), :], preferred_element_type=jnp.float32)
    for ref in before:
        total = total + ref[...]
    out_ref[...] = total.astype(out_ref.dtype)


def project(plan, part, block, weight, before, dtype):
    operands = [block, weight] + ([] if before is None else [before])
    return local(
        functools.partial(project_kernel, plan, part),
        jax.ShapeDtypeStruct((plan.rows, weight.shape[1]), dtype),
        [pltpu.VMEM] * len(operands),
        "project",
    )(*operands)


def per_device(queries, cache, out_weight, offsets, starts):
    plan = Plan(lax.axis_size("ctx"), queries.shape[0])
    half = plan.half
    cache = pltpu.with_memory_space_constraint(cache, pltpu.VMEM)
    out_weight = pltpu.with_memory_space_constraint(out_weight, pltpu.VMEM)

    own = queries.reshape(plan.rows_here, KVH, GROUP, HD)
    own = own.transpose(1, 2, 0, 3).reshape(KVH, GROUP * plan.rows_here, HD)
    far = swap(own, "ctx", half)
    near = [swap(own, "ctx", k) for k in range(1, half)]
    order, one_hot = row_order(plan)
    bias = mask(cache.shape[0], offsets, starts, near[-1])
    if plan.by_device:
        gathered = [own, far]
        for k in range(1, half):
            gathered += [near[k - 1], swap(far, "ctx", k)]
    else:
        pair = jnp.concatenate([own, far], axis=1)
        gathered = [pair] + [swap(pair, "ctx", k) for k in range(1, half)]

    received, given = [], []
    for part in reversed(range(1, half)):
        piece, *given = attend(plan, part, part - 1, gathered, cache, (bias, order, one_hot), given)
        received.append(swap(piece, "ctx", part))
    wide, stats = attend(plan, 0, None, gathered, cache, (bias, order, one_hot), given)

    near, wide = merge(plan, wide, stats, received[:-1])
    near, wide = merge(plan, wide, near, received[-1:])
    block = settle(plan, wide, near, swap(near, "ctx", plan.across), order)

    total = project(plan, 0, block, out_weight, None, jnp.float32)
    blocks = [swap(block, "ctx", k) for k in range(1, half)]
    for k in range(1, half):
        dtype = jnp.float32 if k < half - 1 else jnp.bfloat16
        total = project(plan, k, blocks[k - 1], out_weight, total, dtype)
    return from_behind(total, "segment", 1)


def solution(mesh):
    in_specs = (
        P(("segment", "ctx"), None),
        P(("segment", "ctx"), None),
        P("segment", "ctx"),
        P("segment"),
        P("segment"),
    )
    out_specs = P("segment", "ctx")
    return jax.shard_map(
        per_device, mesh=mesh, in_specs=in_specs, out_specs=out_specs, check_vma=False
    )
```

```python
import functools
import math

import jax
import jax.numpy as jnp
from jax import lax
from jax.experimental import pallas as pl
from jax.experimental.pallas import tpu as pltpu
from jax.sharding import PartitionSpec as P

H = 64
KVH = 8
HD = 128
GROUP = H // KVH
LOG2_SCALE = HD ** (-0.5) * math.log2(math.e)
STEP = 8.0
FLOOR = -4096.0
HIDDEN = -1e30
STATS = 16
VMEM_LIMIT = 12 * 1024 * 1024


def swap(value, axis, bits):
    devices = lax.axis_size(axis)
    return lax.ppermute(value, axis, [(i, i ^ bits) for i in range(devices)])


def from_behind(value, axis, by):
    devices = lax.axis_size(axis)
    return lax.ppermute(value, axis, [(i, (i + by) % devices) for i in range(devices)])


class Plan:
    def __init__(self, ctx, rows_here):
        self.ctx = ctx
        self.half = ctx // 2
        self.fold = self.half // 2
        self.across = self.half | self.fold
        self.rows_here = rows_here
        self.rows = ctx * rows_here
        self.group_rows = GROUP * self.rows
        self.heads = H // self.half
        self.unit_heads = min(self.heads, GROUP)
        self.units = self.heads // self.unit_heads
        self.unit_rows = self.unit_heads * self.rows
        self.blocks = self.unit_rows // 128
        self.share_rows = self.units * self.unit_rows
        self.by_device = self.unit_heads == GROUP and GROUP * rows_here % 16 == 0

    def share(self, part):
        me = lax.axis_index("ctx")
        return (me % self.half) ^ (me // self.half * self.fold) ^ part


def stat_rows(blocks):
    return -(-3 * blocks // 16) * 16


def local(kernel, out_shape, spaces, name, scratch=(), cost=None):
    return pl.pallas_call(
        kernel,
        out_shape=out_shape,
        in_specs=[pl.BlockSpec(memory_space=space) for space in spaces],
        out_specs=jax.tree.map(lambda _: pl.BlockSpec(memory_space=pltpu.VMEM), out_shape),
        scratch_shapes=list(scratch),
        compiler_params=pltpu.CompilerParams(vmem_limit_bytes=VMEM_LIMIT),
        cost_estimate=cost,
        name=name,
    )


def order_kernel(plan, order_ref, one_hot_ref):
    low = lax.axis_index("ctx") % plan.half
    high = lax.axis_index("ctx") // plan.half
    row = lax.broadcasted_iota(jnp.int32, (plan.group_rows, 128), 0)
    lane = lax.broadcasted_iota(jnp.int32, (plan.group_rows, 128), 1)
    query = lax.rem(row, plan.rows)
    device = lax.div(query, plan.rows_here)
    block = device
    if not plan.by_device:
        block = 2 * (lax.rem(device, plan.half) ^ low) + (lax.div(device, plan.half) ^ high)
    origin = (block * GROUP + lax.div(row, plan.rows)) * plan.rows_here + lax.rem(query, plan.rows_here)
    for at in range(0, plan.group_rows, 128):
        order_ref[:, at : at + 128] = jnp.where(lane + at == origin, 1.0, 0.0).astype(jnp.bfloat16)
    if plan.by_device:
        query = lax.div(row, GROUP * plan.rows_here) * plan.rows_here + lax.rem(row, plan.rows_here)
    one_hot_ref[...] = jnp.where(query == lane, 1.0, 0.0).astype(jnp.bfloat16)


def row_order(plan):
    return local(
        functools.partial(order_kernel, plan),
        [
            jax.ShapeDtypeStruct((plan.group_rows, plan.group_rows), jnp.bfloat16),
            jax.ShapeDtypeStruct((plan.group_rows, 128), jnp.bfloat16),
        ],
        [],
        "order",
        cost=pl.CostEstimate(flops=8_000_000_000, bytes_accessed=0, transcendentals=0),
    )()


def mask_kernel(offset_ref, start_ref, after_ref, bias_ref):
    del after_ref
    span = bias_ref.shape[0]
    position = lax.axis_index("ctx") * span + lax.broadcasted_iota(jnp.int32, (span, 128), 0)
    asked = lax.broadcasted_iota(jnp.int32, (span, 128), 1)
    shown = (position >= start_ref[0]) & (position <= offset_ref[0] + asked)
    bias_ref[...] = jnp.where(shown, 0.0, HIDDEN).astype(jnp.bfloat16)


def mask(span, offsets, starts, after):
    return local(
        mask_kernel,
        jax.ShapeDtypeStruct((span, 128), jnp.bfloat16),
        [pltpu.SMEM, pltpu.SMEM, pl.ANY],
        "mask",
        cost=pl.CostEstimate(flops=1_000_000, bytes_accessed=256 * span, transcendentals=0),
    )(offsets, starts, after)


def write_stats(ref, at, rows):
    values = []
    for peak, total in zip(rows[::2], rows[1::2]):
        high = total.astype(jnp.bfloat16).astype(jnp.float32)
        values += [peak, high, total - high]
    size = stat_rows(len(rows) // 2)
    index = lax.broadcasted_iota(jnp.int32, (size, 128), 0)
    table = jnp.zeros((size, 128), jnp.float32)
    for i, value in enumerate(values):
        table = jnp.where(index == i, value, table)
    ref[at : at + size, :] = table.astype(jnp.bfloat16)


def attend_kernel(plan, part, *refs):
    *refs, score_ref, held_ref = refs
    if part == 0:
        *refs, value_ref, stat_ref = refs
        stat_at = 0
    else:
        *refs, value_ref = refs
        stat_ref, stat_at = value_ref, plan.share_rows
    *query_refs, cache_ref, bias_ref, order_ref, one_hot_ref = refs
    span = cache_ref.shape[0]
    me = lax.axis_index("ctx")
    mine = plan.share(part)
    row_at = pl.multiple_of((mine * plan.heads) % GROUP * plan.rows, plan.unit_rows)
    order = order_ref[pl.ds(row_at, plan.unit_rows), :]
    one_hot = one_hot_ref[pl.ds(row_at, plan.unit_rows), :]
    ones = jnp.ones((span, HD), jnp.bfloat16)
    groups = [(mine * plan.heads + unit * plan.unit_heads) // GROUP for unit in range(plan.units)]
    peaks = []
    for unit, group in enumerate(groups):
        if plan.by_device:
            for block, ref in enumerate(query_refs):
                device = me ^ (block // 2) ^ (block % 2 * plan.half)
                to = pl.multiple_of(device * GROUP * plan.rows_here, GROUP * plan.rows_here)
                held_ref[unit, pl.ds(to, GROUP * plan.rows_here), :] = ref[group]
            queries = held_ref[unit]
        else:
            stacked = jnp.concatenate([ref[group] for ref in query_refs], axis=0)
            queries = jnp.dot(order, stacked, preferred_element_type=jnp.float32).astype(jnp.bfloat16)
        queries = jnp.concatenate([queries, one_hot], axis=1)
        key_at = pl.multiple_of(group * HD, HD)
        keys = jnp.concatenate([cache_ref[:, pl.ds(key_at, HD)], bias_ref[...]], axis=1)
        scores = lax.dot_general(queries, keys, (((1,), (1,)), ((), ())), preferred_element_type=jnp.float32)
        score_ref[unit] = scores
        peak = [scores[:, at : at + 128] for at in range(0, span, 128)]
        while len(peak) > 1:
            peak = [jnp.maximum(*peak[i : i + 2]) for i in range(0, len(peak) - 1, 2)] + (
                peak[-1:] if len(peak) % 2 else []
            )
        peak = jnp.max(peak[0], axis=1, keepdims=True) * LOG2_SCALE
        peak = jnp.maximum(jnp.ceil(peak * (1.0 / STEP)), FLOOR / STEP)
        peaks.append(jnp.broadcast_to(peak, (plan.unit_rows, 128)))
    same = lax.broadcasted_iota(jnp.int32, (128, 128), 0) == lax.broadcasted_iota(jnp.int32, (128, 128), 1)
    stats = []
    for unit, group in enumerate(groups):
        shift = jnp.concatenate([peaks[unit] * STEP] * (span // 128), axis=1)
        weights = jnp.exp2(score_ref[unit] * LOG2_SCALE - shift)
        value_at = pl.multiple_of((KVH + group) * HD, HD)
        values = jnp.concatenate([cache_ref[:, pl.ds(value_at, HD)], ones], axis=1)
        both = jnp.dot(weights.astype(jnp.bfloat16), values, preferred_element_type=jnp.float32)
        at = unit * plan.unit_rows
        value_ref[at : at + plan.unit_rows, :] = both[:, :HD].astype(value_ref.dtype)
        for block in range(0, plan.unit_rows, 128):
            for wide in (peaks[unit], both[:, HD:]):
                chosen = jnp.where(same, wide[block : block + 128, :], 0.0)
                stats.append(jnp.sum(chosen, axis=0, keepdims=True))
    write_stats(stat_ref, stat_at, stats)


def attend(plan, part, queries, cache, *tables):
    span = cache.shape[0]
    size = stat_rows(plan.units * plan.blocks)
    if part == 0:
        out_shape = [
            jax.ShapeDtypeStruct((plan.share_rows, HD), jnp.float32),
            jax.ShapeDtypeStruct((size, HD), jnp.bfloat16),
        ]
    else:
        out_shape = [jax.ShapeDtypeStruct((plan.share_rows + size, HD), jnp.bfloat16)]
    return local(
        functools.partial(attend_kernel, plan, part),
        out_shape,
        [pltpu.VMEM] * (len(queries) + 1 + len(tables)),
        "attend",
        [
            pltpu.VMEM((plan.units, plan.unit_rows, span), jnp.float32),
            pltpu.VMEM((plan.units, plan.unit_rows, HD), jnp.bfloat16),
        ],
        pl.CostEstimate(
            flops=4 * plan.share_rows * span * HD,
            bytes_accessed=2 * plan.units * span * HD * 2,
            transcendentals=plan.share_rows * span,
        ),
    )(*queries, cache, *tables)


def columns(rows):
    size = -(-len(rows) // 8) * 8
    index = lax.broadcasted_iota(jnp.int32, (size, 128), 0)
    table = jnp.zeros((size, 128), jnp.float32)
    for i, row in enumerate(rows):
        table = jnp.where(index == i, row, table)
    turned = jnp.transpose(jnp.concatenate([table, jnp.zeros((128 - size, 128), jnp.float32)], axis=0))
    return [turned[:, i : i + 1] for i in range(len(rows))]


def factors(stats, block):
    parts = []
    for ref, at in stats:
        base = 3 * block // 16 * 16
        tile = ref[at + base : at + min(base + 32, stat_rows(block + 1)), :].astype(jnp.float32)
        begin = 3 * block - base
        parts.append([tile[begin + i : begin + i + 1] for i in range(3)])
    joint = functools.reduce(jnp.maximum, [peak for peak, _, _ in parts])
    scale = [jnp.exp2((peak - joint) * STEP) for peak, _, _ in parts]
    total = functools.reduce(jnp.add, [f * (high + low) for f, (_, high, low) in zip(scale, parts)])
    return joint, scale, total


def mix(refs, at, scale):
    terms = [f * ref[at : at + 128, :].astype(jnp.float32) for ref, f in zip(refs, scale)]
    return functools.reduce(jnp.add, terms)


def merge_kernel(plan, wide_ref, stat_ref, *refs):
    *parts, out_ref, wide_out_ref = refs
    size = stat_rows(plan.units * plan.blocks)
    stats = [(stat_ref, stat_ref.shape[0] - size)] + [(ref, plan.share_rows) for ref in parts]
    rows, scales = [], []
    for block in range(plan.units * plan.blocks):
        joint, scale, total = factors(stats, block)
        rows += [joint, total]
        scales += scale
    scales = columns(scales)
    for block in range(plan.units * plan.blocks):
        at = block * 128
        mixed = mix([wide_ref] + parts, at, scales[block * len(stats) : (block + 1) * len(stats)])
        wide_out_ref[at : at + 128, :] = mixed
        out_ref[at : at + 128, :] = mixed.astype(jnp.bfloat16)
    write_stats(out_ref, plan.share_rows, rows)


def merge(plan, wide, stats, parts):
    rows = plan.share_rows + stat_rows(plan.units * plan.blocks)
    return local(
        functools.partial(merge_kernel, plan),
        [
            jax.ShapeDtypeStruct((rows, HD), jnp.bfloat16),
            jax.ShapeDtypeStruct((plan.share_rows, HD), jnp.float32),
        ],
        [pltpu.VMEM] * (len(parts) + 2),
        "merge",
    )(wide, stats, *parts)


def settle_kernel(plan, wide_ref, own_ref, other_ref, order_ref, out_ref):
    stats = [(own_ref, plan.share_rows), (other_ref, plan.share_rows)]
    scales = []
    for block in range(plan.units * plan.blocks):
        _, scale, total = factors(stats, block)
        scales += [f / total for f in scale]
    scales = columns(scales)
    done = []
    for block in range(plan.units * plan.blocks):
        mixed = mix([wide_ref, other_ref], block * 128, scales[2 * block : 2 * block + 2])
        done.append(mixed.astype(jnp.bfloat16))
    done = [done[unit * plan.blocks : (unit + 1) * plan.blocks] for unit in range(plan.units)]
    done = jnp.concatenate([jnp.concatenate(blocks, axis=0) for blocks in done], axis=1)
    if plan.by_device:
        done = jnp.dot(order_ref[...], done, preferred_element_type=jnp.float32).astype(jnp.bfloat16)
    for unit in range(plan.units):
        for head in range(plan.unit_heads):
            to = (unit * plan.unit_heads + head) * HD
            rows = slice(head * plan.rows, (head + 1) * plan.rows)
            out_ref[:, to : to + HD] = done[rows, unit * HD : (unit + 1) * HD]


def settle(plan, wide, own, other, order):
    return local(
        functools.partial(settle_kernel, plan),
        jax.ShapeDtypeStruct((plan.rows, plan.heads * HD), jnp.bfloat16),
        [pltpu.VMEM] * 4,
        "settle",
    )(wide, own, other, order)


def project_kernel(plan, part, *refs):
    block_ref, weight_ref, *before, out_ref = refs
    depth = plan.heads * HD
    at = pl.multiple_of(plan.share(part) * depth, depth)
    total = jnp.dot(block_ref[...], weight_ref[pl.ds(at, depth), :], preferred_element_type=jnp.float32)
    for ref in before:
        total = total + ref[...]
    out_ref[...] = total.astype(out_ref.dtype)


def project(plan, part, block, weight, before, dtype):
    operands = [block, weight] + ([] if before is None else [before])
    return local(
        functools.partial(project_kernel, plan, part),
        jax.ShapeDtypeStruct((plan.rows, weight.shape[1]), dtype),
        [pltpu.VMEM] * len(operands),
        "project",
    )(*operands)


def per_device(queries, cache, out_weight, offsets, starts):
    plan = Plan(lax.axis_size("ctx"), queries.shape[0])
    half = plan.half
    cache = pltpu.with_memory_space_constraint(cache, pltpu.VMEM)
    out_weight = pltpu.with_memory_space_constraint(out_weight, pltpu.VMEM)

    own = queries.reshape(plan.rows_here, KVH, GROUP, HD)
    own = own.transpose(1, 2, 0, 3).reshape(KVH, GROUP * plan.rows_here, HD)
    far = swap(own, "ctx", half)
    near = [swap(own, "ctx", k) for k in range(1, half)]
    order, one_hot = row_order(plan)
    bias = mask(cache.shape[0], offsets, starts, near[-1])
    if plan.by_device:
        gathered = [own, far]
        for k in range(1, half):
            gathered += [near[k - 1], swap(far, "ctx", k)]
    else:
        pair = jnp.concatenate([own, far], axis=1)
        gathered = [pair] + [swap(pair, "ctx", k) for k in range(1, half)]

    received = []
    for part in reversed(range(1, half)):
        (piece,) = attend(plan, part, gathered, cache, bias, order, one_hot)
        received.append(swap(piece, "ctx", part))
    wide, stats = attend(plan, 0, gathered, cache, bias, order, one_hot)

    near, wide = merge(plan, wide, stats, received[:-1])
    near, wide = merge(plan, wide, near, received[-1:])
    block = settle(plan, wide, near, swap(near, "ctx", plan.across), order)

    total = project(plan, 0, block, out_weight, None, jnp.float32)
    for k in list(range(2, half)) + [1]:
        dtype = jnp.float32 if k > 1 else jnp.bfloat16
        total = project(plan, k, swap(block, "ctx", k), out_weight, total, dtype)
    return from_behind(total, "segment", 1)


def solution(mesh):
    in_specs = (
        P(("segment", "ctx"), None),
        P(("segment", "ctx"), None),
        P("segment", "ctx"),
        P("segment"),
        P("segment"),
    )
    out_specs = P("segment", "ctx")
    return jax.shard_map(
        per_device, mesh=mesh, in_specs=in_specs, out_specs=out_specs, check_vma=False
    )
```

```python
import functools
import math

import jax
import jax.numpy as jnp
from jax import lax
from jax.experimental import pallas as pl
from jax.experimental.pallas import tpu as pltpu
from jax.sharding import PartitionSpec as P

H = 64
KVH = 8
HD = 128
GROUP = H // KVH
LOG2_SCALE = HD ** (-0.5) * math.log2(math.e)
STEP = 8.0
FLOOR = -4096.0
HIDDEN = -1e30
STATS = 16
VMEM_LIMIT = 12 * 1024 * 1024


def swap(value, axis, bits):
    devices = lax.axis_size(axis)
    return lax.ppermute(value, axis, [(i, i ^ bits) for i in range(devices)])


def from_behind(value, axis, by):
    devices = lax.axis_size(axis)
    return lax.ppermute(value, axis, [(i, (i + by) % devices) for i in range(devices)])


class Plan:
    def __init__(self, ctx, rows_here):
        self.ctx = ctx
        self.half = ctx // 2
        self.fold = self.half // 2
        self.across = self.half | self.fold
        self.rows_here = rows_here
        self.rows = ctx * rows_here
        self.group_rows = GROUP * self.rows
        self.heads = H // self.half
        self.unit_heads = min(self.heads, GROUP)
        self.units = self.heads // self.unit_heads
        self.unit_rows = self.unit_heads * self.rows
        self.blocks = self.unit_rows // 128
        self.share_rows = self.units * self.unit_rows
        self.by_device = self.unit_heads == GROUP and GROUP * rows_here % 16 == 0

    def share(self, part):
        me = lax.axis_index("ctx")
        return (me % self.half) ^ (me // self.half * self.fold) ^ part


def stat_rows(blocks):
    return -(-3 * blocks // 16) * 16


def local(kernel, out_shape, spaces, name, scratch=(), cost=None):
    return pl.pallas_call(
        kernel,
        out_shape=out_shape,
        in_specs=[pl.BlockSpec(memory_space=space) for space in spaces],
        out_specs=jax.tree.map(lambda _: pl.BlockSpec(memory_space=pltpu.VMEM), out_shape),
        scratch_shapes=list(scratch),
        compiler_params=pltpu.CompilerParams(vmem_limit_bytes=VMEM_LIMIT),
        cost_estimate=cost,
        name=name,
    )


def order_kernel(plan, order_ref, one_hot_ref):
    low = lax.axis_index("ctx") % plan.half
    high = lax.axis_index("ctx") // plan.half
    row = lax.broadcasted_iota(jnp.int32, (plan.group_rows, 128), 0)
    lane = lax.broadcasted_iota(jnp.int32, (plan.group_rows, 128), 1)
    query = lax.rem(row, plan.rows)
    device = lax.div(query, plan.rows_here)
    block = device
    if not plan.by_device:
        block = 2 * (lax.rem(device, plan.half) ^ low) + (lax.div(device, plan.half) ^ high)
    origin = (block * GROUP + lax.div(row, plan.rows)) * plan.rows_here + lax.rem(query, plan.rows_here)
    for at in range(0, plan.group_rows, 128):
        order_ref[:, at : at + 128] = jnp.where(lane + at == origin, 1.0, 0.0).astype(jnp.bfloat16)
    if plan.by_device:
        query = lax.div(row, GROUP * plan.rows_here) * plan.rows_here + lax.rem(row, plan.rows_here)
    one_hot_ref[...] = jnp.where(query == lane, 1.0, 0.0).astype(jnp.bfloat16)


def row_order(plan):
    return local(
        functools.partial(order_kernel, plan),
        [
            jax.ShapeDtypeStruct((plan.group_rows, plan.group_rows), jnp.bfloat16),
            jax.ShapeDtypeStruct((plan.group_rows, 128), jnp.bfloat16),
        ],
        [],
        "order",
        cost=pl.CostEstimate(flops=8_000_000_000, bytes_accessed=0, transcendentals=0),
    )()


def mask_kernel(offset_ref, start_ref, after_ref, bias_ref):
    del after_ref
    span = bias_ref.shape[0]
    position = lax.axis_index("ctx") * span + lax.broadcasted_iota(jnp.int32, (span, 128), 0)
    asked = lax.broadcasted_iota(jnp.int32, (span, 128), 1)
    shown = (position >= start_ref[0]) & (position <= offset_ref[0] + asked)
    bias_ref[...] = jnp.where(shown, 0.0, HIDDEN).astype(jnp.bfloat16)


def mask(span, offsets, starts, after):
    return local(
        mask_kernel,
        jax.ShapeDtypeStruct((span, 128), jnp.bfloat16),
        [pltpu.SMEM, pltpu.SMEM, pl.ANY],
        "mask",
        cost=pl.CostEstimate(flops=1_000_000, bytes_accessed=256 * span, transcendentals=0),
    )(offsets, starts, after)


def write_stats(ref, at, rows):
    values = []
    for peak, total in zip(rows[::2], rows[1::2]):
        high = total.astype(jnp.bfloat16).astype(jnp.float32)
        values += [peak, high, total - high]
    size = stat_rows(len(rows) // 2)
    index = lax.broadcasted_iota(jnp.int32, (size, 128), 0)
    table = jnp.zeros((size, 128), jnp.float32)
    for i, value in enumerate(values):
        table = jnp.where(index == i, value, table)
    ref[at : at + size, :] = table.astype(jnp.bfloat16)


def attend_kernel(plan, part, *refs):
    *refs, score_ref, held_ref = refs
    if part == 0:
        *refs, value_ref, stat_ref = refs
        stat_at = 0
    else:
        *refs, value_ref = refs
        stat_ref, stat_at = value_ref, plan.share_rows
    *query_refs, cache_ref, bias_ref, order_ref, one_hot_ref = refs
    span = cache_ref.shape[0]
    me = lax.axis_index("ctx")
    mine = plan.share(part)
    row_at = pl.multiple_of((mine * plan.heads) % GROUP * plan.rows, plan.unit_rows)
    order = order_ref[pl.ds(row_at, plan.unit_rows), :]
    one_hot = one_hot_ref[pl.ds(row_at, plan.unit_rows), :]
    ones = jnp.ones((span, HD), jnp.bfloat16)
    groups = [(mine * plan.heads + unit * plan.unit_heads) // GROUP for unit in range(plan.units)]
    peaks = []
    for unit, group in enumerate(groups):
        if plan.by_device:
            for block, ref in enumerate(query_refs):
                device = me ^ (-(block // 2) % plan.half) ^ (block % 2 * plan.half)
                to = pl.multiple_of(device * GROUP * plan.rows_here, GROUP * plan.rows_here)
                held_ref[unit, pl.ds(to, GROUP * plan.rows_here), :] = ref[group]
            queries = held_ref[unit]
        else:
            stacked = jnp.concatenate([ref[group] for ref in query_refs], axis=0)
            queries = jnp.dot(order, stacked, preferred_element_type=jnp.float32).astype(jnp.bfloat16)
        queries = jnp.concatenate([queries, one_hot], axis=1)
        key_at = pl.multiple_of(group * HD, HD)
        keys = jnp.concatenate([cache_ref[:, pl.ds(key_at, HD)], bias_ref[...]], axis=1)
        scores = lax.dot_general(queries, keys, (((1,), (1,)), ((), ())), preferred_element_type=jnp.float32)
        score_ref[unit] = scores
        peak = [scores[:, at : at + 128] for at in range(0, span, 128)]
        while len(peak) > 1:
            peak = [jnp.maximum(*peak[i : i + 2]) for i in range(0, len(peak) - 1, 2)] + (
                peak[-1:] if len(peak) % 2 else []
            )
        peak = jnp.max(peak[0], axis=1, keepdims=True) * LOG2_SCALE
        peak = jnp.maximum(jnp.ceil(peak * (1.0 / STEP)), FLOOR / STEP)
        peaks.append(jnp.broadcast_to(peak, (plan.unit_rows, 128)))
    same = lax.broadcasted_iota(jnp.int32, (128, 128), 0) == lax.broadcasted_iota(jnp.int32, (128, 128), 1)
    stats = []
    for unit, group in enumerate(groups):
        shift = jnp.concatenate([peaks[unit] * STEP] * (span // 128), axis=1)
        weights = jnp.exp2(score_ref[unit] * LOG2_SCALE - shift)
        value_at = pl.multiple_of((KVH + group) * HD, HD)
        values = jnp.concatenate([cache_ref[:, pl.ds(value_at, HD)], ones], axis=1)
        both = jnp.dot(weights.astype(jnp.bfloat16), values, preferred_element_type=jnp.float32)
        at = unit * plan.unit_rows
        value_ref[at : at + plan.unit_rows, :] = both[:, :HD].astype(value_ref.dtype)
        for block in range(0, plan.unit_rows, 128):
            for wide in (peaks[unit], both[:, HD:]):
                chosen = jnp.where(same, wide[block : block + 128, :], 0.0)
                stats.append(jnp.sum(chosen, axis=0, keepdims=True))
    write_stats(stat_ref, stat_at, stats)


def attend(plan, part, queries, cache, *tables):
    span = cache.shape[0]
    size = stat_rows(plan.units * plan.blocks)
    if part == 0:
        out_shape = [
            jax.ShapeDtypeStruct((plan.share_rows, HD), jnp.float32),
            jax.ShapeDtypeStruct((size, HD), jnp.bfloat16),
        ]
    else:
        out_shape = [jax.ShapeDtypeStruct((plan.share_rows + size, HD), jnp.bfloat16)]
    return local(
        functools.partial(attend_kernel, plan, part),
        out_shape,
        [pltpu.VMEM] * (len(queries) + 1 + len(tables)),
        "attend",
        [
            pltpu.VMEM((plan.units, plan.unit_rows, span), jnp.float32),
            pltpu.VMEM((plan.units, plan.unit_rows, HD), jnp.bfloat16),
        ],
        pl.CostEstimate(
            flops=4 * plan.share_rows * span * HD,
            bytes_accessed=2 * plan.units * span * HD * 2,
            transcendentals=plan.share_rows * span,
        ),
    )(*queries, cache, *tables)


def columns(rows):
    size = -(-len(rows) // 8) * 8
    index = lax.broadcasted_iota(jnp.int32, (size, 128), 0)
    table = jnp.zeros((size, 128), jnp.float32)
    for i, row in enumerate(rows):
        table = jnp.where(index == i, row, table)
    turned = jnp.transpose(jnp.concatenate([table, jnp.zeros((128 - size, 128), jnp.float32)], axis=0))
    return [turned[:, i : i + 1] for i in range(len(rows))]


def factors(stats, block):
    parts = []
    for ref, at in stats:
        base = 3 * block // 16 * 16
        tile = ref[at + base : at + min(base + 32, stat_rows(block + 1)), :].astype(jnp.float32)
        begin = 3 * block - base
        parts.append([tile[begin + i : begin + i + 1] for i in range(3)])
    joint = functools.reduce(jnp.maximum, [peak for peak, _, _ in parts])
    scale = [jnp.exp2((peak - joint) * STEP) for peak, _, _ in parts]
    total = functools.reduce(jnp.add, [f * (high + low) for f, (_, high, low) in zip(scale, parts)])
    return joint, scale, total


def mix(refs, at, scale):
    terms = [f * ref[at : at + 128, :].astype(jnp.float32) for ref, f in zip(refs, scale)]
    return functools.reduce(jnp.add, terms)


def merge_kernel(plan, wide_ref, stat_ref, *refs):
    *parts, out_ref, wide_out_ref = refs
    size = stat_rows(plan.units * plan.blocks)
    stats = [(stat_ref, stat_ref.shape[0] - size)] + [(ref, plan.share_rows) for ref in parts]
    rows, scales = [], []
    for block in range(plan.units * plan.blocks):
        joint, scale, total = factors(stats, block)
        rows += [joint, total]
        scales += scale
    scales = columns(scales)
    for block in range(plan.units * plan.blocks):
        at = block * 128
        mixed = mix([wide_ref] + parts, at, scales[block * len(stats) : (block + 1) * len(stats)])
        wide_out_ref[at : at + 128, :] = mixed
        out_ref[at : at + 128, :] = mixed.astype(jnp.bfloat16)
    write_stats(out_ref, plan.share_rows, rows)


def merge(plan, wide, stats, parts):
    rows = plan.share_rows + stat_rows(plan.units * plan.blocks)
    return local(
        functools.partial(merge_kernel, plan),
        [
            jax.ShapeDtypeStruct((rows, HD), jnp.bfloat16),
            jax.ShapeDtypeStruct((plan.share_rows, HD), jnp.float32),
        ],
        [pltpu.VMEM] * (len(parts) + 2),
        "merge",
    )(wide, stats, *parts)


def settle_kernel(plan, wide_ref, own_ref, other_ref, order_ref, out_ref):
    stats = [(own_ref, plan.share_rows), (other_ref, plan.share_rows)]
    scales = []
    for block in range(plan.units * plan.blocks):
        _, scale, total = factors(stats, block)
        scales += [f / total for f in scale]
    scales = columns(scales)
    done = []
    for block in range(plan.units * plan.blocks):
        mixed = mix([wide_ref, other_ref], block * 128, scales[2 * block : 2 * block + 2])
        done.append(mixed.astype(jnp.bfloat16))
    done = [done[unit * plan.blocks : (unit + 1) * plan.blocks] for unit in range(plan.units)]
    done = jnp.concatenate([jnp.concatenate(blocks, axis=0) for blocks in done], axis=1)
    if plan.by_device:
        done = jnp.dot(order_ref[...], done, preferred_element_type=jnp.float32).astype(jnp.bfloat16)
    for unit in range(plan.units):
        for head in range(plan.unit_heads):
            to = (unit * plan.unit_heads + head) * HD
            rows = slice(head * plan.rows, (head + 1) * plan.rows)
            out_ref[:, to : to + HD] = done[rows, unit * HD : (unit + 1) * HD]


def settle(plan, wide, own, other, order):
    return local(
        functools.partial(settle_kernel, plan),
        jax.ShapeDtypeStruct((plan.rows, plan.heads * HD), jnp.bfloat16),
        [pltpu.VMEM] * 4,
        "settle",
    )(wide, own, other, order)


def project_kernel(plan, part, *refs):
    block_ref, weight_ref, *before, out_ref = refs
    depth = plan.heads * HD
    at = pl.multiple_of(plan.share(part) * depth, depth)
    total = jnp.dot(block_ref[...], weight_ref[pl.ds(at, depth), :], preferred_element_type=jnp.float32)
    for ref in before:
        total = total + ref[...]
    out_ref[...] = total.astype(out_ref.dtype)


def project(plan, part, block, weight, before, dtype):
    operands = [block, weight] + ([] if before is None else [before])
    return local(
        functools.partial(project_kernel, plan, part),
        jax.ShapeDtypeStruct((plan.rows, weight.shape[1]), dtype),
        [pltpu.VMEM] * len(operands),
        "project",
    )(*operands)


def per_device(queries, cache, out_weight, offsets, starts):
    plan = Plan(lax.axis_size("ctx"), queries.shape[0])
    half = plan.half
    cache = pltpu.with_memory_space_constraint(cache, pltpu.VMEM)
    out_weight = pltpu.with_memory_space_constraint(out_weight, pltpu.VMEM)

    own = queries.reshape(plan.rows_here, KVH, GROUP, HD)
    own = own.transpose(1, 2, 0, 3).reshape(KVH, GROUP * plan.rows_here, HD)
    far = swap(own, "ctx", half)
    near = [swap(own, "ctx", k) for k in range(1, half)]
    order, one_hot = row_order(plan)
    bias = mask(cache.shape[0], offsets, starts, near[0])
    if plan.by_device:
        gathered = [own, far]
        for k in reversed(range(1, half)):
            gathered += [near[k - 1], swap(far, "ctx", k)]
    else:
        pair = jnp.concatenate([own, far], axis=1)
        gathered = [pair] + [swap(pair, "ctx", k) for k in range(1, half)]

    received = []
    for part in reversed(range(1, half)):
        (piece,) = attend(plan, part, gathered, cache, bias, order, one_hot)
        received.append(swap(piece, "ctx", part))
    wide, stats = attend(plan, 0, gathered, cache, bias, order, one_hot)

    near, wide = merge(plan, wide, stats, received[:-1])
    near, wide = merge(plan, wide, near, received[-1:])
    block = settle(plan, wide, near, swap(near, "ctx", plan.across), order)

    total = project(plan, 0, block, out_weight, None, jnp.float32)
    blocks = [swap(block, "ctx", k) for k in range(1, half)]
    for k in range(1, half):
        dtype = jnp.float32 if k < half - 1 else jnp.bfloat16
        total = project(plan, k, blocks[k - 1], out_weight, total, dtype)
    return from_behind(total, "segment", 1)


def solution(mesh):
    in_specs = (
        P(("segment", "ctx"), None),
        P(("segment", "ctx"), None),
        P("segment", "ctx"),
        P("segment"),
        P("segment"),
    )
    out_specs = P("segment", "ctx")
    return jax.shard_map(
        per_device, mesh=mesh, in_specs=in_specs, out_specs=out_specs, check_vma=False
    )
```
